512 devices in a mesh: tm: 8 (over x, core), row: 64 (over z, y).
Axes of the slice: x: 4, y: 8, z: 8, core: 2. Of those that a mesh axis runs over, the one named last changes fastest.
Arguments:
- inputs: bfloat16 [96, 8, 64, 256], P(None, 'tm', 'row'), may hold values from -6 to 6
- cotangent: bfloat16 [96, 8, 64, 256], P(None, 'tm', 'row'), may hold values from -6 to 6
- gain_first: float32 [96], replicated, may hold values from 0.5 to 1.5
- gain_second: float32 [96], replicated, may hold values from 0.5 to 1.5
- bias_first: float32 [96], replicated, may hold values from -3 to 3
- kernel_first: bfloat16 [3, 3, 3, 96, 96], replicated, may hold values from -0.125 to 0.125
- kernel_second: bfloat16 [3, 3, 3, 96, 96], replicated, may hold values from -0.125 to 0.125
Outputs:
- grad_inputs: bfloat16 [96, 8, 64, 256], P(None, 'tm', 'row')
- grad_kernel_first: float32 [3, 3, 3, 96, 96], replicated
- grad_kernel_second: float32 [3, 3, 3, 96, 96], replicated
- grad_vectors: float32 [4, 96], replicated
The draws below stay inside these ranges and needn't reach their ends.
All inputs are finite; a program needn't handle non-finite values.
Results may differ from the reference program's by a relative error of at most 0.0055.
Values may be sent and summed in bfloat16 or wider, within the bound.
A program may use at most 64 MiB of HBM per device.

```python
import jax
import jax.numpy as jnp
from jax import lax

C = 96
W = 256
FRAMES = 8
ROWS = 64


def level_of(key, dims, cuts, least, largest):
    level = 1.0
    for dim, shards_of in cuts:
        steps = jax.random.uniform(jax.random.fold_in(jax.random.fold_in(key, 6), dim), (shards_of,), jnp.float32, least / len(cuts), largest / len(cuts))
        level = level * jnp.repeat(jnp.exp(steps), dims[dim] // shards_of).reshape((-1,) + (1,) * (len(dims) - 1 - dim))
    return level


def scatter_about(stream_key, shape, deviation, limit, split=(), held_as=jnp.bfloat16):
    values = deviation * jax.random.normal(stream_key, shape, jnp.float32)
    if split:
        values = values * level_of(stream_key, shape, split, -0.22, 0.18)
    return jnp.clip(values, -limit, limit).astype(held_as)


def setup_inputs(seed: int = 0) -> dict:
    key_of = jax.random.split(jax.random.key(seed), 8)
    return {
        "inputs": scatter_about(key_of[0], (C, FRAMES, ROWS, W), 1.0, 6.0, ((1, 8), (2, 64))),
        "cotangent": scatter_about(key_of[1], (C, FRAMES, ROWS, W), 1.0, 6.0, ((1, 8), (2, 64))),
        "gain_first": jnp.clip(jax.random.uniform(key_of[2], (C,), jnp.float32, 0.5, 1.5), 0.5, 1.5),
        "gain_second": jnp.clip(jax.random.uniform(key_of[3], (C,), jnp.float32, 0.5, 1.5), 0.5, 1.5),
        "bias_first": scatter_about(key_of[4], (C,), 0.5, 3.0, (), jnp.float32),
        "kernel_first": scatter_about(key_of[5], (3, 3, 3, C, C), (27 * C) ** -0.5, 0.125),
        "kernel_second": scatter_about(key_of[6], (3, 3, 3, C, C), (27 * C) ** -0.5, 0.125),
    }


epsilon = 1e-06
max_norm = 500.0

def norm_act(values, gain):
    meansq = lax.optimization_barrier(jnp.mean(values * values, axis=0, keepdims=True))
    scaled = values * lax.rsqrt(meansq + epsilon) * gain.reshape((-1,) + (1,) * (values.ndim - 1))
    return jax.nn.silu(scaled)

def conv(features, kernel):
    result = lax.conv_general_dilated(features[None], kernel, (1, 1, 1), ((2, 0), (1, 1), (1, 1)), dimension_numbers=('NCDHW', 'DHWOI', 'NCDHW'), precision=lax.Precision.HIGHEST)
    return result[0]

def reference(inputs, cotangent, gain_first, gain_second, bias_first, kernel_first, kernel_second):
    input_wide = inputs.astype(jnp.float32)
    cot_wide = cotangent.astype(jnp.float32)
    first = lax.optimization_barrier(norm_act(input_wide, gain_first).astype(jnp.bfloat16)).astype(jnp.float32)
    kernel_one = kernel_first.astype(jnp.float32)
    kernel_two = kernel_second.astype(jnp.float32)
    hidden = conv(first, kernel_one) + bias_first[:, None, None, None]
    second_wide, act_back = jax.vjp(norm_act, hidden, gain_second)
    second = lax.optimization_barrier(second_wide.astype(jnp.bfloat16)).astype(jnp.float32)
    _, conv_two_back = jax.vjp(conv, second, kernel_two)
    grad_second, raw_second = conv_two_back(cot_wide)
    grad_hidden, raw_gain_second = act_back(grad_second)
    hidden_cot = lax.optimization_barrier(grad_hidden.astype(jnp.bfloat16)).astype(jnp.float32)
    _, conv_one_back = jax.vjp(conv, first, kernel_one)
    grad_first, raw_first = conv_one_back(hidden_cot)
    _, input_back = jax.vjp(norm_act, input_wide, gain_first)
    input_term, raw_gain_first = input_back(grad_first)
    grad_inputs = (cot_wide + input_term).astype(jnp.bfloat16)
    raw_vectors = jnp.stack([lax.optimization_barrier(jnp.sum(grad_hidden, axis=(1, 2, 3))), raw_gain_first, raw_gain_second, lax.optimization_barrier(jnp.sum(cot_wide, axis=(1, 2, 3)))])
    total = jnp.sqrt(jnp.sum(raw_first * raw_first) + jnp.sum(raw_second * raw_second) + jnp.sum(raw_vectors * raw_vectors))
    factor = jnp.minimum(jnp.float32(1.0), max_norm / (total + epsilon))
    return (grad_inputs, raw_first * factor, raw_second * factor, raw_vectors * factor)
```

```python
import jax
import jax.numpy as jnp
from jax import lax
from jax.experimental import pallas as pl
from jax.experimental.pallas import tpu as pltpu
from jax.sharding import PartitionSpec as P

epsilon = 1e-06
max_norm = 500.0


def shifted(block, axis, distance):
    devices = range(lax.axis_size(axis))
    route = [(i - distance, i) for i in devices if i - distance in devices]
    return lax.ppermute(block, axis, route)


def extended(block, sides, width):
    for axis, dim in sides:
        count = lax.axis_size(axis)
        forward = [(i, i + 1) for i in range(count - 1)]
        backward = [(target, source) for source, target in forward]
        low = lax.ppermute(
            lax.slice_in_dim(block, block.shape[dim] - width, None, axis=dim), axis, forward
        )
        high = lax.ppermute(lax.slice_in_dim(block, 0, width, axis=dim), axis, backward)
        block = jnp.concatenate([low, block, high], axis=dim)
    return block


def norm_act(values, gain):
    meansq = jnp.mean(values * values, axis=0, keepdims=True)
    scaled = values * lax.rsqrt(meansq + epsilon) * gain.reshape((-1,) + (1,) * (values.ndim - 1))
    return jax.nn.silu(scaled)


def extend(plane, towards):
    frames = [plane]
    for offset in (1, 2):
        frames.append(shifted(plane, "tm", towards * offset))
    ordered = frames[::-1] if towards > 0 else frames
    banded = extended(jnp.stack(ordered, axis=1), (("row", 2),), 1)
    return jnp.pad(banded, ((0, 0), (0, 0), (0, 0), (1, 1)))


def spread(volume, towards):
    return extend(volume[:, 0], towards)


def forward_conv(padded, kernel, frame_count, row_count, col_count):
    total = jnp.zeros((kernel.shape[3], frame_count, row_count, col_count), jnp.float32)
    for tap_t in range(3):
        for tap_h in range(3):
            for tap_w in range(3):
                window = padded[
                    :,
                    tap_t : tap_t + frame_count,
                    tap_h : tap_h + row_count,
                    tap_w : tap_w + col_count,
                ]
                total = total + jnp.einsum(
                    "oc,ctrw->otrw",
                    kernel[tap_t, tap_h, tap_w],
                    window,
                    preferred_element_type=jnp.float32,
                )
    return total


def input_grad(padded, kernel, frame_count, row_count, col_count):
    total = jnp.zeros((kernel.shape[4], frame_count, row_count, col_count), jnp.float32)
    for tap_t in range(3):
        for tap_h in range(3):
            for tap_w in range(3):
                window = padded[
                    :,
                    2 - tap_t : 2 - tap_t + frame_count,
                    2 - tap_h : 2 - tap_h + row_count,
                    2 - tap_w : 2 - tap_w + col_count,
                ]
                total = total + jnp.einsum(
                    "oc,otrw->ctrw",
                    kernel[tap_t, tap_h, tap_w],
                    window,
                    preferred_element_type=jnp.float32,
                )
    return total


def kernel_grad(padded, upstream, frame_count, row_count, col_count):
    pieces = []
    for tap_t in range(3):
        for tap_h in range(3):
            for tap_w in range(3):
                window = padded[
                    :,
                    tap_t : tap_t + frame_count,
                    tap_h : tap_h + row_count,
                    tap_w : tap_w + col_count,
                ]
                pieces.append(
                    jnp.einsum(
                        "otrw,ctrw->oc", upstream, window, preferred_element_type=jnp.float32
                    )
                )
    stacked = jnp.stack(pieces)
    return stacked.reshape((3, 3, 3) + stacked.shape[1:])


ROWS_ALL = 4096
LANES = 128
MESH = pl.DeviceIdType.MESH


def reduce_kernel(z_ref, g_ref, core_in, part, x_out, x_in, y_in, y_own, z_in, z_all,
                  core_sem, x_sem, y_sem, z_sem, gz_sem, gy_sem, gx_sem, gc_sem):
    tm, row = lax.axis_index("tm"), lax.axis_index("row")
    me_x, me_c = tm // 2, tm % 2
    me_z, me_y = row // 8, row % 8
    peer_c = {"tm": me_x * 2 + 1 - me_c, "row": row}

    def at_x(d):
        return lax.rem(me_x + d, 4)

    def at_y(d):
        return lax.rem(me_y + d, 8)

    def at_z(d):
        return lax.rem(me_z + d, 8)

    def peer_x(d):
        return {"tm": at_x(d) * 2 + me_c, "row": row}

    def peer_y(d):
        return {"tm": tm, "row": me_z * 8 + at_y(d)}

    def peer_z(d):
        return {"tm": tm, "row": at_z(d) * 8 + me_y}

    def send(src, dst, sems, slot, device):
        copy = pltpu.make_async_remote_copy(
            src_ref=src, dst_ref=dst, send_sem=sems.at[0, slot], recv_sem=sems.at[1, slot],
            device_id=device, device_id_type=MESH,
        )
        copy.start()
        return copy

    barrier = pltpu.get_barrier_semaphore()
    peers = [peer_c] + [peer_x(d) for d in range(1, 4)]
    peers += [peer_y(d) for d in range(1, 8)] + [peer_z(d) for d in range(1, 8)]
    for peer in peers:
        pl.semaphore_signal(barrier, inc=1, device_id=peer, device_id_type=MESH)
    pl.semaphore_wait(barrier, len(peers))

    sent = []
    halves = []
    for k in range(4):
        chunk = at_x(k + 1) * 512
        theirs = pl.ds(pl.multiple_of((1 - me_c) * 2048 + chunk, 512), 512)
        land = pl.ds(pl.multiple_of(chunk, 512), 512)
        halves.append(send(z_ref.at[theirs], core_in.at[land], core_sem, k, peer_c))
    arrivals = []
    for k in range(4):
        halves[k].wait_recv()
        chunk = at_x(k + 1) * 512
        mine = pl.ds(pl.multiple_of(me_c * 2048 + chunk, 512), 512)
        land = pl.ds(pl.multiple_of(chunk, 512), 512)
        total = z_ref[mine, :] + core_in[land, :]
        if k < 3:
            x_out[k] = total.astype(jnp.bfloat16)
            arrivals.append(send(x_out.at[k], x_in.at[k], x_sem, k, peer_x(k + 1)))
        else:
            part[...] = total
    sent += halves + arrivals

    for copy in arrivals:
        copy.wait_recv()
    total = part[...]
    for k in range(3):
        total = total + x_in[k].astype(jnp.float32)
    part[...] = total
    arrivals = []
    for d in range(1, 8):
        theirs = pl.ds(pl.multiple_of(at_y(d) * 64, 64), 64)
        arrivals.append(send(part.at[theirs], y_in.at[d - 1], y_sem, d - 1, peer_y(d)))
    sent += arrivals
    for copy in arrivals:
        copy.wait_recv()
    total = part[pl.ds(pl.multiple_of(me_y * 64, 64), 64), :]
    for k in range(7):
        total = total + y_in[k]
    y_own[...] = total
    arrivals = []
    for d in range(1, 8):
        theirs = pl.ds(pl.multiple_of(at_z(d) * 8, 8), 8)
        arrivals.append(send(y_own.at[theirs], z_in.at[d - 1], z_sem, d - 1, peer_z(d)))
    sent += arrivals
    for copy in arrivals:
        copy.wait_recv()
    own = pl.ds(pl.multiple_of(me_z * 8, 8), 8)
    total = y_own[own, :]
    for k in range(7):
        total = total + z_in[k]
    z_all[own, :] = total
    arrivals = []
    for d in range(1, 8):
        arrivals.append(send(z_all.at[own], z_all.at[own], gz_sem, d - 1, peer_z(d)))
    sent += arrivals
    for copy in arrivals:
        copy.wait_recv()
    base = me_c * 2048 + me_x * 512
    mine = pl.ds(pl.multiple_of(base + me_y * 64, 64), 64)
    g_ref[mine, :] = z_all[...].astype(jnp.bfloat16)
    arrivals = []
    for d in range(1, 8):
        arrivals.append(send(g_ref.at[mine], g_ref.at[mine], gy_sem, d - 1, peer_y(d)))
    sent += arrivals
    for copy in arrivals:
        copy.wait_recv()
    mine = pl.ds(pl.multiple_of(base, 512), 512)
    arrivals = []
    for d in range(1, 4):
        arrivals.append(send(g_ref.at[mine], g_ref.at[mine], gx_sem, d - 1, peer_x(d)))
    cores = [send(g_ref.at[mine], g_ref.at[mine], gc_sem, 0, peer_c)]
    sent += arrivals
    for d in range(1, 4):
        arrivals[d - 1].wait_recv()
        there = pl.ds(pl.multiple_of(me_c * 2048 + at_x(4 - d) * 512, 512), 512)
        cores.append(send(g_ref.at[there], g_ref.at[there], gc_sem, d, peer_c))
    sent += cores
    for copy in cores:
        copy.wait_recv()
    for copy in sent:
        copy.wait_send()


def all_sum(packed):
    f32, bf16, dma = jnp.float32, jnp.bfloat16, pltpu.SemaphoreType.DMA
    return pl.pallas_call(
        reduce_kernel,
        out_shape=jax.ShapeDtypeStruct((ROWS_ALL, LANES), bf16),
        in_specs=[pl.BlockSpec(memory_space=pltpu.VMEM)],
        out_specs=pl.BlockSpec(memory_space=pltpu.VMEM),
        scratch_shapes=[
            pltpu.VMEM((2048, LANES), f32),
            pltpu.VMEM((512, LANES), f32),
            pltpu.VMEM((3, 512, LANES), bf16),
            pltpu.VMEM((3, 512, LANES), bf16),
            pltpu.VMEM((7, 64, LANES), f32),
            pltpu.VMEM((64, LANES), f32),
            pltpu.VMEM((7, 8, LANES), f32),
            pltpu.VMEM((64, LANES), f32),
            dma((2, 4)), dma((2, 3)), dma((2, 7)), dma((2, 7)),
            dma((2, 7)), dma((2, 7)), dma((2, 3)), dma((2, 4)),
        ],
        compiler_params=pltpu.CompilerParams(
            collective_id=0, has_side_effects=True, vmem_limit_bytes=40 * 1024 * 1024
        ),
    )(packed)


def body(inputs, cotangent, gain_first, gain_second, bias_first, kernel_first, kernel_second):
    local_in, local_cot = (inputs, cotangent)
    frame_count = local_in.shape[1]
    row_count = local_in.shape[2]
    col_count = local_in.shape[3]
    input_wide = local_in.astype(jnp.float32)
    first = norm_act(input_wide, gain_first).astype(jnp.bfloat16)
    prior_first = spread(first, 1)
    hidden = (
        forward_conv(prior_first, kernel_first, frame_count, row_count, col_count)
        + bias_first[:, None, None, None]
    )
    second_wide, act_back = jax.vjp(norm_act, hidden, gain_second)
    second = second_wide.astype(jnp.bfloat16)
    grad_second = input_grad(
        spread(local_cot, -1), kernel_second, frame_count, row_count, col_count
    )
    raw_second = kernel_grad(spread(second, 1), local_cot, frame_count, row_count, col_count)
    grad_hidden, raw_gain_second = act_back(grad_second)
    hidden_cot = grad_hidden.astype(jnp.bfloat16)
    grad_first = input_grad(spread(hidden_cot, -1), kernel_first, frame_count, row_count, col_count)
    raw_first = kernel_grad(prior_first, hidden_cot, frame_count, row_count, col_count)
    _, input_back = jax.vjp(norm_act, input_wide, gain_first)
    input_term, raw_gain_first = input_back(grad_first)
    cot_wide = local_cot.astype(jnp.float32)
    grad_local = (cot_wide + input_term).astype(jnp.bfloat16)
    raw_vectors = jnp.stack(
        [
            jnp.sum(grad_hidden, axis=(1, 2, 3)),
            raw_gain_first,
            raw_gain_second,
            jnp.sum(cot_wide, axis=(1, 2, 3)),
        ]
    )
    sizes = [raw_first.size, raw_second.size, raw_vectors.size]
    spare = ROWS_ALL * LANES - sum(sizes)
    flat = jnp.concatenate(
        [raw_first.reshape(-1), raw_second.reshape(-1), raw_vectors.reshape(-1), jnp.zeros((spare,), jnp.float32)]
    )
    flat = all_sum(flat.reshape(ROWS_ALL, LANES)).astype(jnp.float32).reshape(-1)
    ends = [sizes[0], sizes[0] + sizes[1], sum(sizes)]
    summed_first = flat[: ends[0]].reshape(raw_first.shape)
    summed_second = flat[ends[0] : ends[1]].reshape(raw_second.shape)
    summed_vectors = flat[ends[1] : ends[2]].reshape(raw_vectors.shape)
    total = jnp.sqrt(
        jnp.sum(summed_first * summed_first)
        + jnp.sum(summed_second * summed_second)
        + jnp.sum(summed_vectors * summed_vectors)
    )
    factor = jnp.minimum(jnp.float32(1.0), max_norm / (total + epsilon))
    grad_kernel_first = summed_first * factor
    grad_kernel_second = summed_second * factor
    return (grad_local, grad_kernel_first, grad_kernel_second, summed_vectors * factor)


def solution(mesh):
    in_specs = (P(None, "tm", "row", None), P(None, "tm", "row", None), P(), P(), P(), P(), P())
    out_specs = (P(None, "tm", "row", None), P(), P(), P())
    return jax.shard_map(body, mesh=mesh, in_specs=in_specs, out_specs=out_specs, check_vma=False)
```

```python
import jax
import jax.numpy as jnp
from jax import lax
from jax.experimental import pallas as pl
from jax.experimental.pallas import tpu as pltpu
from jax.sharding import PartitionSpec as P

epsilon = 1e-06
max_norm = 500.0
C = 96
W = 256
PACKED_ROWS = 4096
LANES = 128
VECTOR_ROW = 7 * 6 * C
MESH = pl.DeviceIdType.MESH
f32, bf16 = jnp.float32, jnp.bfloat16


def dot_nt(a, b):
    return lax.dot_general(a, b, (((1,), (1,)), ((), ())), preferred_element_type=f32)


def dot_nn(a, b):
    return lax.dot_general(a, b, (((1,), (0,)), ((), ())), preferred_element_type=f32)


def eye_mask():
    rows = lax.broadcasted_iota(jnp.int32, (C, C), 0)
    return rows == lax.broadcasted_iota(jnp.int32, (C, C), 1)


def to_column(row):
    spread = jnp.broadcast_to(row, (C, C))
    return jnp.sum(jnp.where(eye_mask(), spread, 0.0), axis=1, keepdims=True)


def to_row(column):
    spread = jnp.broadcast_to(column, (C, C))
    return jnp.sum(jnp.where(eye_mask(), spread, 0.0), axis=0, keepdims=True)


def shift_columns(values, offset):
    if offset == 0:
        return values
    column = lax.broadcasted_iota(jnp.int32, values.shape, 1)
    rolled = pltpu.roll(values, (-offset) % W, 1)
    edge = W - 1 if offset > 0 else 0
    return jnp.where(column == edge, 0.0, rolled)


def normalised(values):
    meansq = jnp.mean(values * values, axis=0, keepdims=True)
    inverse = lax.rsqrt(meansq + epsilon)
    return values * inverse, inverse


def act_parts(values, gain):
    unit, inverse = normalised(values)
    scaled = unit * gain
    gate = 1.0 / (1.0 + jnp.exp(-scaled))
    slope = gate * (1.0 + scaled * (1.0 - gate))
    return scaled * gate, slope, unit, inverse


def back_through_norm(grad_scaled, gain, unit, inverse):
    grad_unit = grad_scaled * gain
    return inverse * (grad_unit - unit * jnp.mean(grad_unit * unit, axis=0, keepdims=True))


CELLS = [(p, q) for p in range(3) for q in range(3)]
OWN = CELLS.index((2, 1))
ORDER = [7, 6, 8, 4, 1, 3, 5, 0, 2]


def band_of(cell):
    return pl.ds(cell * C, C)


def block_kernel(x_ref, cot_ref, gain_first_ref, gain_second_ref, bias_ref, k1_hbm, k2_hbm,
                 g_ref, grad_in_ref,
                 k1, k2, k1t, k2t, x_cells, c_cells, h_cells, f_cells, d_cells,
                 second3, hidden3, packed,
                 core_in, part, x_out, x_in, y_in, y_own, z_in, z_all,
                 local_sem, hx_sem, hc_sem, hh_sem,
                 core_sem, x_sem, y_sem, z_sem, gz_sem, gy_sem, gx_sem, gc_sem):
    tm, row = lax.axis_index("tm"), lax.axis_index("row")
    me_x, me_c = tm // 2, tm % 2
    me_z, me_y = row // 8, row % 8
    peer_c = {"tm": me_x * 2 + 1 - me_c, "row": row}

    def at_x(d):
        return lax.rem(me_x + d, 4)

    def at_y(d):
        return lax.rem(me_y + d, 8)

    def at_z(d):
        return lax.rem(me_z + d, 8)

    def peer_x(d):
        return {"tm": at_x(d) * 2 + me_c, "row": row}

    def peer_y(d):
        return {"tm": tm, "row": me_z * 8 + at_y(d)}

    def peer_z(d):
        return {"tm": tm, "row": at_z(d) * 8 + me_y}

    def later(cell):
        p, q = CELLS[cell]
        return {"tm": lax.rem(tm + 2 - p, 8), "row": lax.rem(row + 65 - q, 64)}

    def earlier(cell):
        p, q = CELLS[cell]
        return {"tm": lax.rem(tm + 6 + p, 8), "row": lax.rem(row + 63 + q, 64)}

    def send(src, dst, sems, slot, device):
        copy = pltpu.make_async_remote_copy(
            src_ref=src, dst_ref=dst, send_sem=sems.at[0, slot], recv_sem=sems.at[1, slot],
            device_id=device, device_id_type=MESH,
        )
        copy.start()
        return copy

    load_k1 = pltpu.make_async_copy(k1_hbm, k1, local_sem.at[0])
    load_k2 = pltpu.make_async_copy(k2_hbm, k2, local_sem.at[1])
    load_k1.start()
    load_k2.start()

    barrier = pltpu.get_barrier_semaphore()
    halo = [cell for cell in ORDER if cell != OWN]
    peers = [later(cell) for cell in halo] + [earlier(cell) for cell in halo]
    peers += [peer_c] + [peer_x(d) for d in range(1, 4)]
    peers += [peer_y(d) for d in range(1, 8)] + [peer_z(d) for d in range(1, 8)]
    for peer in peers:
        pl.semaphore_signal(barrier, inc=1, device_id=peer, device_id_type=MESH)
    pl.semaphore_wait(barrier, len(peers))

    sent = []
    x_copies, c_copies = {}, {}
    for cell in halo:
        x_copies[cell] = send(x_ref, x_cells.at[cell], hx_sem, cell, later(cell))
        c_copies[cell] = send(cot_ref, c_cells.at[band_of(cell)], hc_sem, cell, earlier(cell))
    sent += list(x_copies.values()) + list(c_copies.values())

    gain_first = to_column(gain_first_ref[...])
    gain_second = to_column(gain_second_ref[...])
    bias = to_column(bias_ref[...])
    identity = jnp.where(eye_mask(), 1.0, 0.0).astype(bf16)
    load_k1.wait()
    load_k2.wait()
    for cell in range(9):
        for s in range(3):
            band = pl.ds(s * C, C)
            k2t[cell, band, :] = dot_nt(identity, k2[cell, band, :]).astype(bf16)
            k1t[cell, band, :] = dot_nt(identity, k1[cell, band, :]).astype(bf16)

    pad = jnp.zeros((32, W), bf16)
    f_cells[pl.ds(9 * C, 32), :] = pad
    c_cells[pl.ds(9 * C, 32), :] = pad
    c_own = cot_ref[...]
    c_cells[band_of(OWN), :] = c_own

    def before(cell):
        p, q = CELLS[cell]
        return (tm + p >= 2) & (row + q >= 1) & (row + q <= 64)

    def after(cell):
        p, q = CELLS[cell]
        return (tm + 2 - p <= 7) & (row + 1 - q >= 0) & (row + 1 - q <= 63)

    sums = jnp.zeros((3 * C, W), f32)
    for cell in ORDER:
        if cell == OWN:
            wide = x_ref[...].astype(f32)
        else:
            x_copies[cell].wait_recv()

            @pl.when(jnp.logical_not(before(cell)))
            def _():
                x_cells[cell] = jnp.zeros((C, W), bf16)

            wide = x_cells[cell].astype(f32)
        value, slope, unit, inverse = act_parts(wide, gain_first)
        if cell == OWN:
            own_slope, own_unit, own_inverse = slope, unit, inverse
        band = band_of(cell)
        rounded = value.astype(bf16)
        f_cells[band, :] = rounded
        d_cells[band, :] = (slope * unit).astype(bf16)
        sums = sums + dot_nn(k1[cell], rounded)
    hidden = shift_columns(sums[:C], -1) + sums[C : 2 * C] + shift_columns(sums[2 * C :], 1)
    hidden = hidden + bias
    second, slope, unit, inverse = act_parts(hidden, gain_second)
    second = second.astype(bf16).astype(f32)
    for s in range(3):
        second3[pl.ds(s * C, C), :] = shift_columns(second, s - 1).astype(bf16)

    sums = jnp.zeros((3 * C, W), f32)
    for cell in ORDER:
        if cell != OWN:
            c_copies[cell].wait_recv()

            @pl.when(jnp.logical_not(after(cell)))
            def _():
                c_cells[band_of(cell), :] = jnp.zeros((C, W), bf16)

        sums = sums + dot_nn(k2t[cell], c_cells[band_of(cell), :])
    grad_second = shift_columns(sums[:C], 1) + sums[C : 2 * C] + shift_columns(sums[2 * C :], -1)
    grad_scaled = grad_second * slope
    raw_gain_second = jnp.sum(grad_scaled * unit, axis=1, keepdims=True)
    grad_hidden = back_through_norm(grad_scaled, gain_second, unit, inverse)
    raw_bias = jnp.sum(grad_hidden, axis=1, keepdims=True)
    rounded = grad_hidden.astype(bf16)
    raw_cot = jnp.sum(c_own.astype(f32), axis=1, keepdims=True)
    hidden_cot = rounded.astype(f32)
    for s in range(3):
        hidden3[pl.ds(s * C, C), :] = shift_columns(hidden_cot, 1 - s).astype(bf16)
    h_own = pl.ds(C, C)
    h_copies = {}
    for cell in halo:
        h_copies[cell] = send(hidden3.at[h_own], h_cells.at[cell], hh_sem, cell, earlier(cell))
    sent += list(h_copies.values())

    raw = dot_nt(second3[...], c_cells[...])
    for j in range(7):
        packed[pl.ds(j * 6 * C + 3 * C, 3 * C), :] = raw[:, j * LANES : (j + 1) * LANES]
    raw = dot_nt(hidden3[...], f_cells[...])
    for j in range(7):
        packed[pl.ds(j * 6 * C, 3 * C), :] = raw[:, j * LANES : (j + 1) * LANES]
    gained = jnp.zeros((3 * C, C), f32)
    for cell in range(9):
        gained = gained + k1[cell].astype(f32) * dot_nt(hidden3[...], d_cells[band_of(cell), :])
    packed[pl.ds(VECTOR_ROW, PACKED_ROWS - VECTOR_ROW), :] = jnp.zeros(
        (PACKED_ROWS - VECTOR_ROW, LANES), f32
    )
    packed[pl.ds(VECTOR_ROW, 1), pl.ds(0, C)] = to_row(raw_bias)
    packed[pl.ds(VECTOR_ROW + 1, 1), pl.ds(0, C)] = jnp.sum(gained, axis=0, keepdims=True)
    packed[pl.ds(VECTOR_ROW + 2, 1), pl.ds(0, C)] = to_row(raw_gain_second)
    packed[pl.ds(VECTOR_ROW + 3, 1), pl.ds(0, C)] = to_row(raw_cot)

    halves = []
    for k in range(4):
        chunk = at_x(k + 1) * 512
        theirs = pl.ds(pl.multiple_of((1 - me_c) * 2048 + chunk, 512), 512)
        land = pl.ds(pl.multiple_of(chunk, 512), 512)
        halves.append(send(packed.at[theirs], core_in.at[land], core_sem, k, peer_c))
    arrivals = []
    for k in range(4):
        halves[k].wait_recv()
        chunk = at_x(k + 1) * 512
        mine = pl.ds(pl.multiple_of(me_c * 2048 + chunk, 512), 512)
        land = pl.ds(pl.multiple_of(chunk, 512), 512)
        total = packed[mine, :] + core_in[land, :]
        if k < 3:
            x_out[k] = total.astype(jnp.bfloat16)
            arrivals.append(send(x_out.at[k], x_in.at[k], x_sem, k, peer_x(k + 1)))
        else:
            part[...] = total
    sent += halves + arrivals

    sums = dot_nn(k1t[OWN], hidden3[h_own, :])
    for cell in ORDER[1:]:
        h_copies[cell].wait_recv()

        @pl.when(jnp.logical_not(after(cell)))
        def _():
            h_cells[cell] = jnp.zeros((C, W), bf16)

        sums = sums + dot_nn(k1t[cell], h_cells[cell])
    grad_first = shift_columns(sums[:C], 1) + sums[C : 2 * C] + shift_columns(sums[2 * C :], -1)
    input_term = back_through_norm(grad_first * own_slope, gain_first, own_unit, own_inverse)
    grad_in_ref[...] = (c_own.astype(f32) + input_term).astype(bf16)

    for copy in arrivals:
        copy.wait_recv()
    total = part[...]
    for k in range(3):
        total = total + x_in[k].astype(jnp.float32)
    part[...] = total
    arrivals = []
    for d in range(1, 8):
        theirs = pl.ds(pl.multiple_of(at_y(d) * 64, 64), 64)
        arrivals.append(send(part.at[theirs], y_in.at[d - 1], y_sem, d - 1, peer_y(d)))
    sent += arrivals
    for copy in arrivals:
        copy.wait_recv()
    total = part[pl.ds(pl.multiple_of(me_y * 64, 64), 64), :]
    for k in range(7):
        total = total + y_in[k]
    y_own[...] = total
    arrivals = []
    for d in range(1, 8):
        theirs = pl.ds(pl.multiple_of(at_z(d) * 8, 8), 8)
        arrivals.append(send(y_own.at[theirs], z_in.at[d - 1], z_sem, d - 1, peer_z(d)))
    sent += arrivals
    for copy in arrivals:
        copy.wait_recv()
    own = pl.ds(pl.multiple_of(me_z * 8, 8), 8)
    total = y_own[own, :]
    for k in range(7):
        total = total + z_in[k]
    z_all[own, :] = total
    arrivals = []
    for d in range(1, 8):
        arrivals.append(send(z_all.at[own], z_all.at[own], gz_sem, d - 1, peer_z(d)))
    sent += arrivals
    for copy in arrivals:
        copy.wait_recv()
    base = me_c * 2048 + me_x * 512
    mine = pl.ds(pl.multiple_of(base + me_y * 64, 64), 64)
    g_ref[mine, :] = z_all[...].astype(jnp.bfloat16)
    arrivals = []
    for d in range(1, 8):
        arrivals.append(send(g_ref.at[mine], g_ref.at[mine], gy_sem, d - 1, peer_y(d)))
    sent += arrivals
    for copy in arrivals:
        copy.wait_recv()
    mine = pl.ds(pl.multiple_of(base, 512), 512)
    arrivals = []
    for d in range(1, 4):
        arrivals.append(send(g_ref.at[mine], g_ref.at[mine], gx_sem, d - 1, peer_x(d)))
    cores = [send(g_ref.at[mine], g_ref.at[mine], gc_sem, 0, peer_c)]
    sent += arrivals
    for d in range(1, 4):
        arrivals[d - 1].wait_recv()
        there = pl.ds(pl.multiple_of(me_c * 2048 + at_x(4 - d) * 512, 512), 512)
        cores.append(send(g_ref.at[there], g_ref.at[there], gc_sem, d, peer_c))
    sent += cores
    for copy in cores:
        copy.wait_recv()
    for copy in sent:
        copy.wait_send()


def scale_kernel(g_ref, first_ref, second_ref, vectors_ref):
    squares = jnp.zeros((512, LANES), f32)
    for k in range(8):
        part = g_ref[pl.ds(k * 512, 512), :].astype(f32)
        squares = squares + part * part
    squares = jnp.sum(jnp.sum(squares, axis=0, keepdims=True), axis=1, keepdims=True)
    total = jnp.sqrt(squares)
    factor = jnp.minimum(1.0, max_norm / (total + epsilon))
    target = lax.broadcasted_iota(jnp.int32, (C, LANES), 0)
    lane = lax.broadcasted_iota(jnp.int32, (C, LANES), 1)
    for cell in range(9):
        tiles = range(cell * C // LANES, (cell * C + C - 1) // LANES + 1)
        first = jnp.zeros((3 * C, C), f32)
        second = [jnp.zeros((C, C), f32) for _ in range(3)]
        for j in tiles:
            pick = jnp.where(lane + (j * LANES - cell * C) == target, 1.0, 0.0).astype(bf16)
            first = first + dot_nt(g_ref[pl.ds(j * 6 * C, 3 * C), :], pick)
            for s in range(3):
                start = j * 6 * C + 3 * C + s * C
                second[s] = second[s] + dot_nt(pick, g_ref[pl.ds(start, C), :])
        first_ref[cell] = first * factor
        for s in range(3):
            second_ref[cell, pl.ds(s * C, C), :] = second[s] * factor
    vectors = g_ref[pl.ds(VECTOR_ROW, 16), :].astype(f32)
    vectors_ref[...] = vectors[:4, :C] * factor


def body(inputs, cotangent, gain_first, gain_second, bias_first, kernel_first, kernel_second):
    dma, vmem = pltpu.SemaphoreType.DMA, pltpu.VMEM
    in_vmem = pl.BlockSpec(memory_space=pltpu.VMEM)
    in_any = pl.BlockSpec(memory_space=pl.ANY)
    summed, grad_inputs = pl.pallas_call(
        block_kernel,
        out_shape=(
            jax.ShapeDtypeStruct((PACKED_ROWS, LANES), bf16),
            jax.ShapeDtypeStruct((C, W), bf16),
        ),
        in_specs=[in_vmem] * 5 + [in_any] * 2,
        out_specs=(in_vmem, in_vmem),
        scratch_shapes=[
            vmem((9, 3 * C, C), bf16), vmem((9, 3 * C, C), bf16),
            vmem((9, 3 * C, C), bf16), vmem((9, 3 * C, C), bf16),
            vmem((9, C, W), bf16), vmem((9 * C + 32, W), bf16), vmem((9, C, W), bf16),
            vmem((9 * C + 32, W), bf16), vmem((9 * C, W), bf16),
            vmem((3 * C, W), bf16), vmem((3 * C, W), bf16),
            vmem((PACKED_ROWS, LANES), f32),
            vmem((2048, LANES), f32),
            vmem((512, LANES), f32),
            vmem((3, 512, LANES), bf16),
            vmem((3, 512, LANES), bf16),
            vmem((7, 64, LANES), f32),
            vmem((64, LANES), f32),
            vmem((7, 8, LANES), f32),
            vmem((64, LANES), f32),
            dma((2,)), dma((2, 9)), dma((2, 9)), dma((2, 9)),
            dma((2, 4)), dma((2, 3)), dma((2, 7)), dma((2, 7)),
            dma((2, 7)), dma((2, 7)), dma((2, 3)), dma((2, 4)),
        ],
        compiler_params=pltpu.CompilerParams(
            collective_id=0, has_side_effects=True, vmem_limit_bytes=48 * 1024 * 1024
        ),
    )(
        inputs.reshape(C, W), cotangent.reshape(C, W),
        gain_first.reshape(1, C), gain_second.reshape(1, C), bias_first.reshape(1, C),
        kernel_first.reshape(9, 3 * C, C), kernel_second.reshape(9, 3 * C, C),
    )
    grad_first, grad_second, vectors = pl.pallas_call(
        scale_kernel,
        out_shape=(
            jax.ShapeDtypeStruct((9, 3 * C, C), f32),
            jax.ShapeDtypeStruct((9, 3 * C, C), f32),
            jax.ShapeDtypeStruct((4, C), f32),
        ),
        in_specs=[in_vmem],
        out_specs=(in_vmem,) * 3,
        compiler_params=pltpu.CompilerParams(vmem_limit_bytes=32 * 1024 * 1024),
    )(summed)
    return (
        grad_inputs.reshape(inputs.shape),
        grad_first.reshape(kernel_first.shape),
        grad_second.reshape(kernel_second.shape),
        vectors,
    )


def solution(mesh):
    in_specs = (P(None, "tm", "row", None), P(None, "tm", "row", None), P(), P(), P(), P(), P())
    out_specs = (P(None, "tm", "row", None), P(), P(), P())
    return jax.shard_map(body, mesh=mesh, in_specs=in_specs, out_specs=out_specs, check_vma=False)
```

```python
import jax
import jax.numpy as jnp
from jax import lax
from jax.experimental import pallas as pl
from jax.experimental.pallas import tpu as pltpu
from jax.sharding import PartitionSpec as P

epsilon = 1e-06
max_norm = 500.0
C = 96
W = 256
HALF_ROWS = 2048
LANES = 128
VECTOR_ROW = 7 * 3 * C
MESH = pl.DeviceIdType.MESH
f32, bf16 = jnp.float32, jnp.bfloat16


def dot_nt(a, b):
    return lax.dot_general(a, b, (((1,), (1,)), ((), ())), preferred_element_type=f32)


def dot_nn(a, b):
    return lax.dot_general(a, b, (((1,), (0,)), ((), ())), preferred_element_type=f32)


def eye_mask():
    rows = lax.broadcasted_iota(jnp.int32, (C, C), 0)
    return rows == lax.broadcasted_iota(jnp.int32, (C, C), 1)


def to_column(row):
    spread = jnp.broadcast_to(row, (C, C))
    return jnp.sum(jnp.where(eye_mask(), spread, 0.0), axis=1, keepdims=True)


def to_row(column):
    spread = jnp.broadcast_to(column, (C, C))
    return jnp.sum(jnp.where(eye_mask(), spread, 0.0), axis=0, keepdims=True)


def shift_columns(values, offset):
    if offset == 0:
        return values
    column = lax.broadcasted_iota(jnp.int32, values.shape, 1)
    rolled = pltpu.roll(values, (-offset) % W, 1)
    edge = W - 1 if offset > 0 else 0
    return jnp.where(column == edge, 0.0, rolled)


def normalised(values):
    meansq = jnp.mean(values * values, axis=0, keepdims=True)
    inverse = lax.rsqrt(meansq + epsilon)
    return values * inverse, inverse


def act_parts(values, gain):
    unit, inverse = normalised(values)
    scaled = unit * gain
    gate = 1.0 / (1.0 + jnp.exp(-scaled))
    slope = gate * (1.0 + scaled * (1.0 - gate))
    return scaled * gate, slope, unit, inverse


def back_through_norm(grad_scaled, gain, unit, inverse):
    grad_unit = grad_scaled * gain
    return inverse * (grad_unit - unit * jnp.mean(grad_unit * unit, axis=0, keepdims=True))


CELLS = [(p, q) for p in range(3) for q in range(3)]
OWN = CELLS.index((2, 1))
ORDER = [7, 6, 8, 4, 1, 3, 5, 0, 2]


FAR_FIRST = (4, 5, 3, 6, 2, 7, 1, 0)


def band_of(cell):
    return pl.ds(cell * C, C)


def put_rows(packed, half, raw):
    for n in range(63):
        start = n * 32
        j, r = start // (3 * C), start % (3 * C)
        block = start // 64
        packed[half, block // 8, block % 8, pl.ds(start % 64, 32), :] = raw[
            r : r + 32, j * LANES : (j + 1) * LANES
        ]


def block_kernel(x_hbm, cot_hbm, gain_first_hbm, gain_second_hbm, bias_hbm, k1_hbm, k2_hbm,
                 g_ref, grad_in_ref,
                 x_ref, cot_ref, gain_first_ref, gain_second_ref, bias_ref, k1, k2, k1t, k2t, x_cells, c_cells, h_cells, f_cells, d_cells,
                 second3, hidden3, packed,
                 core_in, part, x_out, x_in, y_out, y_in, z_in,
                 local_sem, hx_sem, hc_sem, hh_sem,
                 core_sem, x_sem, y_sem, z_sem, gy_sem, gx_sem, gc_sem):
    tm, row = lax.axis_index("tm"), lax.axis_index("row")
    me_x, me_c = tm // 2, tm % 2
    me_z, me_y = row // 8, row % 8
    peer_c = {"tm": me_x * 2 + 1 - me_c, "row": row}

    def at_x(d):
        return lax.rem(me_x + d, 4)

    def at_y(d):
        return lax.rem(me_y + d, 8)

    def at_z(d):
        return lax.rem(me_z + d, 8)

    def peer_x(d):
        return {"tm": at_x(d) * 2 + me_c, "row": row}

    def peer_y(d):
        return {"tm": tm, "row": me_z * 8 + at_y(d)}

    def peer_z(d):
        return {"tm": tm, "row": at_z(d) * 8 + me_y}

    def later(cell):
        p, q = CELLS[cell]
        return {"tm": lax.rem(tm + 2 - p, 8), "row": lax.rem(row + 65 - q, 64)}

    def earlier(cell):
        p, q = CELLS[cell]
        return {"tm": lax.rem(tm + 6 + p, 8), "row": lax.rem(row + 63 + q, 64)}

    def send(src, dst, sems, slot, device):
        copy = pltpu.make_async_remote_copy(
            src_ref=src, dst_ref=dst, send_sem=sems.at[0, slot], recv_sem=sems.at[1, slot],
            device_id=device, device_id_type=MESH,
        )
        copy.start()
        return copy

    pairs = [(x_hbm, x_ref), (cot_hbm, cot_ref), (gain_first_hbm, gain_first_ref),
             (gain_second_hbm, gain_second_ref), (bias_hbm, bias_ref), (k1_hbm, k1), (k2_hbm, k2)]
    loads = [pltpu.make_async_copy(a, b, local_sem.at[k]) for k, (a, b) in enumerate(pairs)]
    for load in loads:
        load.start()

    barrier = pltpu.get_barrier_semaphore()
    halo = [cell for cell in ORDER if cell != OWN]
    peers = [later(cell) for cell in halo] + [earlier(cell) for cell in halo]
    peers += [peer_c] + [peer_x(d) for d in range(1, 4)]
    peers += [peer_y(d) for d in range(1, 8)] + [peer_z(d) for d in range(1, 8)]
    for peer in peers:
        pl.semaphore_signal(barrier, inc=1, device_id=peer, device_id_type=MESH)
    for load in loads[:2]:
        load.wait()
    pl.semaphore_wait(barrier, len(peers))

    sent = []
    x_copies, c_copies = {}, {}
    for cell in halo:
        x_copies[cell] = send(x_ref, x_cells.at[cell], hx_sem, cell, later(cell))
        c_copies[cell] = send(cot_ref, c_cells.at[band_of(cell)], hc_sem, cell, earlier(cell))
    sent += list(x_copies.values()) + list(c_copies.values())

    for load in loads[2:]:
        load.wait()
    gain_first = to_column(gain_first_ref[...])
    gain_second = to_column(gain_second_ref[...])
    bias = to_column(bias_ref[...])
    identity = jnp.where(eye_mask(), 1.0, 0.0).astype(bf16)
    for cell in range(9):
        for s in range(3):
            band = pl.ds(s * C, C)
            k2t[cell, band, :] = dot_nt(identity, k2[cell, band, :]).astype(bf16)
            k1t[cell, band, :] = dot_nt(identity, k1[cell, band, :]).astype(bf16)

    pad = jnp.zeros((32, W), bf16)
    f_cells[pl.ds(9 * C, 32), :] = pad
    c_cells[pl.ds(9 * C, 32), :] = pad
    c_own = cot_ref[...]
    c_cells[band_of(OWN), :] = c_own

    def before(cell):
        p, q = CELLS[cell]
        return (tm + p >= 2) & (row + q >= 1) & (row + q <= 64)

    def after(cell):
        p, q = CELLS[cell]
        return (tm + 2 - p <= 7) & (row + 1 - q >= 0) & (row + 1 - q <= 63)

    sums = jnp.zeros((3 * C, W), f32)
    for cell in ORDER:
        if cell == OWN:
            wide = x_ref[...].astype(f32)
        else:
            x_copies[cell].wait_recv()

            @pl.when(jnp.logical_not(before(cell)))
            def _():
                x_cells[cell] = jnp.zeros((C, W), bf16)

            wide = x_cells[cell].astype(f32)
        value, slope, unit, inverse = act_parts(wide, gain_first)
        if cell == OWN:
            own_slope, own_unit, own_inverse = slope, unit, inverse
        band = band_of(cell)
        rounded = value.astype(bf16)
        f_cells[band, :] = rounded
        d_cells[band, :] = (slope * unit).astype(bf16)
        sums = sums + dot_nn(k1[cell], rounded)
    hidden = shift_columns(sums[:C], -1) + sums[C : 2 * C] + shift_columns(sums[2 * C :], 1)
    hidden = hidden + bias
    second, slope, unit, inverse = act_parts(hidden, gain_second)
    second = second.astype(bf16).astype(f32)
    for s in range(3):
        second3[pl.ds(s * C, C), :] = shift_columns(second, s - 1).astype(bf16)

    sums = jnp.zeros((3 * C, W), f32)
    for cell in ORDER:
        if cell != OWN:
            c_copies[cell].wait_recv()

            @pl.when(jnp.logical_not(after(cell)))
            def _():
                c_cells[band_of(cell), :] = jnp.zeros((C, W), bf16)

        sums = sums + dot_nn(k2t[cell], c_cells[band_of(cell), :])
    grad_second = shift_columns(sums[:C], 1) + sums[C : 2 * C] + shift_columns(sums[2 * C :], -1)
    grad_scaled = grad_second * slope
    raw_gain_second = jnp.sum(grad_scaled * unit, axis=1, keepdims=True)
    grad_hidden = back_through_norm(grad_scaled, gain_second, unit, inverse)
    raw_bias = jnp.sum(grad_hidden, axis=1, keepdims=True)
    rounded = grad_hidden.astype(bf16)
    raw_cot = jnp.sum(c_own.astype(f32), axis=1, keepdims=True)
    hidden_cot = rounded.astype(f32)
    for s in range(3):
        hidden3[pl.ds(s * C, C), :] = shift_columns(hidden_cot, 1 - s).astype(bf16)
    h_own = pl.ds(C, C)
    h_copies = {}
    for cell in halo:
        h_copies[cell] = send(hidden3.at[h_own], h_cells.at[cell], hh_sem, cell, earlier(cell))
    sent += list(h_copies.values())

    put_rows(packed, 1, dot_nt(second3[...], c_cells[...]))
    put_rows(packed, 0, dot_nt(hidden3[...], f_cells[...]))
    gained = jnp.zeros((3 * C, C), f32)
    for cell in range(9):
        gained = gained + k1[cell].astype(f32) * dot_nt(hidden3[...], d_cells[band_of(cell), :])
    packed[0, 3, 7, pl.ds(32, 32), :] = jnp.zeros((32, LANES), f32)
    packed[1, 3, 7, pl.ds(32, 32), :] = jnp.zeros((32, LANES), f32)
    lanes = pl.ds(0, C)
    packed[0, 3, 7, pl.ds(32, 1), lanes] = to_row(raw_bias)
    packed[0, 3, 7, pl.ds(33, 1), lanes] = jnp.sum(gained, axis=0, keepdims=True)
    packed[0, 3, 7, pl.ds(34, 1), lanes] = to_row(raw_gain_second)
    packed[0, 3, 7, pl.ds(35, 1), lanes] = to_row(raw_cot)

    core_copies = []
    for k, d in enumerate(FAR_FIRST):
        core_copies.append(send(packed.at[1 - me_c, :, at_y(d)], core_in.at[k], core_sem, k, peer_c))
    x_copies = []
    for k, d in enumerate(FAR_FIRST):
        core_copies[k].wait_recv()
        total = packed[me_c, :, at_y(d)] + core_in[k]
        x_out[k] = total.astype(bf16)
        part[k] = packed[me_c, me_x, at_y(d)] + core_in[k, me_x]
        for e in (2, 1, 3):
            x_copies.append(
                send(x_out.at[k, at_x(e)], x_in.at[k, e - 1], x_sem, k * 3 + e - 1, peer_x(e))
            )
    sent += core_copies + x_copies

    sums = dot_nn(k1t[OWN], hidden3[h_own, :])
    for cell in ORDER[1:]:
        h_copies[cell].wait_recv()

        @pl.when(jnp.logical_not(after(cell)))
        def _():
            h_cells[cell] = jnp.zeros((C, W), bf16)

        sums = sums + dot_nn(k1t[cell], h_cells[cell])
    grad_first = shift_columns(sums[:C], 1) + sums[C : 2 * C] + shift_columns(sums[2 * C :], -1)
    input_term = back_through_norm(grad_first * own_slope, gain_first, own_unit, own_inverse)
    grad_in_ref[...] = (c_own.astype(f32) + input_term).astype(bf16)

    y_copies = []
    for k, d in enumerate(FAR_FIRST):
        total = part[k]
        for copy in x_copies[3 * k : 3 * k + 3]:
            copy.wait_recv()
        for e in range(3):
            total = total + x_in[k, e].astype(f32)
        if d > 0:
            y_out[k] = total.astype(bf16)
            y_copies.append(send(y_out.at[k], y_in.at[d - 1], y_sem, d - 1, peer_y(d)))
    for copy in y_copies:
        copy.wait_recv()
    for e in range(7):
        total = total + y_in[e].astype(f32)

    z_in[me_z] = total.astype(bf16)
    z_copies = []
    for d in (4, 3, 5, 2, 6, 1, 7):
        z_copies.append(send(z_in.at[me_z], z_in.at[me_z], z_sem, d - 1, peer_z(d)))
    for copy in z_copies:
        copy.wait_recv()
    total = z_in[0].astype(f32)
    for e in range(1, 8):
        total = total + z_in[e].astype(f32)
    g_ref[me_c, me_x, me_y] = total.astype(bf16)
    sent += y_copies + z_copies

    own = g_ref.at[me_c, me_x, me_y]
    gy_copies, gx_copies, gc_copies = {}, {}, []
    for d in (4, 3, 5, 2, 6, 1, 7):
        gy_copies[d] = send(own, own, gy_sem, d - 1, peer_y(d))
    for k, d in enumerate((0, 1, 7, 2, 6, 3, 5, 4)):
        piece = g_ref.at[me_c, me_x, at_y(8 - d)]
        if d > 0:
            gy_copies[d].wait_recv()
        for e in (2, 1, 3):
            gx_copies[k, e] = send(piece, piece, gx_sem, k * 3 + e - 1, peer_x(e))
        gc_copies.append(send(piece, piece, gc_sem, k * 4, peer_c))
    for k, d in enumerate((0, 1, 7, 2, 6, 3, 5, 4)):
        for e in (1, 3, 2):
            gx_copies[k, e].wait_recv()
            piece = g_ref.at[me_c, at_x(4 - e), at_y(8 - d)]
            gc_copies.append(send(piece, piece, gc_sem, k * 4 + e, peer_c))
    sent += list(gy_copies.values()) + list(gx_copies.values()) + gc_copies
    for copy in gc_copies:
        copy.wait_recv()
    for copy in sent:
        copy.wait_send()


def scale_kernel(g_ref, grad_in_ref, first_ref, second_ref, vectors_ref, copy_ref):
    copy_ref[...] = grad_in_ref[...]
    squares = jnp.zeros((512, LANES), f32)
    for k in range(8):
        part = g_ref[pl.ds(k * 512, 512), :].astype(f32)
        squares = squares + part * part
    squares = jnp.sum(jnp.sum(squares, axis=0, keepdims=True), axis=1, keepdims=True)
    total = jnp.sqrt(squares)
    factor = jnp.minimum(1.0, max_norm / (total + epsilon))
    target = lax.broadcasted_iota(jnp.int32, (C, LANES), 0)
    lane = lax.broadcasted_iota(jnp.int32, (C, LANES), 1)
    for cell in range(9):
        tiles = range(cell * C // LANES, (cell * C + C - 1) // LANES + 1)
        first = jnp.zeros((3 * C, C), f32)
        second = [jnp.zeros((C, C), f32) for _ in range(3)]
        for j in tiles:
            pick = jnp.where(lane + (j * LANES - cell * C) == target, 1.0, 0.0).astype(bf16)
            first = first + dot_nt(g_ref[pl.ds(j * 3 * C, 3 * C), :], pick)
            for s in range(3):
                start = HALF_ROWS + j * 3 * C + s * C
                second[s] = second[s] + dot_nt(pick, g_ref[pl.ds(start, C), :])
        first_ref[cell] = first * factor
        for s in range(3):
            second_ref[cell, pl.ds(s * C, C), :] = second[s] * factor
    vectors = g_ref[pl.ds(VECTOR_ROW, 16), :].astype(f32)
    vectors_ref[...] = vectors[:4, :C] * factor


def body(inputs, cotangent, gain_first, gain_second, bias_first, kernel_first, kernel_second):
    dma, vmem = pltpu.SemaphoreType.DMA, pltpu.VMEM
    in_vmem = pl.BlockSpec(memory_space=pltpu.VMEM)
    in_any = pl.BlockSpec(memory_space=pl.ANY)
    summed, grad_inputs = pl.pallas_call(
        block_kernel,
        out_shape=(
            jax.ShapeDtypeStruct((2, 4, 8, 64, LANES), bf16),
            jax.ShapeDtypeStruct((C, W), bf16),
        ),
        in_specs=[in_any] * 7,
        out_specs=(in_vmem, in_vmem),
        scratch_shapes=[
            vmem((C, W), bf16), vmem((C, W), bf16),
            vmem((1, C), f32), vmem((1, C), f32), vmem((1, C), f32),
            vmem((9, 3 * C, C), bf16), vmem((9, 3 * C, C), bf16),
            vmem((9, 3 * C, C), bf16), vmem((9, 3 * C, C), bf16),
            vmem((9, C, W), bf16), vmem((9 * C + 32, W), bf16), vmem((9, C, W), bf16),
            vmem((9 * C + 32, W), bf16), vmem((9 * C, W), bf16),
            vmem((3 * C, W), bf16), vmem((3 * C, W), bf16),
            vmem((2, 4, 8, 64, LANES), f32),
            vmem((8, 4, 64, LANES), f32),
            vmem((8, 64, LANES), f32),
            vmem((8, 4, 64, LANES), bf16),
            vmem((8, 3, 64, LANES), bf16),
            vmem((7, 64, LANES), bf16),
            vmem((7, 64, LANES), bf16),
            vmem((8, 64, LANES), bf16),
            dma((7,)), dma((2, 9)), dma((2, 9)), dma((2, 9)),
            dma((2, 8)), dma((2, 24)), dma((2, 7)), dma((2, 7)),
            dma((2, 7)), dma((2, 24)), dma((2, 32)),
        ],
        compiler_params=pltpu.CompilerParams(
            collective_id=0, has_side_effects=True, vmem_limit_bytes=60 * 1024 * 1024
        ),
    )(
        inputs.reshape(C, W), cotangent.reshape(C, W),
        gain_first.reshape(1, C), gain_second.reshape(1, C), bias_first.reshape(1, C),
        kernel_first.reshape(9, 3 * C, C), kernel_second.reshape(9, 3 * C, C),
    )
    grad_first, grad_second, vectors, grad_inputs = pl.pallas_call(
        scale_kernel,
        out_shape=(
            jax.ShapeDtypeStruct((9, 3 * C, C), f32),
            jax.ShapeDtypeStruct((9, 3 * C, C), f32),
            jax.ShapeDtypeStruct((4, C), f32),
            jax.ShapeDtypeStruct((C, W), bf16),
        ),
        in_specs=[in_vmem] * 2,
        out_specs=(in_vmem,) * 4,
        compiler_params=pltpu.CompilerParams(vmem_limit_bytes=32 * 1024 * 1024),
    )(summed.reshape(2 * HALF_ROWS, LANES), grad_inputs)
    return (
        grad_inputs.reshape(inputs.shape),
        grad_first.reshape(kernel_first.shape),
        grad_second.reshape(kernel_second.shape),
        vectors,
    )


def solution(mesh):
    in_specs = (P(None, "tm", "row", None), P(None, "tm", "row", None), P(), P(), P(), P(), P())
    out_specs = (P(None, "tm", "row", None), P(), P(), P())
    return jax.shard_map(body, mesh=mesh, in_specs=in_specs, out_specs=out_specs, check_vma=False)
```

```python
import jax
import jax.numpy as jnp
from jax import lax
from jax.experimental import pallas as pl
from jax.experimental.pallas import tpu as pltpu
from jax.sharding import PartitionSpec as P

epsilon = 1e-06
max_norm = 500.0
C = 96
W = 256
HALF_ROWS = 2048
LANES = 128
MESH = pl.DeviceIdType.MESH
f32, bf16 = jnp.float32, jnp.bfloat16


def dot_nt(a, b):
    return lax.dot_general(a, b, (((1,), (1,)), ((), ())), preferred_element_type=f32)


def dot_nn(a, b):
    return lax.dot_general(a, b, (((1,), (0,)), ((), ())), preferred_element_type=f32)


def eye_mask():
    rows = lax.broadcasted_iota(jnp.int32, (C, C), 0)
    return rows == lax.broadcasted_iota(jnp.int32, (C, C), 1)


def to_column(row):
    spread = jnp.broadcast_to(row, (C, C))
    return jnp.sum(jnp.where(eye_mask(), spread, 0.0), axis=1, keepdims=True)


def to_row(column):
    spread = jnp.broadcast_to(column, (C, C))
    return jnp.sum(jnp.where(eye_mask(), spread, 0.0), axis=0, keepdims=True)


def shift_columns(values, offset):
    if offset == 0:
        return values
    column = lax.broadcasted_iota(jnp.int32, values.shape, 1)
    rolled = pltpu.roll(values, (-offset) % W, 1)
    edge = W - 1 if offset > 0 else 0
    return jnp.where(column == edge, 0.0, rolled)


def normalised(values):
    meansq = jnp.mean(values * values, axis=0, keepdims=True)
    inverse = lax.rsqrt(meansq + epsilon)
    return values * inverse, inverse


def act_parts(values, gain):
    unit, inverse = normalised(values)
    scaled = unit * gain
    gate = 1.0 / (1.0 + jnp.exp(-scaled))
    slope = gate * (1.0 + scaled * (1.0 - gate))
    return scaled * gate, slope, unit, inverse


def back_through_norm(grad_scaled, gain, unit, inverse):
    grad_unit = grad_scaled * gain
    return inverse * (grad_unit - unit * jnp.mean(grad_unit * unit, axis=0, keepdims=True))


CELLS = [(p, q) for p in range(3) for q in range(3)]
OWN = CELLS.index((2, 1))
ORDER = [7, 6, 8, 4, 1, 3, 5, 0, 2]


FAR_FIRST = (4, 5, 3, 6, 2, 7, 1, 0)


def band_of(cell):
    return pl.ds(cell * C, C)


def put_rows(packed, half, raw):
    for n in range(63):
        start = n * 32
        j, r = start // (3 * C), start % (3 * C)
        block = start // 64
        packed[half, block // 8, block % 8, pl.ds(start % 64, 32), :] = raw[
            r : r + 32, j * LANES : (j + 1) * LANES
        ]


def block_kernel(x_hbm, cot_hbm, gain_first_hbm, gain_second_hbm, bias_hbm, k1_hbm, k2_hbm,
                 g_hbm, vector_ref, grad_in_ref,
                 g_ref, x_ref, cot_ref, gain_first_ref, gain_second_ref, bias_ref, k1, k2, k1t, k2t, x_cells, c_cells, h_cells, f_cells, d_cells,
                 second3, hidden3, packed,
                 core_in, part, x_out, x_in, y_out, y_in, z_in, vz, vy, vx, vc,
                 local_sem, hx_sem, hc_sem, hh_sem,
                 core_sem, x_sem, y_sem, z_sem, gy_sem, gx_sem, gc_sem,
                 vz_sem, vy_sem, vx_sem, vc_sem, out_sem):
    tm, row = lax.axis_index("tm"), lax.axis_index("row")
    me_x, me_c = tm // 2, tm % 2
    me_z, me_y = row // 8, row % 8
    peer_c = {"tm": me_x * 2 + 1 - me_c, "row": row}

    def at_x(d):
        return lax.rem(me_x + d, 4)

    def at_y(d):
        return lax.rem(me_y + d, 8)

    def at_z(d):
        return lax.rem(me_z + d, 8)

    def peer_x(d):
        return {"tm": at_x(d) * 2 + me_c, "row": row}

    def peer_y(d):
        return {"tm": tm, "row": me_z * 8 + at_y(d)}

    def peer_z(d):
        return {"tm": tm, "row": at_z(d) * 8 + me_y}

    def later(cell):
        p, q = CELLS[cell]
        return {"tm": lax.rem(tm + 2 - p, 8), "row": lax.rem(row + 65 - q, 64)}

    def earlier(cell):
        p, q = CELLS[cell]
        return {"tm": lax.rem(tm + 6 + p, 8), "row": lax.rem(row + 63 + q, 64)}

    def send(src, dst, sems, slot, device):
        copy = pltpu.make_async_remote_copy(
            src_ref=src, dst_ref=dst, send_sem=sems.at[0, slot], recv_sem=sems.at[1, slot],
            device_id=device, device_id_type=MESH,
        )
        copy.start()
        return copy

    pairs = [(x_hbm, x_ref), (cot_hbm, cot_ref), (gain_first_hbm, gain_first_ref),
             (gain_second_hbm, gain_second_ref), (bias_hbm, bias_ref), (k1_hbm, k1), (k2_hbm, k2)]
    loads = [pltpu.make_async_copy(a, b, local_sem.at[k]) for k, (a, b) in enumerate(pairs)]
    for load in loads:
        load.start()

    barrier = pltpu.get_barrier_semaphore()
    halo = [cell for cell in ORDER if cell != OWN]
    peers = [later(cell) for cell in halo] + [earlier(cell) for cell in halo]
    peers += [peer_c] + [peer_x(d) for d in range(1, 4)]
    peers += [peer_y(d) for d in range(1, 8)] + [peer_z(d) for d in range(1, 8)]
    for peer in peers:
        pl.semaphore_signal(barrier, inc=1, device_id=peer, device_id_type=MESH)
    for load in loads[:2]:
        load.wait()
    pl.semaphore_wait(barrier, len(peers))

    sent = []
    x_copies, c_copies = {}, {}
    for cell in halo:
        x_copies[cell] = send(x_ref, x_cells.at[cell], hx_sem, cell, later(cell))
        c_copies[cell] = send(cot_ref, c_cells.at[band_of(cell)], hc_sem, cell, earlier(cell))
    sent += list(x_copies.values()) + list(c_copies.values())

    for load in loads[2:]:
        load.wait()
    gain_first = to_column(gain_first_ref[...])
    gain_second = to_column(gain_second_ref[...])
    bias = to_column(bias_ref[...])
    identity = jnp.where(eye_mask(), 1.0, 0.0).astype(bf16)
    for cell in range(9):
        for s in range(3):
            band = pl.ds(s * C, C)
            k2t[cell, band, :] = dot_nt(identity, k2[cell, band, :]).astype(bf16)
            k1t[cell, band, :] = dot_nt(identity, k1[cell, band, :]).astype(bf16)

    pad = jnp.zeros((32, W), bf16)
    f_cells[pl.ds(9 * C, 32), :] = pad
    c_cells[pl.ds(9 * C, 32), :] = pad
    c_own = cot_ref[...]
    c_cells[band_of(OWN), :] = c_own

    def before(cell):
        p, q = CELLS[cell]
        return (tm + p >= 2) & (row + q >= 1) & (row + q <= 64)

    def after(cell):
        p, q = CELLS[cell]
        return (tm + 2 - p <= 7) & (row + 1 - q >= 0) & (row + 1 - q <= 63)

    sums = jnp.zeros((3 * C, W), f32)
    for cell in ORDER:
        if cell == OWN:
            wide = x_ref[...].astype(f32)
        else:
            x_copies[cell].wait_recv()

            @pl.when(jnp.logical_not(before(cell)))
            def _():
                x_cells[cell] = jnp.zeros((C, W), bf16)

            wide = x_cells[cell].astype(f32)
        value, slope, unit, inverse = act_parts(wide, gain_first)
        if cell == OWN:
            own_slope, own_unit, own_inverse = slope, unit, inverse
        band = band_of(cell)
        rounded = value.astype(bf16)
        f_cells[band, :] = rounded
        d_cells[band, :] = (slope * unit).astype(bf16)
        sums = sums + dot_nn(k1[cell], rounded)
    hidden = shift_columns(sums[:C], -1) + sums[C : 2 * C] + shift_columns(sums[2 * C :], 1)
    hidden = hidden + bias
    second, slope, unit, inverse = act_parts(hidden, gain_second)
    second = second.astype(bf16).astype(f32)
    for s in range(3):
        second3[pl.ds(s * C, C), :] = shift_columns(second, s - 1).astype(bf16)

    sums = jnp.zeros((3 * C, W), f32)
    for cell in ORDER:
        if cell != OWN:
            c_copies[cell].wait_recv()

            @pl.when(jnp.logical_not(after(cell)))
            def _():
                c_cells[band_of(cell), :] = jnp.zeros((C, W), bf16)

        sums = sums + dot_nn(k2t[cell], c_cells[band_of(cell), :])
    grad_second = shift_columns(sums[:C], 1) + sums[C : 2 * C] + shift_columns(sums[2 * C :], -1)
    grad_scaled = grad_second * slope
    raw_gain_second = jnp.sum(grad_scaled * unit, axis=1, keepdims=True)
    grad_hidden = back_through_norm(grad_scaled, gain_second, unit, inverse)
    raw_bias = jnp.sum(grad_hidden, axis=1, keepdims=True)
    rounded = grad_hidden.astype(bf16)
    raw_cot = jnp.sum(c_own.astype(f32), axis=1, keepdims=True)
    hidden_cot = rounded.astype(f32)
    for s in range(3):
        hidden3[pl.ds(s * C, C), :] = shift_columns(hidden_cot, 1 - s).astype(bf16)
    h_own = pl.ds(C, C)

    put_rows(packed, 1, dot_nt(second3[...], c_cells[...]))
    put_rows(packed, 0, dot_nt(hidden3[...], f_cells[...]))
    gained = jnp.zeros((3 * C, C), f32)
    for cell in range(9):
        gained = gained + k1[cell].astype(f32) * dot_nt(hidden3[...], d_cells[band_of(cell), :])
    packed[0, 3, 7, pl.ds(32, 32), :] = jnp.zeros((32, LANES), f32)
    packed[1, 3, 7, pl.ds(32, 32), :] = jnp.zeros((32, LANES), f32)

    core_copies = []
    for k, d in enumerate(FAR_FIRST):
        core_copies.append(send(packed.at[1 - me_c, :, at_y(d)], core_in.at[k], core_sem, k, peer_c))
    x_copies = []
    for k, d in enumerate(FAR_FIRST):
        core_copies[k].wait_recv()
        total = packed[me_c, :, at_y(d)] + core_in[k]
        x_out[k] = total.astype(bf16)
        part[k] = packed[me_c, me_x, at_y(d)] + core_in[k, me_x]
        for e in (2, 1, 3):
            x_copies.append(
                send(x_out.at[k, at_x(e)], x_in.at[k, e - 1], x_sem, k * 3 + e - 1, peer_x(e))
            )
    sent += core_copies + x_copies

    vz[me_z] = jnp.zeros((8, LANES), f32)
    lanes = pl.ds(0, C)
    vz[me_z, pl.ds(0, 1), lanes] = to_row(raw_bias)
    vz[me_z, pl.ds(1, 1), lanes] = jnp.sum(gained, axis=0, keepdims=True)
    vz[me_z, pl.ds(2, 1), lanes] = to_row(raw_gain_second)
    vz[me_z, pl.ds(3, 1), lanes] = to_row(raw_cot)
    v_copies = [send(vz.at[me_z], vz.at[me_z], vz_sem, d - 1, peer_z(d)) for d in range(1, 8)]

    def vector_total(slots, count):
        for copy in v_copies:
            copy.wait_recv()
        sent.extend(v_copies)
        whole = slots[0]
        for e in range(1, count):
            whole = whole + slots[e]
        return whole

    vy[me_y] = vector_total(vz, 8)
    v_copies = [send(vy.at[me_y], vy.at[me_y], vy_sem, d - 1, peer_y(d)) for d in range(1, 8)]

    y_copies = []
    for k, d in enumerate(FAR_FIRST):
        total = part[k]
        for copy in x_copies[3 * k : 3 * k + 3]:
            copy.wait_recv()
        for e in range(3):
            total = total + x_in[k, e].astype(f32)
        if d > 0:
            y_out[k] = total.astype(bf16)
            y_copies.append(send(y_out.at[k], y_in.at[d - 1], y_sem, d - 1, peer_y(d)))
    h_copies = {}
    for cell in halo:
        h_copies[cell] = send(hidden3.at[h_own], h_cells.at[cell], hh_sem, cell, earlier(cell))
    sent += list(h_copies.values())
    for copy in y_copies:
        copy.wait_recv()
    for e in range(7):
        total = total + y_in[e].astype(f32)

    z_in[me_z] = total.astype(bf16)
    z_copies = []
    for d in (4, 3, 5, 2, 6, 1, 7):
        z_copies.append(send(z_in.at[me_z], z_in.at[me_z], z_sem, d - 1, peer_z(d)))
    vx[me_x] = vector_total(vy, 8)
    v_copies = [send(vx.at[me_x], vx.at[me_x], vx_sem, d - 1, peer_x(d)) for d in range(1, 4)]
    for copy in z_copies:
        copy.wait_recv()
    total = z_in[0].astype(f32)
    for e in range(1, 8):
        total = total + z_in[e].astype(f32)
    g_ref[me_c, me_x, me_y] = total.astype(bf16)
    sent += y_copies + z_copies

    own = g_ref.at[me_c, me_x, me_y]
    gy_copies, gx_copies, gc_copies = {}, {}, []
    for d in (4, 3, 5, 2, 6, 1, 7):
        gy_copies[d] = send(own, own, gy_sem, d - 1, peer_y(d))

    def pass_on(k, d):
        piece = g_ref.at[me_c, me_x, at_y(8 - d)]
        for e in (2, 1, 3):
            gx_copies[k, e] = send(piece, piece, gx_sem, k * 3 + e - 1, peer_x(e))
        gc_copies.append(send(piece, piece, gc_sem, k * 4, peer_c))

    pass_on(0, 0)

    sums = dot_nn(k1t[OWN], hidden3[h_own, :])
    for cell in ORDER[1:]:
        h_copies[cell].wait_recv()

        @pl.when(jnp.logical_not(after(cell)))
        def _():
            h_cells[cell] = jnp.zeros((C, W), bf16)

        sums = sums + dot_nn(k1t[cell], h_cells[cell])
    grad_first = shift_columns(sums[:C], 1) + sums[C : 2 * C] + shift_columns(sums[2 * C :], -1)
    input_term = back_through_norm(grad_first * own_slope, gain_first, own_unit, own_inverse)
    grad_in_ref[...] = (c_own.astype(f32) + input_term).astype(bf16)

    for k, d in enumerate((1, 7, 2, 6, 3, 5, 4)):
        gy_copies[d].wait_recv()
        pass_on(k + 1, d)
    for k, d in enumerate((0, 1, 7, 2, 6, 3, 5, 4)):
        for e in (1, 3, 2):
            gx_copies[k, e].wait_recv()
            piece = g_ref.at[me_c, at_x(4 - e), at_y(8 - d)]
            gc_copies.append(send(piece, piece, gc_sem, k * 4 + e, peer_c))
        if k == 0:
            vc[me_c] = vector_total(vx, 4)
            v_copies = [send(vc.at[me_c], vc.at[me_c], vc_sem, 0, peer_c)]
    outs = []

    def store(c, x):
        copy = pltpu.make_async_copy(g_ref.at[c, x], g_hbm.at[c, x], out_sem.at[len(outs)])
        copy.start()
        outs.append(copy)

    for x in range(4):
        store(me_c, x)
    sent += list(gy_copies.values()) + list(gx_copies.values()) + gc_copies
    vector_ref[...] = vector_total(vc, 2)
    for copy in gc_copies:
        copy.wait_recv()
    for x in range(4):
        store(1 - me_c, x)
    for copy in sent:
        copy.wait_send()
    for copy in outs:
        copy.wait()


def scale_kernel(g_hbm, vector_hbm, grad_in_hbm, first_hbm, second_hbm, vectors_ref, copy_hbm,
                 g_ref, vector_ref, first_ref, second_ref, load_sem, first_sem, second_sem):
    through = pltpu.make_async_copy(grad_in_hbm, copy_hbm, load_sem.at[0])
    vector_load = pltpu.make_async_copy(vector_hbm, vector_ref, load_sem.at[1])
    loads = []
    for k in range(8):
        rows = pl.ds(k * 512, 512)
        loads.append(pltpu.make_async_copy(g_hbm.at[rows], g_ref.at[rows], load_sem.at[2 + k]))
    for load in loads + [vector_load, through]:
        load.start()
    squares = jnp.zeros((64, LANES), f32)
    for k in range(8):
        loads[k].wait()
        for n in range(8):
            part = g_ref[pl.ds(k * 512 + n * 64, 64), :].astype(f32)
            squares = squares + part * part
    vector_load.wait()
    vectors = vector_ref[...]
    squares = jnp.sum(squares, axis=0, keepdims=True)
    squares = squares + jnp.sum(vectors * vectors, axis=0, keepdims=True)
    total = jnp.sqrt(jnp.sum(squares, axis=1, keepdims=True))
    factor = jnp.minimum(1.0, max_norm / (total + epsilon))
    vectors_ref[...] = vectors[:4, :C] * factor
    target = lax.broadcasted_iota(jnp.int32, (C, LANES), 0)
    lane = lax.broadcasted_iota(jnp.int32, (C, LANES), 1)
    stores = []
    for cell in range(9):
        tiles = range(cell * C // LANES, (cell * C + C - 1) // LANES + 1)
        first = jnp.zeros((3 * C, C), f32)
        second = [jnp.zeros((C, C), f32) for _ in range(3)]
        for j in tiles:
            pick = jnp.where(lane + (j * LANES - cell * C) == target, 1.0, 0.0).astype(bf16)
            first = first + dot_nt(g_ref[pl.ds(j * 3 * C, 3 * C), :], pick)
            for s in range(3):
                start = HALF_ROWS + j * 3 * C + s * C
                second[s] = second[s] + dot_nt(pick, g_ref[pl.ds(start, C), :])
        first_ref[cell] = first * factor
        for s in range(3):
            second_ref[cell, pl.ds(s * C, C), :] = second[s] * factor
        stores.append(
            pltpu.make_async_copy(first_ref.at[cell], first_hbm.at[cell], first_sem.at[cell])
        )
        stores[-1].start()
        stores.append(
            pltpu.make_async_copy(second_ref.at[cell], second_hbm.at[cell], second_sem.at[cell])
        )
        stores[-1].start()
    through.wait()
    for copy in stores:
        copy.wait()


def body(inputs, cotangent, gain_first, gain_second, bias_first, kernel_first, kernel_second):
    dma, vmem = pltpu.SemaphoreType.DMA, pltpu.VMEM
    in_vmem = pl.BlockSpec(memory_space=pltpu.VMEM)
    in_any = pl.BlockSpec(memory_space=pl.ANY)
    summed, summed_vectors, grad_inputs = pl.pallas_call(
        block_kernel,
        out_shape=(
            jax.ShapeDtypeStruct((2, 4, 8, 64, LANES), bf16),
            jax.ShapeDtypeStruct((8, LANES), f32),
            jax.ShapeDtypeStruct((C, W), bf16),
        ),
        in_specs=[in_any] * 7,
        out_specs=(in_any, in_vmem, in_vmem),
        scratch_shapes=[
            vmem((2, 4, 8, 64, LANES), bf16),
            vmem((C, W), bf16), vmem((C, W), bf16),
            vmem((1, C), f32), vmem((1, C), f32), vmem((1, C), f32),
            vmem((9, 3 * C, C), bf16), vmem((9, 3 * C, C), bf16),
            vmem((9, 3 * C, C), bf16), vmem((9, 3 * C, C), bf16),
            vmem((9, C, W), bf16), vmem((9 * C + 32, W), bf16), vmem((9, C, W), bf16),
            vmem((9 * C + 32, W), bf16), vmem((9 * C, W), bf16),
            vmem((3 * C, W), bf16), vmem((3 * C, W), bf16),
            vmem((2, 4, 8, 64, LANES), f32),
            vmem((8, 4, 64, LANES), f32),
            vmem((8, 64, LANES), f32),
            vmem((8, 4, 64, LANES), bf16),
            vmem((8, 3, 64, LANES), bf16),
            vmem((7, 64, LANES), bf16),
            vmem((7, 64, LANES), bf16),
            vmem((8, 64, LANES), bf16),
            vmem((8, 8, LANES), f32), vmem((8, 8, LANES), f32),
            vmem((4, 8, LANES), f32), vmem((2, 8, LANES), f32),
            dma((7,)), dma((2, 9)), dma((2, 9)), dma((2, 9)),
            dma((2, 8)), dma((2, 24)), dma((2, 7)), dma((2, 7)),
            dma((2, 7)), dma((2, 24)), dma((2, 32)),
            dma((2, 7)), dma((2, 7)), dma((2, 3)), dma((2, 1)), dma((8,)),
        ],
        compiler_params=pltpu.CompilerParams(
            collective_id=0, has_side_effects=True, vmem_limit_bytes=60 * 1024 * 1024
        ),
    )(
        inputs.reshape(C, W), cotangent.reshape(C, W),
        gain_first.reshape(1, C), gain_second.reshape(1, C), bias_first.reshape(1, C),
        kernel_first.reshape(9, 3 * C, C), kernel_second.reshape(9, 3 * C, C),
    )
    grad_first, grad_second, vectors, grad_inputs = pl.pallas_call(
        scale_kernel,
        out_shape=(
            jax.ShapeDtypeStruct((9, 3 * C, C), f32),
            jax.ShapeDtypeStruct((9, 3 * C, C), f32),
            jax.ShapeDtypeStruct((4, C), f32),
            jax.ShapeDtypeStruct((C, W), bf16),
        ),
        in_specs=[in_any] * 3,
        out_specs=(in_any, in_any, in_vmem, in_any),
        scratch_shapes=[
            vmem((2 * HALF_ROWS, LANES), bf16), vmem((8, LANES), f32),
            vmem((9, 3 * C, C), f32), vmem((9, 3 * C, C), f32),
            dma((10,)), dma((9,)), dma((9,)),
        ],
        compiler_params=pltpu.CompilerParams(vmem_limit_bytes=60 * 1024 * 1024),
    )(summed.reshape(2 * HALF_ROWS, LANES), summed_vectors, grad_inputs)
    return (
        grad_inputs.reshape(inputs.shape),
        grad_first.reshape(kernel_first.shape),
        grad_second.reshape(kernel_second.shape),
        vectors,
    )


def solution(mesh):
    in_specs = (P(None, "tm", "row", None), P(None, "tm", "row", None), P(), P(), P(), P(), P())
    out_specs = (P(None, "tm", "row", None), P(), P(), P())
    return jax.shard_map(body, mesh=mesh, in_specs=in_specs, out_specs=out_specs, check_vma=False)
```

```python
import jax
import jax.numpy as jnp
from jax import lax
from jax.experimental import pallas as pl
from jax.experimental.pallas import tpu as pltpu
from jax.sharding import PartitionSpec as P

epsilon = 1e-06
max_norm = 500.0
C = 96
W = 256
HALF_ROWS = 2048
LANES = 128
MESH = pl.DeviceIdType.MESH
f32, bf16 = jnp.float32, jnp.bfloat16


def dot_nt(a, b):
    return lax.dot_general(a, b, (((1,), (1,)), ((), ())), preferred_element_type=f32)


def dot_nn(a, b):
    return lax.dot_general(a, b, (((1,), (0,)), ((), ())), preferred_element_type=f32)


def eye_mask():
    rows = lax.broadcasted_iota(jnp.int32, (C, C), 0)
    return rows == lax.broadcasted_iota(jnp.int32, (C, C), 1)


def to_column(row):
    spread = jnp.broadcast_to(row, (C, C))
    return jnp.sum(jnp.where(eye_mask(), spread, 0.0), axis=1, keepdims=True)


def to_row(column):
    spread = jnp.broadcast_to(column, (C, C))
    return jnp.sum(jnp.where(eye_mask(), spread, 0.0), axis=0, keepdims=True)


def shift_columns(values, offset):
    if offset == 0:
        return values
    column = lax.broadcasted_iota(jnp.int32, values.shape, 1)
    rolled = pltpu.roll(values, (-offset) % W, 1)
    edge = W - 1 if offset > 0 else 0
    return jnp.where(column == edge, 0.0, rolled)


def normalised(values):
    meansq = jnp.mean(values * values, axis=0, keepdims=True)
    inverse = lax.rsqrt(meansq + epsilon)
    return values * inverse, inverse


def act_parts(values, gain):
    unit, inverse = normalised(values)
    scaled = unit * gain
    gate = 1.0 / (1.0 + jnp.exp(-scaled))
    slope = gate * (1.0 + scaled * (1.0 - gate))
    return scaled * gate, slope, unit, inverse


def back_through_norm(grad_scaled, gain, unit, inverse):
    grad_unit = grad_scaled * gain
    return inverse * (grad_unit - unit * jnp.mean(grad_unit * unit, axis=0, keepdims=True))


CELLS = [(p, q) for p in range(3) for q in range(3)]
OWN = CELLS.index((2, 1))
ORDER = [7, 6, 8, 4, 1, 3, 5, 0, 2]


FAR_FIRST = (4, 5, 3, 6, 2, 7, 1, 0)


def band_of(cell):
    return pl.ds(cell * C, C)


def put_rows(packed, half, raw):
    for n in range(63):
        start = n * 32
        j, r = start // (3 * C), start % (3 * C)
        block = start // 64
        packed[half, block // 8, block % 8, pl.ds(start % 64, 32), :] = raw[
            r : r + 32, j * LANES : (j + 1) * LANES
        ]


def block_kernel(x_hbm, cot_hbm, gain_first_hbm, gain_second_hbm, bias_hbm, k1_hbm, k2_hbm,
                 g_hbm, vector_ref, grad_in_ref,
                 g_ref, x_ref, cot_ref, gain_first_ref, gain_second_ref, bias_ref, k1, k2, k1t, k2t, x_cells, h_cells, d_cells,
                 left, cells, packed,
                 core_in, part, x_out, x_in, y_out, y_in, z_in, vz, vy, vx, vc,
                 local_sem, hx_sem, hc_sem, hh_sem,
                 core_sem, x_sem, y_sem, z_sem, gy_sem, gx_sem, gc_sem,
                 vz_sem, vy_sem, vx_sem, vc_sem, out_sem):
    tm, row = lax.axis_index("tm"), lax.axis_index("row")
    me_x, me_c = tm // 2, tm % 2
    me_z, me_y = row // 8, row % 8
    peer_c = {"tm": me_x * 2 + 1 - me_c, "row": row}

    def at_x(d):
        return lax.rem(me_x + d, 4)

    def at_y(d):
        return lax.rem(me_y + d, 8)

    def at_z(d):
        return lax.rem(me_z + d, 8)

    def peer_x(d):
        return {"tm": at_x(d) * 2 + me_c, "row": row}

    def peer_y(d):
        return {"tm": tm, "row": me_z * 8 + at_y(d)}

    def peer_z(d):
        return {"tm": tm, "row": at_z(d) * 8 + me_y}

    def later(cell):
        p, q = CELLS[cell]
        return {"tm": lax.rem(tm + 2 - p, 8), "row": lax.rem(row + 65 - q, 64)}

    def earlier(cell):
        p, q = CELLS[cell]
        return {"tm": lax.rem(tm + 6 + p, 8), "row": lax.rem(row + 63 + q, 64)}

    def send(src, dst, sems, slot, device):
        copy = pltpu.make_async_remote_copy(
            src_ref=src, dst_ref=dst, send_sem=sems.at[0, slot], recv_sem=sems.at[1, slot],
            device_id=device, device_id_type=MESH,
        )
        copy.start()
        return copy

    pairs = [(x_hbm, x_ref), (cot_hbm, cot_ref), (gain_first_hbm, gain_first_ref),
             (gain_second_hbm, gain_second_ref), (bias_hbm, bias_ref), (k1_hbm, k1), (k2_hbm, k2)]
    loads = [pltpu.make_async_copy(a, b, local_sem.at[k]) for k, (a, b) in enumerate(pairs)]
    for load in loads:
        load.start()

    barrier = pltpu.get_barrier_semaphore()
    halo = [cell for cell in ORDER if cell != OWN]
    peers = [later(cell) for cell in halo] + [earlier(cell) for cell in halo]
    peers += [peer_c] + [peer_x(d) for d in range(1, 4)]
    peers += [peer_y(d) for d in range(1, 8)] + [peer_z(d) for d in range(1, 8)]
    for peer in peers:
        pl.semaphore_signal(barrier, inc=1, device_id=peer, device_id_type=MESH)
    for load in loads[:2]:
        load.wait()
    pl.semaphore_wait(barrier, len(peers))

    sent = []
    x_copies, c_copies = {}, {}
    for cell in halo:
        x_copies[cell] = send(x_ref, x_cells.at[cell], hx_sem, cell, later(cell))
        c_copies[cell] = send(cot_ref, cells.at[1, band_of(cell)], hc_sem, cell, earlier(cell))
    sent += list(x_copies.values()) + list(c_copies.values())

    for load in loads[2:]:
        load.wait()
    gain_first = to_column(gain_first_ref[...])
    gain_second = to_column(gain_second_ref[...])
    bias = to_column(bias_ref[...])
    identity = jnp.where(eye_mask(), 1.0, 0.0).astype(bf16)
    for cell in range(9):
        for s in range(3):
            band = pl.ds(s * C, C)
            k2t[cell, band, :] = dot_nt(identity, k2[cell, band, :]).astype(bf16)
            k1t[cell, band, :] = dot_nt(identity, k1[cell, band, :]).astype(bf16)

    pad = jnp.zeros((32, W), bf16)
    cells[0, pl.ds(9 * C, 32), :] = pad
    cells[1, pl.ds(9 * C, 32), :] = pad
    c_own = cot_ref[...]
    cells[1, band_of(OWN), :] = c_own

    def before(cell):
        p, q = CELLS[cell]
        return (tm + p >= 2) & (row + q >= 1) & (row + q <= 64)

    def after(cell):
        p, q = CELLS[cell]
        return (tm + 2 - p <= 7) & (row + 1 - q >= 0) & (row + 1 - q <= 63)

    sums = jnp.zeros((3 * C, W), f32)
    for cell in ORDER:
        if cell == OWN:
            wide = x_ref[...].astype(f32)
        else:
            x_copies[cell].wait_recv()

            @pl.when(jnp.logical_not(before(cell)))
            def _():
                x_cells[cell] = jnp.zeros((C, W), bf16)

            wide = x_cells[cell].astype(f32)
        value, slope, unit, inverse = act_parts(wide, gain_first)
        if cell == OWN:
            own_slope, own_unit, own_inverse = slope, unit, inverse
        band = band_of(cell)
        rounded = value.astype(bf16)
        cells[0, band, :] = rounded
        d_cells[band, :] = (slope * unit).astype(bf16)
        sums = sums + dot_nn(k1[cell], rounded)
    hidden = shift_columns(sums[:C], -1) + sums[C : 2 * C] + shift_columns(sums[2 * C :], 1)
    hidden = hidden + bias
    second, slope, unit, inverse = act_parts(hidden, gain_second)
    second = second.astype(bf16).astype(f32)
    for s in range(3):
        left[1, pl.ds(s * C, C), :] = shift_columns(second, s - 1).astype(bf16)

    sums = jnp.zeros((3 * C, W), f32)
    for cell in ORDER:
        if cell != OWN:
            c_copies[cell].wait_recv()

            @pl.when(jnp.logical_not(after(cell)))
            def _():
                cells[1, band_of(cell), :] = jnp.zeros((C, W), bf16)

        sums = sums + dot_nn(k2t[cell], cells[1, band_of(cell), :])
    grad_second = shift_columns(sums[:C], 1) + sums[C : 2 * C] + shift_columns(sums[2 * C :], -1)
    grad_scaled = grad_second * slope
    raw_gain_second = jnp.sum(grad_scaled * unit, axis=1, keepdims=True)
    grad_hidden = back_through_norm(grad_scaled, gain_second, unit, inverse)
    raw_bias = jnp.sum(grad_hidden, axis=1, keepdims=True)
    rounded = grad_hidden.astype(bf16)
    raw_cot = jnp.sum(c_own.astype(f32), axis=1, keepdims=True)
    hidden_cot = rounded.astype(f32)
    for s in range(3):
        left[0, pl.ds(s * C, C), :] = shift_columns(hidden_cot, 1 - s).astype(bf16)
    h_own = pl.ds(C, C)

    for half in (0, 1):
        packed[half, 3, 7, pl.ds(32, 32), :] = jnp.zeros((32, LANES), f32)
    put_rows(packed, 1 - me_c, dot_nt(left[1 - me_c], cells[1 - me_c]))
    core_copies = []
    for k, d in enumerate(FAR_FIRST):
        core_copies.append(send(packed.at[1 - me_c, :, at_y(d)], core_in.at[k], core_sem, k, peer_c))
    put_rows(packed, me_c, dot_nt(left[me_c], cells[me_c]))
    x_copies = []
    for k, d in enumerate(FAR_FIRST):
        core_copies[k].wait_recv()
        total = packed[me_c, :, at_y(d)] + core_in[k]
        x_out[k] = total.astype(bf16)
        part[k] = packed[me_c, me_x, at_y(d)] + core_in[k, me_x]
        for e in (2, 1, 3):
            x_copies.append(
                send(x_out.at[k, at_x(e)], x_in.at[k, e - 1], x_sem, k * 3 + e - 1, peer_x(e))
            )
    sent += core_copies + x_copies

    gained = jnp.zeros((3 * C, C), f32)
    for cell in range(9):
        gained = gained + k1[cell].astype(f32) * dot_nt(left[0], d_cells[band_of(cell), :])
    vz[me_z] = jnp.zeros((8, LANES), f32)
    lanes = pl.ds(0, C)
    vz[me_z, pl.ds(0, 1), lanes] = to_row(raw_bias)
    vz[me_z, pl.ds(1, 1), lanes] = jnp.sum(gained, axis=0, keepdims=True)
    vz[me_z, pl.ds(2, 1), lanes] = to_row(raw_gain_second)
    vz[me_z, pl.ds(3, 1), lanes] = to_row(raw_cot)
    v_copies = [send(vz.at[me_z], vz.at[me_z], vz_sem, d - 1, peer_z(d)) for d in range(1, 8)]

    def vector_total(slots, count):
        for copy in v_copies:
            copy.wait_recv()
        sent.extend(v_copies)
        whole = slots[0]
        for e in range(1, count):
            whole = whole + slots[e]
        return whole

    vy[me_y] = vector_total(vz, 8)
    v_copies = [send(vy.at[me_y], vy.at[me_y], vy_sem, d - 1, peer_y(d)) for d in range(1, 8)]

    y_copies = []
    for k, d in enumerate(FAR_FIRST):
        total = part[k]
        for copy in x_copies[3 * k : 3 * k + 3]:
            copy.wait_recv()
        for e in range(3):
            total = total + x_in[k, e].astype(f32)
        if d > 0:
            y_out[k] = total.astype(bf16)
            y_copies.append(send(y_out.at[k], y_in.at[d - 1], y_sem, d - 1, peer_y(d)))
    h_copies = {}
    for cell in halo:
        h_copies[cell] = send(left.at[0, h_own], h_cells.at[cell], hh_sem, cell, earlier(cell))
    for copy in y_copies:
        copy.wait_recv()
    for e in range(7):
        total = total + y_in[e].astype(f32)

    z_in[me_z] = total.astype(bf16)
    z_copies = []
    for d in (4, 3, 5, 2, 6, 1, 7):
        z_copies.append(send(z_in.at[me_z], z_in.at[me_z], z_sem, d - 1, peer_z(d)))
    for copy in sent:
        copy.wait_send()
    sent = []
    vx[me_x] = vector_total(vy, 8)
    v_copies = [send(vx.at[me_x], vx.at[me_x], vx_sem, d - 1, peer_x(d)) for d in range(1, 4)]
    for copy in z_copies:
        copy.wait_recv()
    total = z_in[0].astype(f32)
    for e in range(1, 8):
        total = total + z_in[e].astype(f32)
    g_ref[me_c, me_x, me_y] = total.astype(bf16)
    sent += y_copies + z_copies

    own = g_ref.at[me_c, me_x, me_y]
    gy_copies, gx_copies, gc_copies = {}, {}, []
    for d in (4, 3, 5, 2, 6, 1, 7):
        gy_copies[d] = send(own, own, gy_sem, d - 1, peer_y(d))

    def pass_on(k, d):
        piece = g_ref.at[me_c, me_x, at_y(8 - d)]
        for e in (2, 1, 3):
            gx_copies[k, e] = send(piece, piece, gx_sem, k * 3 + e - 1, peer_x(e))
        gc_copies.append(send(piece, piece, gc_sem, k * 4, peer_c))

    pass_on(0, 0)

    for copy in sent:
        copy.wait_send()
    sent = list(h_copies.values())
    sums = dot_nn(k1t[OWN], left[0, h_own, :])
    for cell in ORDER[1:]:
        h_copies[cell].wait_recv()

        @pl.when(jnp.logical_not(after(cell)))
        def _():
            h_cells[cell] = jnp.zeros((C, W), bf16)

        sums = sums + dot_nn(k1t[cell], h_cells[cell])
    grad_first = shift_columns(sums[:C], 1) + sums[C : 2 * C] + shift_columns(sums[2 * C :], -1)
    input_term = back_through_norm(grad_first * own_slope, gain_first, own_unit, own_inverse)
    grad_in_ref[...] = (c_own.astype(f32) + input_term).astype(bf16)

    for k, d in enumerate((1, 7, 2, 6, 3, 5, 4)):
        gy_copies[d].wait_recv()
        pass_on(k + 1, d)
    for k, d in enumerate((0, 1, 7, 2, 6, 3, 5, 4)):
        for e in (1, 3, 2):
            gx_copies[k, e].wait_recv()
            piece = g_ref.at[me_c, at_x(4 - e), at_y(8 - d)]
            gc_copies.append(send(piece, piece, gc_sem, k * 4 + e, peer_c))
        if k == 0:
            vc[me_c] = vector_total(vx, 4)
            v_copies = [send(vc.at[me_c], vc.at[me_c], vc_sem, 0, peer_c)]
    outs = []

    def store(c, x):
        copy = pltpu.make_async_copy(g_ref.at[c, x], g_hbm.at[c, x], out_sem.at[len(outs)])
        copy.start()
        outs.append(copy)

    for x in range(4):
        store(me_c, x)
    for copy in sent:
        copy.wait_send()
    sent = list(gy_copies.values()) + list(gx_copies.values()) + gc_copies
    vector_ref[...] = vector_total(vc, 2)
    for copy in gc_copies:
        copy.wait_recv()
    for x in range(4):
        store(1 - me_c, x)
    for copy in sent:
        copy.wait_send()
    for copy in outs:
        copy.wait()


def scale_kernel(g_hbm, vector_hbm, grad_in_hbm, first_hbm, second_hbm, vectors_ref, copy_hbm,
                 g_ref, vector_ref, first_ref, second_ref, load_sem, first_sem, second_sem):
    through = pltpu.make_async_copy(grad_in_hbm, copy_hbm, load_sem.at[0])
    vector_load = pltpu.make_async_copy(vector_hbm, vector_ref, load_sem.at[1])
    loads = []
    for k in range(8):
        rows = pl.ds(k * 512, 512)
        loads.append(pltpu.make_async_copy(g_hbm.at[rows], g_ref.at[rows], load_sem.at[2 + k]))
    for load in loads + [vector_load, through]:
        load.start()
    squares = jnp.zeros((64, LANES), f32)
    for k in range(8):
        loads[k].wait()
        for n in range(8):
            part = g_ref[pl.ds(k * 512 + n * 64, 64), :].astype(f32)
            squares = squares + part * part
    vector_load.wait()
    vectors = vector_ref[...]
    squares = jnp.sum(squares, axis=0, keepdims=True)
    squares = squares + jnp.sum(vectors * vectors, axis=0, keepdims=True)
    total = jnp.sqrt(jnp.sum(squares, axis=1, keepdims=True))
    factor = jnp.minimum(1.0, max_norm / (total + epsilon))
    vectors_ref[...] = vectors[:4, :C] * factor
    target = lax.broadcasted_iota(jnp.int32, (C, LANES), 0)
    lane = lax.broadcasted_iota(jnp.int32, (C, LANES), 1)
    stores = []
    for cell in range(9):
        tiles = range(cell * C // LANES, (cell * C + C - 1) // LANES + 1)
        first = jnp.zeros((3 * C, C), f32)
        second = [jnp.zeros((C, C), f32) for _ in range(3)]
        for j in tiles:
            pick = jnp.where(lane + (j * LANES - cell * C) == target, 1.0, 0.0).astype(bf16)
            first = first + dot_nt(g_ref[pl.ds(j * 3 * C, 3 * C), :], pick)
            for s in range(3):
                start = HALF_ROWS + j * 3 * C + s * C
                second[s] = second[s] + dot_nt(pick, g_ref[pl.ds(start, C), :])
        first_ref[cell] = first * factor
        for s in range(3):
            second_ref[cell, pl.ds(s * C, C), :] = second[s] * factor
        stores.append(
            pltpu.make_async_copy(first_ref.at[cell], first_hbm.at[cell], first_sem.at[cell])
        )
        stores[-1].start()
        stores.append(
            pltpu.make_async_copy(second_ref.at[cell], second_hbm.at[cell], second_sem.at[cell])
        )
        stores[-1].start()
    through.wait()
    for copy in stores:
        copy.wait()


def body(inputs, cotangent, gain_first, gain_second, bias_first, kernel_first, kernel_second):
    dma, vmem = pltpu.SemaphoreType.DMA, pltpu.VMEM
    in_vmem = pl.BlockSpec(memory_space=pltpu.VMEM)
    in_any = pl.BlockSpec(memory_space=pl.ANY)
    summed, summed_vectors, grad_inputs = pl.pallas_call(
        block_kernel,
        out_shape=(
            jax.ShapeDtypeStruct((2, 4, 8, 64, LANES), bf16),
            jax.ShapeDtypeStruct((8, LANES), f32),
            jax.ShapeDtypeStruct((C, W), bf16),
        ),
        in_specs=[in_any] * 7,
        out_specs=(in_any, in_vmem, in_vmem),
        scratch_shapes=[
            vmem((2, 4, 8, 64, LANES), bf16),
            vmem((C, W), bf16), vmem((C, W), bf16),
            vmem((1, C), f32), vmem((1, C), f32), vmem((1, C), f32),
            vmem((9, 3 * C, C), bf16), vmem((9, 3 * C, C), bf16),
            vmem((9, 3 * C, C), bf16), vmem((9, 3 * C, C), bf16),
            vmem((9, C, W), bf16), vmem((9, C, W), bf16), vmem((9 * C, W), bf16),
            vmem((2, 3 * C, W), bf16), vmem((2, 9 * C + 32, W), bf16),
            vmem((2, 4, 8, 64, LANES), f32),
            vmem((8, 4, 64, LANES), f32),
            vmem((8, 64, LANES), f32),
            vmem((8, 4, 64, LANES), bf16),
            vmem((8, 3, 64, LANES), bf16),
            vmem((7, 64, LANES), bf16),
            vmem((7, 64, LANES), bf16),
            vmem((8, 64, LANES), bf16),
            vmem((8, 8, LANES), f32), vmem((8, 8, LANES), f32),
            vmem((4, 8, LANES), f32), vmem((2, 8, LANES), f32),
            dma((7,)), dma((2, 9)), dma((2, 9)), dma((2, 9)),
            dma((2, 8)), dma((2, 24)), dma((2, 7)), dma((2, 7)),
            dma((2, 7)), dma((2, 24)), dma((2, 32)),
            dma((2, 7)), dma((2, 7)), dma((2, 3)), dma((2, 1)), dma((8,)),
        ],
        compiler_params=pltpu.CompilerParams(
            collective_id=0, has_side_effects=True, vmem_limit_bytes=60 * 1024 * 1024
        ),
    )(
        inputs.reshape(C, W), cotangent.reshape(C, W),
        gain_first.reshape(1, C), gain_second.reshape(1, C), bias_first.reshape(1, C),
        kernel_first.reshape(9, 3 * C, C), kernel_second.reshape(9, 3 * C, C),
    )
    grad_first, grad_second, vectors, grad_inputs = pl.pallas_call(
        scale_kernel,
        out_shape=(
            jax.ShapeDtypeStruct((9, 3 * C, C), f32),
            jax.ShapeDtypeStruct((9, 3 * C, C), f32),
            jax.ShapeDtypeStruct((4, C), f32),
            jax.ShapeDtypeStruct((C, W), bf16),
        ),
        in_specs=[in_any] * 3,
        out_specs=(in_any, in_any, in_vmem, in_any),
        scratch_shapes=[
            vmem((2 * HALF_ROWS, LANES), bf16), vmem((8, LANES), f32),
            vmem((9, 3 * C, C), f32), vmem((9, 3 * C, C), f32),
            dma((10,)), dma((9,)), dma((9,)),
        ],
        compiler_params=pltpu.CompilerParams(vmem_limit_bytes=60 * 1024 * 1024),
    )(summed.reshape(2 * HALF_ROWS, LANES), summed_vectors, grad_inputs)
    return (
        grad_inputs.reshape(inputs.shape),
        grad_first.reshape(kernel_first.shape),
        grad_second.reshape(kernel_second.shape),
        vectors,
    )


def solution(mesh):
    in_specs = (P(None, "tm", "row", None), P(None, "tm", "row", None), P(), P(), P(), P(), P())
    out_specs = (P(None, "tm", "row", None), P(), P(), P())
    return jax.shard_map(body, mesh=mesh, in_specs=in_specs, out_specs=out_specs, check_vma=False)
```

```python
import jax
import jax.numpy as jnp
from jax import lax
from jax.experimental import pallas as pl
from jax.experimental.pallas import tpu as pltpu
from jax.sharding import PartitionSpec as P

epsilon = 1e-06
max_norm = 500.0
C = 96
W = 256
HALF_ROWS = 2048
LANES = 128
MESH = pl.DeviceIdType.MESH
f32, bf16 = jnp.float32, jnp.bfloat16


def dot_nt(a, b):
    return lax.dot_general(a, b, (((1,), (1,)), ((), ())), preferred_element_type=f32)


def dot_nn(a, b):
    return lax.dot_general(a, b, (((1,), (0,)), ((), ())), preferred_element_type=f32)


def eye_mask():
    rows = lax.broadcasted_iota(jnp.int32, (C, C), 0)
    return rows == lax.broadcasted_iota(jnp.int32, (C, C), 1)


def to_column(row):
    spread = jnp.broadcast_to(row, (C, C))
    return jnp.sum(jnp.where(eye_mask(), spread, 0.0), axis=1, keepdims=True)


def to_row(column):
    spread = jnp.broadcast_to(column, (C, C))
    return jnp.sum(jnp.where(eye_mask(), spread, 0.0), axis=0, keepdims=True)


def shift_columns(values, offset):
    if offset == 0:
        return values
    column = lax.broadcasted_iota(jnp.int32, values.shape, 1)
    rolled = pltpu.roll(values, (-offset) % W, 1)
    edge = W - 1 if offset > 0 else 0
    return jnp.where(column == edge, 0.0, rolled)


def normalised(values):
    meansq = jnp.mean(values * values, axis=0, keepdims=True)
    inverse = lax.rsqrt(meansq + epsilon)
    return values * inverse, inverse


def act_parts(values, gain):
    unit, inverse = normalised(values)
    scaled = unit * gain
    gate = 1.0 / (1.0 + jnp.exp(-scaled))
    slope = gate * (1.0 + scaled * (1.0 - gate))
    return scaled * gate, slope, unit, inverse


def back_through_norm(grad_scaled, gain, unit, inverse):
    grad_unit = grad_scaled * gain
    return inverse * (grad_unit - unit * jnp.mean(grad_unit * unit, axis=0, keepdims=True))


CELLS = [(p, q) for p in range(3) for q in range(3)]
OWN = CELLS.index((2, 1))
ORDER = [7, 6, 8, 4, 1, 3, 5, 0, 2]


FAR_FIRST = (4, 5, 3, 6, 2, 7, 1, 0)


def band_of(cell):
    return pl.ds(cell * C, C)


def put_rows(packed, half, raw):
    for n in range(63):
        start = n * 32
        j, r = start // (3 * C), start % (3 * C)
        block = start // 64
        packed[half, block // 8, block % 8, pl.ds(start % 64, 32), :] = raw[
            r : r + 32, j * LANES : (j + 1) * LANES
        ]


def block_kernel(x_hbm, cot_hbm, gain_first_hbm, gain_second_hbm, bias_hbm, k1_hbm, k2_hbm,
                 g_hbm, stats_ref, grad_in_ref,
                 g_ref, squares, x_ref, cot_ref, gain_first_ref, gain_second_ref, bias_ref, k1, k2, k1t, k2t, x_cells, h_cells, d_cells,
                 left, cells, packed,
                 core_in, part, x_out, x_in, y_out, y_in, z_in, vz, vy, vx, vc,
                 local_sem, hx_sem, hc_sem, hh_sem,
                 core_sem, x_sem, y_sem, z_sem, gy_sem, gx_sem, gc_sem,
                 vz_sem, vy_sem, vx_sem, vc_sem, out_sem):
    tm, row = lax.axis_index("tm"), lax.axis_index("row")
    me_x, me_c = tm // 2, tm % 2
    me_z, me_y = row // 8, row % 8
    peer_c = {"tm": me_x * 2 + 1 - me_c, "row": row}

    def at_x(d):
        return lax.rem(me_x + d, 4)

    def at_y(d):
        return lax.rem(me_y + d, 8)

    def at_z(d):
        return lax.rem(me_z + d, 8)

    def peer_x(d):
        return {"tm": at_x(d) * 2 + me_c, "row": row}

    def peer_y(d):
        return {"tm": tm, "row": me_z * 8 + at_y(d)}

    def peer_z(d):
        return {"tm": tm, "row": at_z(d) * 8 + me_y}

    def later(cell):
        p, q = CELLS[cell]
        return {"tm": lax.rem(tm + 2 - p, 8), "row": lax.rem(row + 65 - q, 64)}

    def earlier(cell):
        p, q = CELLS[cell]
        return {"tm": lax.rem(tm + 6 + p, 8), "row": lax.rem(row + 63 + q, 64)}

    def send(src, dst, sems, slot, device):
        copy = pltpu.make_async_remote_copy(
            src_ref=src, dst_ref=dst, send_sem=sems.at[0, slot], recv_sem=sems.at[1, slot],
            device_id=device, device_id_type=MESH,
        )
        copy.start()
        return copy

    pairs = [(x_hbm, x_ref), (cot_hbm, cot_ref), (gain_first_hbm, gain_first_ref),
             (gain_second_hbm, gain_second_ref), (bias_hbm, bias_ref), (k1_hbm, k1), (k2_hbm, k2)]
    loads = [pltpu.make_async_copy(a, b, local_sem.at[k]) for k, (a, b) in enumerate(pairs)]
    for load in loads:
        load.start()

    barrier = pltpu.get_barrier_semaphore()
    halo = [cell for cell in ORDER if cell != OWN]
    peers = [later(cell) for cell in halo] + [earlier(cell) for cell in halo]
    peers += [peer_c] + [peer_x(d) for d in range(1, 4)]
    peers += [peer_y(d) for d in range(1, 8)] + [peer_z(d) for d in range(1, 8)]
    for peer in peers:
        pl.semaphore_signal(barrier, inc=1, device_id=peer, device_id_type=MESH)
    for load in loads[:2]:
        load.wait()
    pl.semaphore_wait(barrier, len(peers))

    sent = []
    x_copies, c_copies = {}, {}
    for cell in halo:
        x_copies[cell] = send(x_ref, x_cells.at[cell], hx_sem, cell, later(cell))
        c_copies[cell] = send(cot_ref, cells.at[1, band_of(cell)], hc_sem, cell, earlier(cell))
    sent += list(x_copies.values()) + list(c_copies.values())

    for load in loads[2:]:
        load.wait()
    gain_first = to_column(gain_first_ref[...])
    gain_second = to_column(gain_second_ref[...])
    bias = to_column(bias_ref[...])
    identity = jnp.where(eye_mask(), 1.0, 0.0).astype(bf16)
    for cell in range(9):
        for s in range(3):
            band = pl.ds(s * C, C)
            k2t[cell, band, :] = dot_nt(identity, k2[cell, band, :]).astype(bf16)
            k1t[cell, band, :] = dot_nt(identity, k1[cell, band, :]).astype(bf16)

    pad = jnp.zeros((32, W), bf16)
    cells[0, pl.ds(9 * C, 32), :] = pad
    cells[1, pl.ds(9 * C, 32), :] = pad
    c_own = cot_ref[...]
    cells[1, band_of(OWN), :] = c_own

    def before(cell):
        p, q = CELLS[cell]
        return (tm + p >= 2) & (row + q >= 1) & (row + q <= 64)

    def after(cell):
        p, q = CELLS[cell]
        return (tm + 2 - p <= 7) & (row + 1 - q >= 0) & (row + 1 - q <= 63)

    sums = jnp.zeros((3 * C, W), f32)
    for cell in ORDER:
        if cell == OWN:
            wide = x_ref[...].astype(f32)
        else:
            x_copies[cell].wait_recv()

            @pl.when(jnp.logical_not(before(cell)))
            def _():
                x_cells[cell] = jnp.zeros((C, W), bf16)

            wide = x_cells[cell].astype(f32)
        value, slope, unit, inverse = act_parts(wide, gain_first)
        if cell == OWN:
            own_slope, own_unit, own_inverse = slope, unit, inverse
        band = band_of(cell)
        rounded = value.astype(bf16)
        cells[0, band, :] = rounded
        d_cells[band, :] = (slope * unit).astype(bf16)
        sums = sums + dot_nn(k1[cell], rounded)
    hidden = shift_columns(sums[:C], -1) + sums[C : 2 * C] + shift_columns(sums[2 * C :], 1)
    hidden = hidden + bias
    second, slope, unit, inverse = act_parts(hidden, gain_second)
    second = second.astype(bf16).astype(f32)
    for s in range(3):
        left[1, pl.ds(s * C, C), :] = shift_columns(second, s - 1).astype(bf16)

    sums = jnp.zeros((3 * C, W), f32)
    for cell in ORDER:
        if cell != OWN:
            c_copies[cell].wait_recv()

            @pl.when(jnp.logical_not(after(cell)))
            def _():
                cells[1, band_of(cell), :] = jnp.zeros((C, W), bf16)

        sums = sums + dot_nn(k2t[cell], cells[1, band_of(cell), :])
    grad_second = shift_columns(sums[:C], 1) + sums[C : 2 * C] + shift_columns(sums[2 * C :], -1)
    grad_scaled = grad_second * slope
    raw_gain_second = jnp.sum(grad_scaled * unit, axis=1, keepdims=True)
    grad_hidden = back_through_norm(grad_scaled, gain_second, unit, inverse)
    raw_bias = jnp.sum(grad_hidden, axis=1, keepdims=True)
    rounded = grad_hidden.astype(bf16)
    raw_cot = jnp.sum(c_own.astype(f32), axis=1, keepdims=True)
    hidden_cot = rounded.astype(f32)
    for s in range(3):
        left[0, pl.ds(s * C, C), :] = shift_columns(hidden_cot, 1 - s).astype(bf16)
    h_own = pl.ds(C, C)

    for half in (0, 1):
        packed[half, 3, 7, pl.ds(32, 32), :] = jnp.zeros((32, LANES), f32)
    put_rows(packed, 1 - me_c, dot_nt(left[1 - me_c], cells[1 - me_c]))
    core_copies = []
    for k, d in enumerate(FAR_FIRST):
        core_copies.append(send(packed.at[1 - me_c, :, at_y(d)], core_in.at[k], core_sem, k, peer_c))
    put_rows(packed, me_c, dot_nt(left[me_c], cells[me_c]))
    x_copies = []
    for k, d in enumerate(FAR_FIRST):
        core_copies[k].wait_recv()
        total = packed[me_c, :, at_y(d)] + core_in[k]
        x_out[k] = total.astype(bf16)
        part[k] = packed[me_c, me_x, at_y(d)] + core_in[k, me_x]
        for e in (2, 1, 3):
            x_copies.append(
                send(x_out.at[k, at_x(e)], x_in.at[k, e - 1], x_sem, k * 3 + e - 1, peer_x(e))
            )
    sent += core_copies + x_copies

    gained = jnp.zeros((3 * C, C), f32)
    for cell in range(9):
        gained = gained + k1[cell].astype(f32) * dot_nt(left[0], d_cells[band_of(cell), :])
    vz[me_z] = jnp.zeros((8, LANES), f32)
    lanes = pl.ds(0, C)
    vz[me_z, pl.ds(0, 1), lanes] = to_row(raw_bias)
    vz[me_z, pl.ds(1, 1), lanes] = jnp.sum(gained, axis=0, keepdims=True)
    vz[me_z, pl.ds(2, 1), lanes] = to_row(raw_gain_second)
    vz[me_z, pl.ds(3, 1), lanes] = to_row(raw_cot)
    v_copies = [send(vz.at[me_z], vz.at[me_z], vz_sem, d - 1, peer_z(d)) for d in range(1, 8)]

    def vector_total(slots, count):
        for copy in v_copies:
            copy.wait_recv()
        sent.extend(v_copies)
        whole = slots[0]
        for e in range(1, count):
            whole = whole + slots[e]
        return whole

    vy[me_y] = vector_total(vz, 8)
    v_copies = [send(vy.at[me_y], vy.at[me_y], vy_sem, d - 1, peer_y(d)) for d in range(1, 8)]

    y_copies = []
    for k, d in enumerate(FAR_FIRST):
        total = part[k]
        for copy in x_copies[3 * k : 3 * k + 3]:
            copy.wait_recv()
        for e in range(3):
            total = total + x_in[k, e].astype(f32)
        if d > 0:
            y_out[k] = total.astype(bf16)
            y_copies.append(send(y_out.at[k], y_in.at[d - 1], y_sem, d - 1, peer_y(d)))
    h_copies = {}
    for cell in halo:
        h_copies[cell] = send(left.at[0, h_own], h_cells.at[cell], hh_sem, cell, earlier(cell))
    for copy in y_copies:
        copy.wait_recv()
    for e in range(7):
        total = total + y_in[e].astype(f32)

    z_in[me_z] = total.astype(bf16)
    z_copies = []
    for d in (4, 3, 5, 2, 6, 1, 7):
        z_copies.append(send(z_in.at[me_z], z_in.at[me_z], z_sem, d - 1, peer_z(d)))
    for copy in sent:
        copy.wait_send()
    sent = []
    vx[me_x] = vector_total(vy, 8)
    v_copies = [send(vx.at[me_x], vx.at[me_x], vx_sem, d - 1, peer_x(d)) for d in range(1, 4)]
    for copy in z_copies:
        copy.wait_recv()
    total = z_in[0].astype(f32)
    for e in range(1, 8):
        total = total + z_in[e].astype(f32)
    rounded = total.astype(bf16)
    g_ref[me_c, me_x, me_y] = rounded
    own_squares = rounded.astype(f32)
    own_squares = own_squares * own_squares
    sent += y_copies + z_copies

    own = g_ref.at[me_c, me_x, me_y]
    gy_copies, gx_copies, gc_copies = {}, {}, []
    for d in (4, 3, 5, 2, 6, 1, 7):
        gy_copies[d] = send(own, own, gy_sem, d - 1, peer_y(d))

    def square(c, x, y):
        whole = jnp.zeros((16, LANES), f32)
        for n in range(4):
            part = g_ref[c, x, y, pl.ds(16 * n, 16), :].astype(f32)
            whole = whole + part * part
        squares[pl.ds(pl.multiple_of((c * 32 + x * 8 + y) * 16, 16), 16), :] = whole

    def pass_on(k, d):
        piece = g_ref.at[me_c, me_x, at_y(8 - d)]
        for e in (2, 1, 3):
            gx_copies[k, e] = send(piece, piece, gx_sem, k * 3 + e - 1, peer_x(e))
        gc_copies.append(send(piece, piece, gc_sem, k * 4, peer_c))
        if d > 0:
            square(me_c, me_x, at_y(8 - d))

    pass_on(0, 0)
    own_rows = pl.ds(pl.multiple_of((me_c * 32 + me_x * 8 + me_y) * 16, 16), 16)
    squares[own_rows, :] = (
        own_squares[:16] + own_squares[16:32] + own_squares[32:48] + own_squares[48:]
    )

    for copy in sent:
        copy.wait_send()
    sent = list(h_copies.values())
    sums = dot_nn(k1t[OWN], left[0, h_own, :])
    for cell in ORDER[1:]:
        h_copies[cell].wait_recv()

        @pl.when(jnp.logical_not(after(cell)))
        def _():
            h_cells[cell] = jnp.zeros((C, W), bf16)

        sums = sums + dot_nn(k1t[cell], h_cells[cell])
    grad_first = shift_columns(sums[:C], 1) + sums[C : 2 * C] + shift_columns(sums[2 * C :], -1)
    input_term = back_through_norm(grad_first * own_slope, gain_first, own_unit, own_inverse)
    grad_in_ref[...] = (c_own.astype(f32) + input_term).astype(bf16)

    for k, d in enumerate((1, 7, 2, 6, 3, 5, 4)):
        gy_copies[d].wait_recv()
        pass_on(k + 1, d)
    for k, d in enumerate((0, 1, 7, 2, 6, 3, 5, 4)):
        for e in (1, 3, 2):
            gx_copies[k, e].wait_recv()
            piece = g_ref.at[me_c, at_x(4 - e), at_y(8 - d)]
            gc_copies.append(send(piece, piece, gc_sem, k * 4 + e, peer_c))
            square(me_c, at_x(4 - e), at_y(8 - d))
        if k == 0:
            vc[me_c] = vector_total(vx, 4)
            v_copies = [send(vc.at[me_c], vc.at[me_c], vc_sem, 0, peer_c)]
    outs = []

    def store(c, x):
        copy = pltpu.make_async_copy(g_ref.at[c, x], g_hbm.at[c, x], out_sem.at[len(outs)])
        copy.start()
        outs.append(copy)

    for x in range(4):
        store(me_c, x)
    for copy in sent:
        copy.wait_send()
    sent = list(gy_copies.values()) + list(gx_copies.values()) + gc_copies
    stats_ref[pl.ds(0, 8), :] = vector_total(vc, 2)
    for k, d in enumerate((0, 1, 7, 2, 6, 3, 5, 4)):
        gc_copies[k].wait_recv()
        square(1 - me_c, me_x, at_y(8 - d))
    for k, d in enumerate((0, 1, 7, 2, 6, 3, 5, 4)):
        for n, e in enumerate((1, 3, 2)):
            gc_copies[8 + 3 * k + n].wait_recv()
            square(1 - me_c, at_x(4 - e), at_y(8 - d))
    for x in range(4):
        store(1 - me_c, x)

    def add_squares(n, whole):
        return whole + squares[pl.ds(pl.multiple_of(n * 128, 128), 128), :]

    whole = lax.fori_loop(0, 8, add_squares, jnp.zeros((128, LANES), f32))
    whole = jnp.sum(whole, axis=0, keepdims=True)
    stats_ref[pl.ds(8, 8), :] = jnp.broadcast_to(whole * 0.125, (8, LANES))
    for copy in sent:
        copy.wait_send()
    for copy in outs:
        copy.wait()


def scale_kernel(g_hbm, stats_hbm, grad_in_hbm, first_hbm, second_hbm, vectors_ref, copy_hbm,
                 g_ref, stats_ref, first_ref, second_ref, load_sem, tile_sem, first_sem, second_sem):
    through = pltpu.make_async_copy(grad_in_hbm, copy_hbm, load_sem.at[0])
    stats_load = pltpu.make_async_copy(stats_hbm, stats_ref, load_sem.at[1])
    stats_load.start()
    loads = []
    for j in range(7):
        for half in (0, 1):
            rows = pl.ds(half * HALF_ROWS + j * 3 * C, 3 * C)
            loads.append(pltpu.make_async_copy(g_hbm.at[rows], g_ref.at[rows], tile_sem.at[half, j]))
            loads[-1].start()
    through.start()
    stats_load.wait()
    stats = stats_ref[...]
    kind = lax.broadcasted_iota(jnp.int32, (16, LANES), 0)
    total = jnp.sum(jnp.where(kind < 8, stats * stats, stats), axis=1, keepdims=True)
    total = jnp.sqrt(jnp.sum(total, axis=0, keepdims=True))
    factor = jnp.minimum(1.0, max_norm / (total + epsilon))
    vectors_ref[...] = stats_ref[pl.ds(0, 4), pl.ds(0, C)] * factor
    target = lax.broadcasted_iota(jnp.int32, (C, LANES), 0)
    lane = lax.broadcasted_iota(jnp.int32, (C, LANES), 1)
    stores = []
    for load in loads:
        load.wait()
    for cell in range(9):
        tiles = range(cell * C // LANES, (cell * C + C - 1) // LANES + 1)
        first = jnp.zeros((3 * C, C), f32)
        second = [jnp.zeros((C, C), f32) for _ in range(3)]
        for j in tiles:
            pick = jnp.where(lane + (j * LANES - cell * C) == target, 1.0, 0.0).astype(bf16)
            first = first + dot_nt(g_ref[pl.ds(j * 3 * C, 3 * C), :], pick)
            for s in range(3):
                start = HALF_ROWS + j * 3 * C + s * C
                second[s] = second[s] + dot_nt(pick, g_ref[pl.ds(start, C), :])
        first_ref[cell] = first * factor
        for s in range(3):
            second_ref[cell, pl.ds(s * C, C), :] = second[s] * factor
        stores.append(
            pltpu.make_async_copy(first_ref.at[cell], first_hbm.at[cell], first_sem.at[cell])
        )
        stores[-1].start()
        stores.append(
            pltpu.make_async_copy(second_ref.at[cell], second_hbm.at[cell], second_sem.at[cell])
        )
        stores[-1].start()
    through.wait()
    for copy in stores:
        copy.wait()


def body(inputs, cotangent, gain_first, gain_second, bias_first, kernel_first, kernel_second):
    dma, vmem = pltpu.SemaphoreType.DMA, pltpu.VMEM
    in_vmem = pl.BlockSpec(memory_space=pltpu.VMEM)
    in_any = pl.BlockSpec(memory_space=pl.ANY)
    summed, stats, grad_inputs = pl.pallas_call(
        block_kernel,
        out_shape=(
            jax.ShapeDtypeStruct((2, 4, 8, 64, LANES), bf16),
            jax.ShapeDtypeStruct((16, LANES), f32),
            jax.ShapeDtypeStruct((C, W), bf16),
        ),
        in_specs=[in_any] * 7,
        out_specs=(in_any, in_vmem, in_vmem),
        scratch_shapes=[
            vmem((2, 4, 8, 64, LANES), bf16), vmem((1024, LANES), f32),
            vmem((C, W), bf16), vmem((C, W), bf16),
            vmem((1, C), f32), vmem((1, C), f32), vmem((1, C), f32),
            vmem((9, 3 * C, C), bf16), vmem((9, 3 * C, C), bf16),
            vmem((9, 3 * C, C), bf16), vmem((9, 3 * C, C), bf16),
            vmem((9, C, W), bf16), vmem((9, C, W), bf16), vmem((9 * C, W), bf16),
            vmem((2, 3 * C, W), bf16), vmem((2, 9 * C + 32, W), bf16),
            vmem((2, 4, 8, 64, LANES), f32),
            vmem((8, 4, 64, LANES), f32),
            vmem((8, 64, LANES), f32),
            vmem((8, 4, 64, LANES), bf16),
            vmem((8, 3, 64, LANES), bf16),
            vmem((7, 64, LANES), bf16),
            vmem((7, 64, LANES), bf16),
            vmem((8, 64, LANES), bf16),
            vmem((8, 8, LANES), f32), vmem((8, 8, LANES), f32),
            vmem((4, 8, LANES), f32), vmem((2, 8, LANES), f32),
            dma((7,)), dma((2, 9)), dma((2, 9)), dma((2, 9)),
            dma((2, 8)), dma((2, 24)), dma((2, 7)), dma((2, 7)),
            dma((2, 7)), dma((2, 24)), dma((2, 32)),
            dma((2, 7)), dma((2, 7)), dma((2, 3)), dma((2, 1)), dma((8,)),
        ],
        compiler_params=pltpu.CompilerParams(
            collective_id=0, has_side_effects=True, vmem_limit_bytes=60 * 1024 * 1024
        ),
    )(
        inputs.reshape(C, W), cotangent.reshape(C, W),
        gain_first.reshape(1, C), gain_second.reshape(1, C), bias_first.reshape(1, C),
        kernel_first.reshape(9, 3 * C, C), kernel_second.reshape(9, 3 * C, C),
    )
    grad_first, grad_second, vectors, grad_inputs = pl.pallas_call(
        scale_kernel,
        out_shape=(
            jax.ShapeDtypeStruct((9, 3 * C, C), f32),
            jax.ShapeDtypeStruct((9, 3 * C, C), f32),
            jax.ShapeDtypeStruct((4, C), f32),
            jax.ShapeDtypeStruct((C, W), bf16),
        ),
        in_specs=[in_any] * 3,
        out_specs=(in_any, in_any, in_vmem, in_any),
        scratch_shapes=[
            vmem((2 * HALF_ROWS, LANES), bf16), vmem((16, LANES), f32),
            vmem((9, 3 * C, C), f32), vmem((9, 3 * C, C), f32),
            dma((2,)), dma((2, 7)), dma((9,)), dma((9,)),
        ],
        compiler_params=pltpu.CompilerParams(vmem_limit_bytes=60 * 1024 * 1024),
    )(summed.reshape(2 * HALF_ROWS, LANES), stats, grad_inputs)
    return (
        grad_inputs.reshape(inputs.shape),
        grad_first.reshape(kernel_first.shape),
        grad_second.reshape(kernel_second.shape),
        vectors,
    )


def solution(mesh):
    in_specs = (P(None, "tm", "row", None), P(None, "tm", "row", None), P(), P(), P(), P(), P())
    out_specs = (P(None, "tm", "row", None), P(), P(), P())
    return jax.shard_map(body, mesh=mesh, in_specs=in_specs, out_specs=out_specs, check_vma=False)
```

```python
import jax
import jax.numpy as jnp
from jax import lax
from jax.experimental import pallas as pl
from jax.experimental.pallas import tpu as pltpu
from jax.sharding import PartitionSpec as P

epsilon = 1e-06
max_norm = 500.0
C = 96
W = 256
HALF_ROWS = 2048
LANES = 128
MESH = pl.DeviceIdType.MESH
f32, bf16 = jnp.float32, jnp.bfloat16


def dot_nt(a, b):
    return lax.dot_general(a, b, (((1,), (1,)), ((), ())), preferred_element_type=f32)


def dot_nn(a, b):
    return lax.dot_general(a, b, (((1,), (0,)), ((), ())), preferred_element_type=f32)


def eye_mask():
    rows = lax.broadcasted_iota(jnp.int32, (C, C), 0)
    return rows == lax.broadcasted_iota(jnp.int32, (C, C), 1)


def to_column(row):
    spread = jnp.broadcast_to(row, (C, C))
    return jnp.sum(jnp.where(eye_mask(), spread, 0.0), axis=1, keepdims=True)


def to_row(column):
    spread = jnp.broadcast_to(column, (C, C))
    return jnp.sum(jnp.where(eye_mask(), spread, 0.0), axis=0, keepdims=True)


def shift_columns(values, offset):
    if offset == 0:
        return values
    column = lax.broadcasted_iota(jnp.int32, values.shape, 1)
    rolled = pltpu.roll(values, (-offset) % W, 1)
    edge = W - 1 if offset > 0 else 0
    return jnp.where(column == edge, 0.0, rolled)


def normalised(values):
    meansq = jnp.mean(values * values, axis=0, keepdims=True)
    inverse = lax.rsqrt(meansq + epsilon)
    return values * inverse, inverse


def act_parts(values, gain):
    unit, inverse = normalised(values)
    scaled = unit * gain
    gate = 1.0 / (1.0 + jnp.exp(-scaled))
    slope = gate * (1.0 + scaled * (1.0 - gate))
    return scaled * gate, slope, unit, inverse


def back_through_norm(grad_scaled, gain, unit, inverse):
    grad_unit = grad_scaled * gain
    return inverse * (grad_unit - unit * jnp.mean(grad_unit * unit, axis=0, keepdims=True))


CELLS = [(p, q) for p in range(3) for q in range(3)]
OWN = CELLS.index((2, 1))
ORDER = [7, 6, 8, 4, 1, 3, 5, 0, 2]


FAR_FIRST = (4, 5, 3, 6, 2, 7, 1, 0)


def band_of(cell):
    return pl.ds(cell * C, C)


def put_rows(packed, half, raw):
    for n in range(63):
        start = n * 32
        j, r = start // (3 * C), start % (3 * C)
        block = start // 64
        packed[half, block // 8, block % 8, pl.ds(start % 64, 32), :] = raw[
            r : r + 32, j * LANES : (j + 1) * LANES
        ]


def block_kernel(x_hbm, cot_hbm, gain_first_hbm, gain_second_hbm, bias_hbm, k1_hbm, k2_hbm,
                 g_ref, stats_ref, grad_in_ref,
                 squares, x_ref, cot_ref, gain_first_ref, gain_second_ref, bias_ref, k1, k2, k1t, k2t, x_cells, h_cells, d_cells,
                 left, cells, packed,
                 core_in, part, x_out, x_in, y_out, y_in, z_in, vz, vy, vx, vc,
                 local_sem, hx_sem, hc_sem, hh_sem,
                 core_sem, x_sem, y_sem, z_sem, gy_sem, gx_sem, gc_sem,
                 vz_sem, vy_sem, vx_sem, vc_sem):
    tm, row = lax.axis_index("tm"), lax.axis_index("row")
    me_x, me_c = tm // 2, tm % 2
    me_z, me_y = row // 8, row % 8
    peer_c = {"tm": me_x * 2 + 1 - me_c, "row": row}

    def at_x(d):
        return lax.rem(me_x + d, 4)

    def at_y(d):
        return lax.rem(me_y + d, 8)

    def at_z(d):
        return lax.rem(me_z + d, 8)

    def peer_x(d):
        return {"tm": at_x(d) * 2 + me_c, "row": row}

    def peer_y(d):
        return {"tm": tm, "row": me_z * 8 + at_y(d)}

    def peer_z(d):
        return {"tm": tm, "row": at_z(d) * 8 + me_y}

    def later(cell):
        p, q = CELLS[cell]
        return {"tm": lax.rem(tm + 2 - p, 8), "row": lax.rem(row + 65 - q, 64)}

    def earlier(cell):
        p, q = CELLS[cell]
        return {"tm": lax.rem(tm + 6 + p, 8), "row": lax.rem(row + 63 + q, 64)}

    def send(src, dst, sems, slot, device):
        copy = pltpu.make_async_remote_copy(
            src_ref=src, dst_ref=dst, send_sem=sems.at[0, slot], recv_sem=sems.at[1, slot],
            device_id=device, device_id_type=MESH,
        )
        copy.start()
        return copy

    pairs = [(x_hbm, x_ref), (cot_hbm, cot_ref), (gain_first_hbm, gain_first_ref),
             (gain_second_hbm, gain_second_ref), (bias_hbm, bias_ref), (k1_hbm, k1), (k2_hbm, k2)]
    loads = [pltpu.make_async_copy(a, b, local_sem.at[k]) for k, (a, b) in enumerate(pairs)]
    for load in loads:
        load.start()

    barrier = pltpu.get_barrier_semaphore()
    halo = [cell for cell in ORDER if cell != OWN]
    peers = [later(cell) for cell in halo] + [earlier(cell) for cell in halo]
    peers += [peer_c] + [peer_x(d) for d in range(1, 4)]
    peers += [peer_y(d) for d in range(1, 8)] + [peer_z(d) for d in range(1, 8)]
    for peer in peers:
        pl.semaphore_signal(barrier, inc=1, device_id=peer, device_id_type=MESH)
    for load in loads[:2]:
        load.wait()
    pl.semaphore_wait(barrier, len(peers))

    sent = []
    x_copies, c_copies = {}, {}
    for cell in halo:
        x_copies[cell] = send(x_ref, x_cells.at[cell], hx_sem, cell, later(cell))
        c_copies[cell] = send(cot_ref, cells.at[1, band_of(cell)], hc_sem, cell, earlier(cell))
    sent += list(x_copies.values()) + list(c_copies.values())

    for load in loads[2:]:
        load.wait()
    gain_first = to_column(gain_first_ref[...])
    gain_second = to_column(gain_second_ref[...])
    bias = to_column(bias_ref[...])
    identity = jnp.where(eye_mask(), 1.0, 0.0).astype(bf16)
    for cell in range(9):
        for s in range(3):
            band = pl.ds(s * C, C)
            k2t[cell, band, :] = dot_nt(identity, k2[cell, band, :]).astype(bf16)
            k1t[cell, band, :] = dot_nt(identity, k1[cell, band, :]).astype(bf16)

    pad = jnp.zeros((32, W), bf16)
    cells[0, pl.ds(9 * C, 32), :] = pad
    cells[1, pl.ds(9 * C, 32), :] = pad
    c_own = cot_ref[...]
    cells[1, band_of(OWN), :] = c_own

    def before(cell):
        p, q = CELLS[cell]
        return (tm + p >= 2) & (row + q >= 1) & (row + q <= 64)

    def after(cell):
        p, q = CELLS[cell]
        return (tm + 2 - p <= 7) & (row + 1 - q >= 0) & (row + 1 - q <= 63)

    sums = jnp.zeros((3 * C, W), f32)
    for cell in ORDER:
        if cell == OWN:
            wide = x_ref[...].astype(f32)
        else:
            x_copies[cell].wait_recv()

            @pl.when(jnp.logical_not(before(cell)))
            def _():
                x_cells[cell] = jnp.zeros((C, W), bf16)

            wide = x_cells[cell].astype(f32)
        value, slope, unit, inverse = act_parts(wide, gain_first)
        if cell == OWN:
            own_slope, own_unit, own_inverse = slope, unit, inverse
        band = band_of(cell)
        rounded = value.astype(bf16)
        cells[0, band, :] = rounded
        d_cells[band, :] = (slope * unit).astype(bf16)
        sums = sums + dot_nn(k1[cell], rounded)
    hidden = shift_columns(sums[:C], -1) + sums[C : 2 * C] + shift_columns(sums[2 * C :], 1)
    hidden = hidden + bias
    second, slope, unit, inverse = act_parts(hidden, gain_second)
    second = second.astype(bf16).astype(f32)
    for s in range(3):
        left[1, pl.ds(s * C, C), :] = shift_columns(second, s - 1).astype(bf16)

    sums = jnp.zeros((3 * C, W), f32)
    for cell in ORDER:
        if cell != OWN:
            c_copies[cell].wait_recv()

            @pl.when(jnp.logical_not(after(cell)))
            def _():
                cells[1, band_of(cell), :] = jnp.zeros((C, W), bf16)

        sums = sums + dot_nn(k2t[cell], cells[1, band_of(cell), :])
    grad_second = shift_columns(sums[:C], 1) + sums[C : 2 * C] + shift_columns(sums[2 * C :], -1)
    grad_scaled = grad_second * slope
    raw_gain_second = jnp.sum(grad_scaled * unit, axis=1, keepdims=True)
    grad_hidden = back_through_norm(grad_scaled, gain_second, unit, inverse)
    raw_bias = jnp.sum(grad_hidden, axis=1, keepdims=True)
    rounded = grad_hidden.astype(bf16)
    raw_cot = jnp.sum(c_own.astype(f32), axis=1, keepdims=True)
    hidden_cot = rounded.astype(f32)
    for s in range(3):
        left[0, pl.ds(s * C, C), :] = shift_columns(hidden_cot, 1 - s).astype(bf16)
    h_own = pl.ds(C, C)

    for half in (0, 1):
        packed[half, 3, 7, pl.ds(32, 32), :] = jnp.zeros((32, LANES), f32)
    put_rows(packed, 1 - me_c, dot_nt(left[1 - me_c], cells[1 - me_c]))
    core_copies = []
    for k, d in enumerate(FAR_FIRST):
        core_copies.append(send(packed.at[1 - me_c, :, at_y(d)], core_in.at[k], core_sem, k, peer_c))
    put_rows(packed, me_c, dot_nt(left[me_c], cells[me_c]))
    x_copies = []
    for k, d in enumerate(FAR_FIRST):
        core_copies[k].wait_recv()
        total = packed[me_c, :, at_y(d)] + core_in[k]
        x_out[k] = total.astype(bf16)
        part[k] = packed[me_c, me_x, at_y(d)] + core_in[k, me_x]
        for e in (2, 1, 3):
            x_copies.append(
                send(x_out.at[k, at_x(e)], x_in.at[k, e - 1], x_sem, k * 3 + e - 1, peer_x(e))
            )
    sent += core_copies + x_copies

    gained = jnp.zeros((3 * C, C), f32)
    for cell in range(9):
        gained = gained + k1[cell].astype(f32) * dot_nt(left[0], d_cells[band_of(cell), :])
    vz[me_z] = jnp.zeros((8, LANES), f32)
    lanes = pl.ds(0, C)
    vz[me_z, pl.ds(0, 1), lanes] = to_row(raw_bias)
    vz[me_z, pl.ds(1, 1), lanes] = jnp.sum(gained, axis=0, keepdims=True)
    vz[me_z, pl.ds(2, 1), lanes] = to_row(raw_gain_second)
    vz[me_z, pl.ds(3, 1), lanes] = to_row(raw_cot)
    v_copies = [send(vz.at[me_z], vz.at[me_z], vz_sem, d - 1, peer_z(d)) for d in range(1, 8)]

    def vector_total(slots, count):
        for copy in v_copies:
            copy.wait_recv()
        sent.extend(v_copies)
        whole = slots[0]
        for e in range(1, count):
            whole = whole + slots[e]
        return whole

    vy[me_y] = vector_total(vz, 8)
    v_copies = [send(vy.at[me_y], vy.at[me_y], vy_sem, d - 1, peer_y(d)) for d in range(1, 8)]

    y_copies = []
    for k, d in enumerate(FAR_FIRST):
        total = part[k]
        for copy in x_copies[3 * k : 3 * k + 3]:
            copy.wait_recv()
        for e in range(3):
            total = total + x_in[k, e].astype(f32)
        if d > 0:
            y_out[k] = total.astype(bf16)
            y_copies.append(send(y_out.at[k], y_in.at[d - 1], y_sem, d - 1, peer_y(d)))
    h_copies = {}
    for cell in halo:
        h_copies[cell] = send(left.at[0, h_own], h_cells.at[cell], hh_sem, cell, earlier(cell))
    for copy in y_copies:
        copy.wait_recv()
    for e in range(7):
        total = total + y_in[e].astype(f32)

    z_in[me_z] = total.astype(bf16)
    z_copies = []
    for d in (4, 3, 5, 2, 6, 1, 7):
        z_copies.append(send(z_in.at[me_z], z_in.at[me_z], z_sem, d - 1, peer_z(d)))
    for copy in sent:
        copy.wait_send()
    sent = []
    vx[me_x] = vector_total(vy, 8)
    v_copies = [send(vx.at[me_x], vx.at[me_x], vx_sem, d - 1, peer_x(d)) for d in range(1, 4)]
    for copy in z_copies:
        copy.wait_recv()
    total = z_in[0].astype(f32)
    for e in range(1, 8):
        total = total + z_in[e].astype(f32)
    rounded = total.astype(bf16)
    g_ref[me_c, me_x, me_y] = rounded
    own_squares = rounded.astype(f32)
    own_squares = own_squares * own_squares
    sent += y_copies + z_copies

    own = g_ref.at[me_c, me_x, me_y]
    gy_copies, gx_copies, gc_copies = {}, {}, []
    for d in (4, 3, 5, 2, 6, 1, 7):
        gy_copies[d] = send(own, own, gy_sem, d - 1, peer_y(d))

    def square(c, x, y):
        whole = jnp.zeros((16, LANES), f32)
        for n in range(4):
            part = g_ref[c, x, y, pl.ds(16 * n, 16), :].astype(f32)
            whole = whole + part * part
        squares[pl.ds(pl.multiple_of((c * 32 + x * 8 + y) * 16, 16), 16), :] = whole

    def pass_on(k, d):
        piece = g_ref.at[me_c, me_x, at_y(8 - d)]
        for e in (2, 1, 3):
            gx_copies[k, e] = send(piece, piece, gx_sem, k * 3 + e - 1, peer_x(e))
        gc_copies.append(send(piece, piece, gc_sem, k * 4, peer_c))
        if d > 0:
            square(me_c, me_x, at_y(8 - d))

    pass_on(0, 0)
    own_rows = pl.ds(pl.multiple_of((me_c * 32 + me_x * 8 + me_y) * 16, 16), 16)
    squares[own_rows, :] = (
        own_squares[:16] + own_squares[16:32] + own_squares[32:48] + own_squares[48:]
    )

    for copy in sent:
        copy.wait_send()
    sent = list(h_copies.values())
    sums = dot_nn(k1t[OWN], left[0, h_own, :])
    for cell in ORDER[1:]:
        h_copies[cell].wait_recv()

        @pl.when(jnp.logical_not(after(cell)))
        def _():
            h_cells[cell] = jnp.zeros((C, W), bf16)

        sums = sums + dot_nn(k1t[cell], h_cells[cell])
    grad_first = shift_columns(sums[:C], 1) + sums[C : 2 * C] + shift_columns(sums[2 * C :], -1)
    input_term = back_through_norm(grad_first * own_slope, gain_first, own_unit, own_inverse)
    grad_in_ref[...] = (c_own.astype(f32) + input_term).astype(bf16)

    for k, d in enumerate((1, 7, 2, 6, 3, 5, 4)):
        gy_copies[d].wait_recv()
        pass_on(k + 1, d)
    for k, d in enumerate((0, 1, 7, 2, 6, 3, 5, 4)):
        for e in (1, 3, 2):
            gx_copies[k, e].wait_recv()
            piece = g_ref.at[me_c, at_x(4 - e), at_y(8 - d)]
            gc_copies.append(send(piece, piece, gc_sem, k * 4 + e, peer_c))
            square(me_c, at_x(4 - e), at_y(8 - d))
        if k == 0:
            vc[me_c] = vector_total(vx, 4)
            v_copies = [send(vc.at[me_c], vc.at[me_c], vc_sem, 0, peer_c)]
    for copy in sent:
        copy.wait_send()
    sent = list(gy_copies.values()) + list(gx_copies.values()) + gc_copies
    stats_ref[pl.ds(0, 8), :] = vector_total(vc, 2)
    for k, d in enumerate((0, 1, 7, 2, 6, 3, 5, 4)):
        gc_copies[k].wait_recv()
        square(1 - me_c, me_x, at_y(8 - d))
    for k, d in enumerate((0, 1, 7, 2, 6, 3, 5, 4)):
        for n, e in enumerate((1, 3, 2)):
            gc_copies[8 + 3 * k + n].wait_recv()
            square(1 - me_c, at_x(4 - e), at_y(8 - d))

    def add_squares(n, whole):
        return whole + squares[pl.ds(pl.multiple_of(n * 128, 128), 128), :]

    whole = lax.fori_loop(0, 8, add_squares, jnp.zeros((128, LANES), f32))
    whole = jnp.sum(whole, axis=0, keepdims=True)
    stats_ref[pl.ds(8, 8), :] = jnp.broadcast_to(whole * 0.125, (8, LANES))
    for copy in sent:
        copy.wait_send()


def scale_kernel(g_ref, stats_ref, grad_in_ref, first_hbm, second_hbm, vectors_ref, copy_hbm,
                 first_ref, second_ref, copy_sem, first_sem, second_sem):
    through = pltpu.make_async_copy(grad_in_ref, copy_hbm, copy_sem.at[0])
    through.start()
    stats = stats_ref[...]
    kind = lax.broadcasted_iota(jnp.int32, (16, LANES), 0)
    total = jnp.sum(jnp.where(kind < 8, stats * stats, stats), axis=1, keepdims=True)
    total = jnp.sqrt(jnp.sum(total, axis=0, keepdims=True))
    factor = jnp.minimum(1.0, max_norm / (total + epsilon))
    vectors_ref[...] = stats_ref[pl.ds(0, 4), pl.ds(0, C)] * factor
    target = lax.broadcasted_iota(jnp.int32, (C, LANES), 0)
    lane = lax.broadcasted_iota(jnp.int32, (C, LANES), 1)
    stores = []
    for cell in range(9):
        tiles = range(cell * C // LANES, (cell * C + C - 1) // LANES + 1)
        first = jnp.zeros((3 * C, C), f32)
        second = [jnp.zeros((C, C), f32) for _ in range(3)]
        for j in tiles:
            pick = jnp.where(lane + (j * LANES - cell * C) == target, 1.0, 0.0).astype(bf16)
            first = first + dot_nt(g_ref[pl.ds(j * 3 * C, 3 * C), :], pick)
            for s in range(3):
                start = HALF_ROWS + j * 3 * C + s * C
                second[s] = second[s] + dot_nt(pick, g_ref[pl.ds(start, C), :])
        first_ref[cell] = first * factor
        for s in range(3):
            second_ref[cell, pl.ds(s * C, C), :] = second[s] * factor
        stores.append(
            pltpu.make_async_copy(first_ref.at[cell], first_hbm.at[cell], first_sem.at[cell])
        )
        stores[-1].start()
        stores.append(
            pltpu.make_async_copy(second_ref.at[cell], second_hbm.at[cell], second_sem.at[cell])
        )
        stores[-1].start()
    through.wait()
    for copy in stores:
        copy.wait()


def body(inputs, cotangent, gain_first, gain_second, bias_first, kernel_first, kernel_second):
    dma, vmem = pltpu.SemaphoreType.DMA, pltpu.VMEM
    in_vmem = pl.BlockSpec(memory_space=pltpu.VMEM)
    in_any = pl.BlockSpec(memory_space=pl.ANY)
    summed, stats, grad_inputs = pl.pallas_call(
        block_kernel,
        out_shape=(
            jax.ShapeDtypeStruct((2, 4, 8, 64, LANES), bf16),
            jax.ShapeDtypeStruct((16, LANES), f32),
            jax.ShapeDtypeStruct((C, W), bf16),
        ),
        in_specs=[pl.BlockSpec(memory_space=pltpu.HBM)] * 7,
        out_specs=(in_vmem, in_vmem, in_vmem),
        scratch_shapes=[
            vmem((1024, LANES), f32),
            vmem((C, W), bf16), vmem((C, W), bf16),
            vmem((1, C), f32), vmem((1, C), f32), vmem((1, C), f32),
            vmem((9, 3 * C, C), bf16), vmem((9, 3 * C, C), bf16),
            vmem((9, 3 * C, C), bf16), vmem((9, 3 * C, C), bf16),
            vmem((9, C, W), bf16), vmem((9, C, W), bf16), vmem((9 * C, W), bf16),
            vmem((2, 3 * C, W), bf16), vmem((2, 9 * C + 32, W), bf16),
            vmem((2, 4, 8, 64, LANES), f32),
            vmem((8, 4, 64, LANES), f32),
            vmem((8, 64, LANES), f32),
            vmem((8, 4, 64, LANES), bf16),
            vmem((8, 3, 64, LANES), bf16),
            vmem((7, 64, LANES), bf16),
            vmem((7, 64, LANES), bf16),
            vmem((8, 64, LANES), bf16),
            vmem((8, 8, LANES), f32), vmem((8, 8, LANES), f32),
            vmem((4, 8, LANES), f32), vmem((2, 8, LANES), f32),
            dma((7,)), dma((2, 9)), dma((2, 9)), dma((2, 9)),
            dma((2, 8)), dma((2, 24)), dma((2, 7)), dma((2, 7)),
            dma((2, 7)), dma((2, 24)), dma((2, 32)),
            dma((2, 7)), dma((2, 7)), dma((2, 3)), dma((2, 1)),
        ],
        compiler_params=pltpu.CompilerParams(
            collective_id=0, has_side_effects=True, vmem_limit_bytes=44 * 1024 * 1024
        ),
    )(
        *(
            pltpu.with_memory_space_constraint(operand, pltpu.HBM)
            for operand in (
                inputs.reshape(C, W), cotangent.reshape(C, W),
                gain_first.reshape(1, C), gain_second.reshape(1, C), bias_first.reshape(1, C),
                kernel_first.reshape(9, 3 * C, C), kernel_second.reshape(9, 3 * C, C),
            )
        )
    )
    grad_first, grad_second, vectors, grad_inputs = pl.pallas_call(
        scale_kernel,
        out_shape=(
            jax.ShapeDtypeStruct((9, 3 * C, C), f32),
            jax.ShapeDtypeStruct((9, 3 * C, C), f32),
            jax.ShapeDtypeStruct((4, C), f32),
            jax.ShapeDtypeStruct((C, W), bf16),
        ),
        in_specs=[in_vmem] * 3,
        out_specs=(in_any, in_any, in_vmem, in_any),
        scratch_shapes=[
            vmem((9, 3 * C, C), f32), vmem((9, 3 * C, C), f32),
            dma((1,)), dma((9,)), dma((9,)),
        ],
        compiler_params=pltpu.CompilerParams(vmem_limit_bytes=44 * 1024 * 1024),
    )(summed.reshape(2 * HALF_ROWS, LANES), stats, grad_inputs)
    return (
        grad_inputs.reshape(inputs.shape),
        grad_first.reshape(kernel_first.shape),
        grad_second.reshape(kernel_second.shape),
        vectors,
    )


def solution(mesh):
    in_specs = (P(None, "tm", "row", None), P(None, "tm", "row", None), P(), P(), P(), P(), P())
    out_specs = (P(None, "tm", "row", None), P(), P(), P())
    return jax.shard_map(body, mesh=mesh, in_specs=in_specs, out_specs=out_specs, check_vma=False)
```

```python
import jax
import jax.numpy as jnp
from jax import lax
from jax.experimental import pallas as pl
from jax.experimental.pallas import tpu as pltpu
from jax.sharding import PartitionSpec as P

epsilon = 1e-06
max_norm = 500.0
C = 96
W = 256
HALF_ROWS = 2048
LANES = 128
MESH = pl.DeviceIdType.MESH
f32, bf16 = jnp.float32, jnp.bfloat16


def dot_nt(a, b):
    return lax.dot_general(a, b, (((1,), (1,)), ((), ())), preferred_element_type=f32)


def dot_nn(a, b):
    return lax.dot_general(a, b, (((1,), (0,)), ((), ())), preferred_element_type=f32)


def eye_mask():
    rows = lax.broadcasted_iota(jnp.int32, (C, C), 0)
    return rows == lax.broadcasted_iota(jnp.int32, (C, C), 1)


def to_column(row):
    spread = jnp.broadcast_to(row, (C, C))
    return jnp.sum(jnp.where(eye_mask(), spread, 0.0), axis=1, keepdims=True)


def to_row(column):
    spread = jnp.broadcast_to(column, (C, C))
    return jnp.sum(jnp.where(eye_mask(), spread, 0.0), axis=0, keepdims=True)


def shift_columns(values, offset):
    if offset == 0:
        return values
    column = lax.broadcasted_iota(jnp.int32, values.shape, 1)
    rolled = pltpu.roll(values, (-offset) % W, 1)
    edge = W - 1 if offset > 0 else 0
    return jnp.where(column == edge, 0.0, rolled)


def normalised(values):
    meansq = jnp.mean(values * values, axis=0, keepdims=True)
    inverse = lax.rsqrt(meansq + epsilon)
    return values * inverse, inverse


def act_parts(values, gain):
    unit, inverse = normalised(values)
    scaled = unit * gain
    gate = 1.0 / (1.0 + jnp.exp(-scaled))
    slope = gate * (1.0 + scaled * (1.0 - gate))
    return scaled * gate, slope, unit, inverse


def back_through_norm(grad_scaled, gain, unit, inverse):
    grad_unit = grad_scaled * gain
    return inverse * (grad_unit - unit * jnp.mean(grad_unit * unit, axis=0, keepdims=True))


CELLS = [(p, q) for p in range(3) for q in range(3)]
OWN = CELLS.index((2, 1))
ORDER = [7, 6, 8, 4, 1, 3, 5, 0, 2]


FAR_FIRST = (4, 5, 3, 6, 2, 7, 1, 0)


def band_of(cell):
    return pl.ds(cell * C, C)


def put_rows(packed, half, raw):
    for n in range(63):
        start = n * 32
        j, r = start // (3 * C), start % (3 * C)
        block = start // 64
        packed[half, block // 8, block % 8, pl.ds(start % 64, 32), :] = raw[
            r : r + 32, j * LANES : (j + 1) * LANES
        ]


def block_kernel(x_hbm, cot_hbm, gain_first_hbm, gain_second_hbm, bias_hbm, k1_hbm, k2_hbm,
                 g_ref, stats_ref, grad_in_ref,
                 squares, x_ref, cot_ref, gain_first_ref, gain_second_ref, bias_ref, k1, k2, k1t, k2t, x_cells, h_cells, d_cells,
                 left, cells, packed,
                 core_in, part, x_out, x_in, y_out, y_in, z_in, vz, vy, vx, vc,
                 local_sem, hx_sem, hc_sem, hh_sem,
                 core_sem, x_sem, y_sem, z_sem, gy_sem, gx_sem, gc_sem,
                 vz_sem, vy_sem, vx_sem, vc_sem):
    tm, row = lax.axis_index("tm"), lax.axis_index("row")
    me_x, me_c = tm // 2, tm % 2
    me_z, me_y = row // 8, row % 8
    peer_c = {"tm": me_x * 2 + 1 - me_c, "row": row}

    def at_x(d):
        return lax.rem(me_x + d, 4)

    def at_y(d):
        return lax.rem(me_y + d, 8)

    def at_z(d):
        return lax.rem(me_z + d, 8)

    def peer_x(d):
        return {"tm": at_x(d) * 2 + me_c, "row": row}

    def peer_y(d):
        return {"tm": tm, "row": me_z * 8 + at_y(d)}

    def peer_z(d):
        return {"tm": tm, "row": at_z(d) * 8 + me_y}

    def later(cell):
        p, q = CELLS[cell]
        return {"tm": lax.rem(tm + 2 - p, 8), "row": lax.rem(row + 65 - q, 64)}

    def earlier(cell):
        p, q = CELLS[cell]
        return {"tm": lax.rem(tm + 6 + p, 8), "row": lax.rem(row + 63 + q, 64)}

    def send(src, dst, sems, slot, device):
        copy = pltpu.make_async_remote_copy(
            src_ref=src, dst_ref=dst, send_sem=sems.at[0, slot], recv_sem=sems.at[1, slot],
            device_id=device, device_id_type=MESH,
        )
        copy.start()
        return copy

    pairs = [(x_hbm, x_ref), (cot_hbm, cot_ref), (gain_first_hbm, gain_first_ref),
             (gain_second_hbm, gain_second_ref), (bias_hbm, bias_ref), (k1_hbm, k1), (k2_hbm, k2)]
    loads = [pltpu.make_async_copy(a, b, local_sem.at[k]) for k, (a, b) in enumerate(pairs)]
    for load in loads:
        load.start()

    barrier = pltpu.get_barrier_semaphore()
    halo = [cell for cell in ORDER if cell != OWN]
    peers = [later(cell) for cell in halo] + [earlier(cell) for cell in halo]
    peers += [peer_c] + [peer_x(d) for d in range(1, 4)]
    peers += [peer_y(d) for d in range(1, 8)] + [peer_z(d) for d in range(1, 8)]
    for peer in peers:
        pl.semaphore_signal(barrier, inc=1, device_id=peer, device_id_type=MESH)
    for load in loads[:2]:
        load.wait()
    pl.semaphore_wait(barrier, len(peers))

    sent = []
    x_copies, c_copies = {}, {}
    for cell in halo:
        x_copies[cell] = send(x_ref, x_cells.at[cell], hx_sem, cell, later(cell))
        c_copies[cell] = send(cot_ref, cells.at[1, band_of(cell)], hc_sem, cell, earlier(cell))
    sent += list(x_copies.values()) + list(c_copies.values())

    for load in loads[2:]:
        load.wait()
    gain_first = to_column(gain_first_ref[...])
    gain_second = to_column(gain_second_ref[...])
    bias = to_column(bias_ref[...])
    identity = jnp.where(eye_mask(), 1.0, 0.0).astype(bf16)
    for cell in range(9):
        for s in range(3):
            band = pl.ds(s * C, C)
            k2t[cell, band, :] = dot_nt(identity, k2[cell, band, :]).astype(bf16)
            k1t[cell, band, :] = dot_nt(identity, k1[cell, band, :]).astype(bf16)

    pad = jnp.zeros((32, W), bf16)
    cells[0, pl.ds(9 * C, 32), :] = pad
    cells[1, pl.ds(9 * C, 32), :] = pad
    c_own = cot_ref[...]
    cells[1, band_of(OWN), :] = c_own

    def before(cell):
        p, q = CELLS[cell]
        return (tm + p >= 2) & (row + q >= 1) & (row + q <= 64)

    def after(cell):
        p, q = CELLS[cell]
        return (tm + 2 - p <= 7) & (row + 1 - q >= 0) & (row + 1 - q <= 63)

    sums = jnp.zeros((3 * C, W), f32)
    for cell in ORDER:
        if cell == OWN:
            wide = x_ref[...].astype(f32)
        else:
            x_copies[cell].wait_recv()

            @pl.when(jnp.logical_not(before(cell)))
            def _():
                x_cells[cell] = jnp.zeros((C, W), bf16)

            wide = x_cells[cell].astype(f32)
        value, slope, unit, inverse = act_parts(wide, gain_first)
        if cell == OWN:
            own_slope, own_unit, own_inverse = slope, unit, inverse
        band = band_of(cell)
        rounded = value.astype(bf16)
        cells[0, band, :] = rounded
        d_cells[band, :] = (slope * unit).astype(bf16)
        sums = sums + dot_nn(k1[cell], rounded)
    hidden = shift_columns(sums[:C], -1) + sums[C : 2 * C] + shift_columns(sums[2 * C :], 1)
    hidden = hidden + bias
    second, slope, unit, inverse = act_parts(hidden, gain_second)
    second = second.astype(bf16).astype(f32)
    for s in range(3):
        left[1, pl.ds(s * C, C), :] = shift_columns(second, s - 1).astype(bf16)

    sums = jnp.zeros((3 * C, W), f32)
    for cell in ORDER:
        if cell != OWN:
            c_copies[cell].wait_recv()

            @pl.when(jnp.logical_not(after(cell)))
            def _():
                cells[1, band_of(cell), :] = jnp.zeros((C, W), bf16)

        sums = sums + dot_nn(k2t[cell], cells[1, band_of(cell), :])
    grad_second = shift_columns(sums[:C], 1) + sums[C : 2 * C] + shift_columns(sums[2 * C :], -1)
    grad_scaled = grad_second * slope
    raw_gain_second = jnp.sum(grad_scaled * unit, axis=1, keepdims=True)
    grad_hidden = back_through_norm(grad_scaled, gain_second, unit, inverse)
    raw_bias = jnp.sum(grad_hidden, axis=1, keepdims=True)
    rounded = grad_hidden.astype(bf16)
    raw_cot = jnp.sum(c_own.astype(f32), axis=1, keepdims=True)
    hidden_cot = rounded.astype(f32)
    for s in range(3):
        left[0, pl.ds(s * C, C), :] = shift_columns(hidden_cot, 1 - s).astype(bf16)
    h_own = pl.ds(C, C)

    for half in (0, 1):
        packed[half, 3, 7, pl.ds(32, 32), :] = jnp.zeros((32, LANES), f32)
    put_rows(packed, 1 - me_c, dot_nt(left[1 - me_c], cells[1 - me_c]))
    core_copies = []
    for k, d in enumerate(FAR_FIRST):
        core_copies.append(send(packed.at[1 - me_c, :, at_y(d)], core_in.at[k], core_sem, k, peer_c))
    put_rows(packed, me_c, dot_nt(left[me_c], cells[me_c]))
    x_copies = []
    for k, d in enumerate(FAR_FIRST):
        core_copies[k].wait_recv()
        total = packed[me_c, :, at_y(d)] + core_in[k]
        x_out[k] = total.astype(bf16)
        part[k] = packed[me_c, me_x, at_y(d)] + core_in[k, me_x]
        for e in (2, 1, 3):
            x_copies.append(
                send(x_out.at[k, at_x(e)], x_in.at[k, e - 1], x_sem, k * 3 + e - 1, peer_x(e))
            )
    sent += core_copies + x_copies

    h_copies = {}
    for cell in halo:
        h_copies[cell] = send(left.at[0, h_own], h_cells.at[cell], hh_sem, cell, earlier(cell))

    gained = jnp.zeros((3 * C, C), f32)
    for cell in range(9):
        gained = gained + k1[cell].astype(f32) * dot_nt(left[0], d_cells[band_of(cell), :])
    vz[me_z] = jnp.zeros((8, LANES), f32)
    lanes = pl.ds(0, C)
    vz[me_z, pl.ds(0, 1), lanes] = to_row(raw_bias)
    vz[me_z, pl.ds(1, 1), lanes] = jnp.sum(gained, axis=0, keepdims=True)
    vz[me_z, pl.ds(2, 1), lanes] = to_row(raw_gain_second)
    vz[me_z, pl.ds(3, 1), lanes] = to_row(raw_cot)
    v_copies = [send(vz.at[me_z], vz.at[me_z], vz_sem, d - 1, peer_z(d)) for d in range(1, 8)]

    def vector_total(slots, count):
        for copy in v_copies:
            copy.wait_recv()
        sent.extend(v_copies)
        whole = slots[0]
        for e in range(1, count):
            whole = whole + slots[e]
        return whole

    y_copies = []
    for k, d in enumerate(FAR_FIRST):
        total = part[k]
        for copy in x_copies[3 * k : 3 * k + 3]:
            copy.wait_recv()
        for e in range(3):
            total = total + x_in[k, e].astype(f32)
        if d > 0:
            y_out[k] = total.astype(bf16)
            y_copies.append(send(y_out.at[k], y_in.at[d - 1], y_sem, d - 1, peer_y(d)))
    vy[me_y] = vector_total(vz, 8)
    v_copies = [send(vy.at[me_y], vy.at[me_y], vy_sem, d - 1, peer_y(d)) for d in range(1, 8)]
    for copy in y_copies:
        copy.wait_recv()
    for e in range(7):
        total = total + y_in[e].astype(f32)

    z_in[me_z] = total.astype(bf16)
    z_copies = []
    for d in (4, 3, 5, 2, 6, 1, 7):
        z_copies.append(send(z_in.at[me_z], z_in.at[me_z], z_sem, d - 1, peer_z(d)))
    for copy in sent:
        copy.wait_send()
    sent = []
    sums = dot_nn(k1t[OWN], left[0, h_own, :])
    for cell in ORDER[1:]:
        h_copies[cell].wait_recv()

        @pl.when(jnp.logical_not(after(cell)))
        def _():
            h_cells[cell] = jnp.zeros((C, W), bf16)

        sums = sums + dot_nn(k1t[cell], h_cells[cell])
    grad_first = shift_columns(sums[:C], 1) + sums[C : 2 * C] + shift_columns(sums[2 * C :], -1)
    input_term = back_through_norm(grad_first * own_slope, gain_first, own_unit, own_inverse)
    grad_in_ref[...] = (c_own.astype(f32) + input_term).astype(bf16)

    sent += list(h_copies.values())
    vx[me_x] = vector_total(vy, 8)
    v_copies = [send(vx.at[me_x], vx.at[me_x], vx_sem, d - 1, peer_x(d)) for d in range(1, 4)]
    for copy in z_copies:
        copy.wait_recv()
    total = z_in[0].astype(f32)
    for e in range(1, 8):
        total = total + z_in[e].astype(f32)
    rounded = total.astype(bf16)
    g_ref[me_c, me_x, me_y] = rounded
    own_squares = rounded.astype(f32)
    own_squares = own_squares * own_squares
    sent += y_copies + z_copies

    own = g_ref.at[me_c, me_x, me_y]
    gy_copies, gx_copies, gc_copies = {}, {}, []
    for d in (4, 3, 5, 2, 6, 1, 7):
        gy_copies[d] = send(own, own, gy_sem, d - 1, peer_y(d))

    def square(c, x, y):
        whole = jnp.zeros((16, LANES), f32)
        for n in range(4):
            part = g_ref[c, x, y, pl.ds(16 * n, 16), :].astype(f32)
            whole = whole + part * part
        squares[pl.ds(pl.multiple_of((c * 32 + x * 8 + y) * 16, 16), 16), :] = whole

    def pass_on(k, d):
        piece = g_ref.at[me_c, me_x, at_y(8 - d)]
        for e in (2, 1, 3):
            gx_copies[k, e] = send(piece, piece, gx_sem, k * 3 + e - 1, peer_x(e))
        gc_copies.append(send(piece, piece, gc_sem, k * 4, peer_c))
        if d > 0:
            square(me_c, me_x, at_y(8 - d))

    pass_on(0, 0)
    own_rows = pl.ds(pl.multiple_of((me_c * 32 + me_x * 8 + me_y) * 16, 16), 16)
    squares[own_rows, :] = (
        own_squares[:16] + own_squares[16:32] + own_squares[32:48] + own_squares[48:]
    )

    for k, d in enumerate((1, 7, 2, 6, 3, 5, 4)):
        gy_copies[d].wait_recv()
        pass_on(k + 1, d)
    for k, d in enumerate((0, 1, 7, 2, 6, 3, 5, 4)):
        for e in (1, 3, 2):
            gx_copies[k, e].wait_recv()
            piece = g_ref.at[me_c, at_x(4 - e), at_y(8 - d)]
            gc_copies.append(send(piece, piece, gc_sem, k * 4 + e, peer_c))
            square(me_c, at_x(4 - e), at_y(8 - d))
        if k == 0:
            vc[me_c] = vector_total(vx, 4)
            v_copies = [send(vc.at[me_c], vc.at[me_c], vc_sem, 0, peer_c)]
    for copy in sent:
        copy.wait_send()
    sent = list(gy_copies.values()) + list(gx_copies.values()) + gc_copies
    stats_ref[pl.ds(0, 8), :] = vector_total(vc, 2)
    for k, d in enumerate((0, 1, 7, 2, 6, 3, 5, 4)):
        gc_copies[k].wait_recv()
        square(1 - me_c, me_x, at_y(8 - d))
    for k, d in enumerate((0, 1, 7, 2, 6, 3, 5, 4)):
        for n, e in enumerate((1, 3, 2)):
            gc_copies[8 + 3 * k + n].wait_recv()
            square(1 - me_c, at_x(4 - e), at_y(8 - d))

    def add_squares(n, whole):
        return whole + squares[pl.ds(pl.multiple_of(n * 128, 128), 128), :]

    whole = lax.fori_loop(0, 8, add_squares, jnp.zeros((128, LANES), f32))
    whole = jnp.sum(whole, axis=0, keepdims=True)
    stats_ref[pl.ds(8, 8), :] = jnp.broadcast_to(whole * 0.125, (8, LANES))
    for copy in sent:
        copy.wait_send()


def scale_kernel(g_ref, stats_ref, grad_in_ref, first_hbm, second_hbm, vectors_ref, copy_hbm,
                 first_ref, second_ref, copy_sem, first_sem, second_sem):
    through = pltpu.make_async_copy(grad_in_ref, copy_hbm, copy_sem.at[0])
    through.start()
    stats = stats_ref[...]
    kind = lax.broadcasted_iota(jnp.int32, (16, LANES), 0)
    total = jnp.sum(jnp.where(kind < 8, stats * stats, stats), axis=1, keepdims=True)
    total = jnp.sqrt(jnp.sum(total, axis=0, keepdims=True))
    factor = jnp.minimum(1.0, max_norm / (total + epsilon))
    vectors_ref[...] = stats_ref[pl.ds(0, 4), pl.ds(0, C)] * factor
    target = lax.broadcasted_iota(jnp.int32, (C, LANES), 0)
    lane = lax.broadcasted_iota(jnp.int32, (C, LANES), 1)
    stores = []
    for cell in range(9):
        tiles = range(cell * C // LANES, (cell * C + C - 1) // LANES + 1)
        first = jnp.zeros((3 * C, C), f32)
        second = [jnp.zeros((C, C), f32) for _ in range(3)]
        for j in tiles:
            pick = jnp.where(lane + (j * LANES - cell * C) == target, 1.0, 0.0).astype(bf16)
            first = first + dot_nt(g_ref[pl.ds(j * 3 * C, 3 * C), :], pick)
            for s in range(3):
                start = HALF_ROWS + j * 3 * C + s * C
                second[s] = second[s] + dot_nt(pick, g_ref[pl.ds(start, C), :])
        first_ref[cell] = first * factor
        for s in range(3):
            second_ref[cell, pl.ds(s * C, C), :] = second[s] * factor
        stores.append(
            pltpu.make_async_copy(first_ref.at[cell], first_hbm.at[cell], first_sem.at[cell])
        )
        stores[-1].start()
        stores.append(
            pltpu.make_async_copy(second_ref.at[cell], second_hbm.at[cell], second_sem.at[cell])
        )
        stores[-1].start()
    through.wait()
    for copy in stores:
        copy.wait()


def body(inputs, cotangent, gain_first, gain_second, bias_first, kernel_first, kernel_second):
    dma, vmem = pltpu.SemaphoreType.DMA, pltpu.VMEM
    in_vmem = pl.BlockSpec(memory_space=pltpu.VMEM)
    in_any = pl.BlockSpec(memory_space=pl.ANY)
    summed, stats, grad_inputs = pl.pallas_call(
        block_kernel,
        out_shape=(
            jax.ShapeDtypeStruct((2, 4, 8, 64, LANES), bf16),
            jax.ShapeDtypeStruct((16, LANES), f32),
            jax.ShapeDtypeStruct((C, W), bf16),
        ),
        in_specs=[pl.BlockSpec(memory_space=pltpu.HBM)] * 7,
        out_specs=(in_vmem, in_vmem, in_vmem),
        scratch_shapes=[
            vmem((1024, LANES), f32),
            vmem((C, W), bf16), vmem((C, W), bf16),
            vmem((1, C), f32), vmem((1, C), f32), vmem((1, C), f32),
            vmem((9, 3 * C, C), bf16), vmem((9, 3 * C, C), bf16),
            vmem((9, 3 * C, C), bf16), vmem((9, 3 * C, C), bf16),
            vmem((9, C, W), bf16), vmem((9, C, W), bf16), vmem((9 * C, W), bf16),
            vmem((2, 3 * C, W), bf16), vmem((2, 9 * C + 32, W), bf16),
            vmem((2, 4, 8, 64, LANES), f32),
            vmem((8, 4, 64, LANES), f32),
            vmem((8, 64, LANES), f32),
            vmem((8, 4, 64, LANES), bf16),
            vmem((8, 3, 64, LANES), bf16),
            vmem((7, 64, LANES), bf16),
            vmem((7, 64, LANES), bf16),
            vmem((8, 64, LANES), bf16),
            vmem((8, 8, LANES), f32), vmem((8, 8, LANES), f32),
            vmem((4, 8, LANES), f32), vmem((2, 8, LANES), f32),
            dma((7,)), dma((2, 9)), dma((2, 9)), dma((2, 9)),
            dma((2, 8)), dma((2, 24)), dma((2, 7)), dma((2, 7)),
            dma((2, 7)), dma((2, 24)), dma((2, 32)),
            dma((2, 7)), dma((2, 7)), dma((2, 3)), dma((2, 1)),
        ],
        compiler_params=pltpu.CompilerParams(
            collective_id=0, has_side_effects=True, vmem_limit_bytes=44 * 1024 * 1024
        ),
    )(
        *(
            pltpu.with_memory_space_constraint(operand, pltpu.HBM)
            for operand in (
                inputs.reshape(C, W), cotangent.reshape(C, W),
                gain_first.reshape(1, C), gain_second.reshape(1, C), bias_first.reshape(1, C),
                kernel_first.reshape(9, 3 * C, C), kernel_second.reshape(9, 3 * C, C),
            )
        )
    )
    grad_first, grad_second, vectors, grad_inputs = pl.pallas_call(
        scale_kernel,
        out_shape=(
            jax.ShapeDtypeStruct((9, 3 * C, C), f32),
            jax.ShapeDtypeStruct((9, 3 * C, C), f32),
            jax.ShapeDtypeStruct((4, C), f32),
            jax.ShapeDtypeStruct((C, W), bf16),
        ),
        in_specs=[in_vmem] * 3,
        out_specs=(in_any, in_any, in_vmem, in_any),
        scratch_shapes=[
            vmem((9, 3 * C, C), f32), vmem((9, 3 * C, C), f32),
            dma((1,)), dma((9,)), dma((9,)),
        ],
        compiler_params=pltpu.CompilerParams(vmem_limit_bytes=44 * 1024 * 1024),
    )(summed.reshape(2 * HALF_ROWS, LANES), stats, grad_inputs)
    return (
        grad_inputs.reshape(inputs.shape),
        grad_first.reshape(kernel_first.shape),
        grad_second.reshape(kernel_second.shape),
        vectors,
    )


def solution(mesh):
    in_specs = (P(None, "tm", "row", None), P(None, "tm", "row", None), P(), P(), P(), P(), P())
    out_specs = (P(None, "tm", "row", None), P(), P(), P())
    return jax.shard_map(body, mesh=mesh, in_specs=in_specs, out_specs=out_specs, check_vma=False)
```

```python
import jax
import jax.numpy as jnp
from jax import lax
from jax.experimental import pallas as pl
from jax.experimental.pallas import tpu as pltpu
from jax.sharding import PartitionSpec as P

epsilon = 1e-06
max_norm = 500.0
C = 96
W = 256
HALF_ROWS = 2048
LANES = 128
MESH = pl.DeviceIdType.MESH
f32, bf16 = jnp.float32, jnp.bfloat16


def dot_nt(a, b):
    return lax.dot_general(a, b, (((1,), (1,)), ((), ())), preferred_element_type=f32)


def dot_nn(a, b):
    return lax.dot_general(a, b, (((1,), (0,)), ((), ())), preferred_element_type=f32)


def eye_mask():
    rows = lax.broadcasted_iota(jnp.int32, (C, C), 0)
    return rows == lax.broadcasted_iota(jnp.int32, (C, C), 1)


def to_column(row):
    spread = jnp.broadcast_to(row, (C, C))
    return jnp.sum(jnp.where(eye_mask(), spread, 0.0), axis=1, keepdims=True)


def to_row(column):
    spread = jnp.broadcast_to(column, (C, C))
    return jnp.sum(jnp.where(eye_mask(), spread, 0.0), axis=0, keepdims=True)


def shift_columns(values, offset):
    if offset == 0:
        return values
    column = lax.broadcasted_iota(jnp.int32, values.shape, 1)
    rolled = pltpu.roll(values, (-offset) % W, 1)
    edge = W - 1 if offset > 0 else 0
    return jnp.where(column == edge, 0.0, rolled)


def normalised(values):
    meansq = jnp.mean(values * values, axis=0, keepdims=True)
    inverse = lax.rsqrt(meansq + epsilon)
    return values * inverse, inverse


def act_parts(values, gain):
    unit, inverse = normalised(values)
    scaled = unit * gain
    gate = 1.0 / (1.0 + jnp.exp(-scaled))
    slope = gate * (1.0 + scaled * (1.0 - gate))
    return scaled * gate, slope, unit, inverse


def back_through_norm(grad_scaled, gain, unit, inverse):
    grad_unit = grad_scaled * gain
    return inverse * (grad_unit - unit * jnp.mean(grad_unit * unit, axis=0, keepdims=True))


CELLS = [(p, q) for p in range(3) for q in range(3)]
OWN = CELLS.index((2, 1))
ORDER = [7, 6, 8, 4, 1, 3, 5, 0, 2]


SHARED = [3, 5, 4, 6, 8]
UNSHARED = [1, 0, 2]
FAR_FIRST = (4, 5, 3, 6, 2, 7, 1, 0)


def band_of(cell):
    return pl.ds(cell * C, C)


def put_rows(packed, half, raw):
    for n in range(63):
        start = n * 32
        j, r = start // (3 * C), start % (3 * C)
        block = start // 64
        packed[half, block // 8, block % 8, pl.ds(start % 64, 32), :] = raw[
            r : r + 32, j * LANES : (j + 1) * LANES
        ]


def block_kernel(x_hbm, cot_hbm, gain_first_hbm, gain_second_hbm, bias_hbm, k1_hbm, k2_hbm,
                 g_ref, stats_ref, grad_in_ref,
                 squares, x_ref, cot_ref, gain_first_ref, gain_second_ref, bias_ref, k1, k2, k1t, k2t, x_cells, h_cells, d_cells,
                 left, cells, packed,
                 core_in, part, x_out, x_in, y_out, y_in, z_in, vz, vy, vx, vc,
                 local_sem, hx_sem, hc_sem, hh_sem, relay_sem,
                 core_sem, x_sem, y_sem, z_sem, gy_sem, gx_sem, gc_sem,
                 vz_sem, vy_sem, vx_sem, vc_sem):
    tm, row = lax.axis_index("tm"), lax.axis_index("row")
    me_x, me_c = tm // 2, tm % 2
    me_z, me_y = row // 8, row % 8
    peer_c = {"tm": me_x * 2 + 1 - me_c, "row": row}

    def at_x(d):
        return lax.rem(me_x + d, 4)

    def at_y(d):
        return lax.rem(me_y + d, 8)

    def at_z(d):
        return lax.rem(me_z + d, 8)

    def peer_x(d):
        return {"tm": at_x(d) * 2 + me_c, "row": row}

    def peer_y(d):
        return {"tm": tm, "row": me_z * 8 + at_y(d)}

    def peer_z(d):
        return {"tm": tm, "row": at_z(d) * 8 + me_y}

    def later(cell):
        p, q = CELLS[cell]
        return {"tm": lax.rem(tm + 2 - p, 8), "row": lax.rem(row + 65 - q, 64)}

    def earlier(cell):
        p, q = CELLS[cell]
        return {"tm": lax.rem(tm + 6 + p, 8), "row": lax.rem(row + 63 + q, 64)}

    def remote(src, dst, sems, slot, device):
        return pltpu.make_async_remote_copy(
            src_ref=src, dst_ref=dst, send_sem=sems.at[0, slot], recv_sem=sems.at[1, slot],
            device_id=device, device_id_type=MESH,
        )

    def send(src, dst, sems, slot, device):
        copy = remote(src, dst, sems, slot, device)
        copy.start()
        return copy

    pairs = [(x_hbm, x_ref), (cot_hbm, cot_ref), (gain_first_hbm, gain_first_ref),
             (gain_second_hbm, gain_second_ref), (bias_hbm, bias_ref), (k1_hbm, k1), (k2_hbm, k2)]
    loads = [pltpu.make_async_copy(a, b, local_sem.at[k]) for k, (a, b) in enumerate(pairs)]
    for load in loads:
        load.start()

    barrier = pltpu.get_barrier_semaphore()
    halo = [cell for cell in ORDER if cell != OWN]
    peers = [later(cell) for cell in halo] + [earlier(cell) for cell in halo]
    peers += [peer_c] + [peer_x(d) for d in range(1, 4)]
    peers += [peer_y(d) for d in range(1, 8)] + [peer_z(d) for d in range(1, 8)]
    for peer in peers:
        pl.semaphore_signal(barrier, inc=1, device_id=peer, device_id_type=MESH)
    for load in loads[:2]:
        load.wait()
    pl.semaphore_wait(barrier, len(peers))

    sent = []
    x_copies, c_copies = {}, {}
    for cell in halo:
        x_copies[cell] = remote(x_ref, x_cells.at[cell], hx_sem, cell, later(cell))
        c_copies[cell] = remote(
            cot_ref, cells.at[1, band_of(cell)], hc_sem, cell, earlier(cell)
        )

    def each_sent(act, here):
        for cell in SHARED:
            p, q = CELLS[cell]
            if here == 1 or (p, q) == (1, 1) or p == 2:
                act(x_copies[cell])
            if here == 0 or (p, q) == (1, 1) or p == 2:
                act(c_copies[cell])
        for cell in UNSHARED:
            act((x_copies if here == 0 else c_copies)[cell])

    for here in (0, 1):

        @pl.when(me_c == here)
        def _():
            each_sent(lambda copy: copy.start(), here)

    for load in loads[2:]:
        load.wait()
    gain_first = to_column(gain_first_ref[...])
    gain_second = to_column(gain_second_ref[...])
    bias = to_column(bias_ref[...])
    identity = jnp.where(eye_mask(), 1.0, 0.0).astype(bf16)
    for cell in range(9):
        for s in range(3):
            band = pl.ds(s * C, C)
            k2t[cell, band, :] = dot_nt(identity, k2[cell, band, :]).astype(bf16)
            k1t[cell, band, :] = dot_nt(identity, k1[cell, band, :]).astype(bf16)

    pad = jnp.zeros((32, W), bf16)
    cells[0, pl.ds(9 * C, 32), :] = pad
    cells[1, pl.ds(9 * C, 32), :] = pad
    c_own = cot_ref[...]
    cells[1, band_of(OWN), :] = c_own

    def before(cell):
        p, q = CELLS[cell]
        return (tm + p >= 2) & (row + q >= 1) & (row + q <= 64)

    def after(cell):
        p, q = CELLS[cell]
        return (tm + 2 - p <= 7) & (row + 1 - q >= 0) & (row + 1 - q <= 63)

    def take_x(cell):
        x_copies[cell].wait_recv()

        @pl.when(jnp.logical_not(before(cell)))
        def _():
            x_cells[cell] = jnp.zeros((C, W), bf16)

    def take_c(cell):
        c_copies[cell].wait_recv()

        @pl.when(jnp.logical_not(after(cell)))
        def _():
            cells[1, band_of(cell), :] = jnp.zeros((C, W), bf16)

    def relay(src, dst, sems, relay_sem, n, cell):
        return pltpu.make_async_remote_copy(
            src_ref=src, dst_ref=dst, send_sem=relay_sem.at[n], recv_sem=sems.at[1, cell - 3],
            device_id=peer_c, device_id_type=MESH,
        )

    x_relays = [
        relay(x_cells.at[cell], x_cells.at[cell - 3], hx_sem, relay_sem, n, cell)
        for n, cell in enumerate(SHARED)
    ]
    c_relays = [
        relay(
            cells.at[1, band_of(cell)], cells.at[1, band_of(cell - 3)], hc_sem, relay_sem, n, cell
        )
        for n, cell in enumerate(SHARED)
    ]

    @pl.when(me_c == 0)
    def _():
        for n, cell in enumerate(SHARED):
            take_x(cell)
            x_relays[n].start()

    @pl.when(me_c == 1)
    def _():
        for n, cell in enumerate(SHARED):
            take_c(cell)
            c_relays[n].start()

    sums = jnp.zeros((3 * C, W), f32)
    for cell in ORDER:
        if cell == OWN:
            wide = x_ref[...].astype(f32)
        else:
            if cell in SHARED:
                pl.when(me_c == 1)(lambda cell=cell: take_x(cell))
            else:
                take_x(cell)
            wide = x_cells[cell].astype(f32)
        value, slope, unit, inverse = act_parts(wide, gain_first)
        if cell == OWN:
            own_slope, own_unit, own_inverse = slope, unit, inverse
        band = band_of(cell)
        rounded = value.astype(bf16)
        cells[0, band, :] = rounded
        d_cells[band, :] = (slope * unit).astype(bf16)
        sums = sums + dot_nn(k1[cell], rounded)
    hidden = shift_columns(sums[:C], -1) + sums[C : 2 * C] + shift_columns(sums[2 * C :], 1)
    hidden = hidden + bias
    second, slope, unit, inverse = act_parts(hidden, gain_second)
    second = second.astype(bf16).astype(f32)
    for s in range(3):
        left[1, pl.ds(s * C, C), :] = shift_columns(second, s - 1).astype(bf16)

    sums = jnp.zeros((3 * C, W), f32)
    for cell in ORDER:
        if cell != OWN:
            if cell in SHARED:
                pl.when(me_c == 0)(lambda cell=cell: take_c(cell))
            else:
                take_c(cell)

        sums = sums + dot_nn(k2t[cell], cells[1, band_of(cell), :])
    grad_second = shift_columns(sums[:C], 1) + sums[C : 2 * C] + shift_columns(sums[2 * C :], -1)
    grad_scaled = grad_second * slope
    raw_gain_second = jnp.sum(grad_scaled * unit, axis=1, keepdims=True)
    grad_hidden = back_through_norm(grad_scaled, gain_second, unit, inverse)
    raw_bias = jnp.sum(grad_hidden, axis=1, keepdims=True)
    rounded = grad_hidden.astype(bf16)
    raw_cot = jnp.sum(c_own.astype(f32), axis=1, keepdims=True)
    hidden_cot = rounded.astype(f32)
    for s in range(3):
        left[0, pl.ds(s * C, C), :] = shift_columns(hidden_cot, 1 - s).astype(bf16)
    h_own = pl.ds(C, C)

    for half in (0, 1):
        packed[half, 3, 7, pl.ds(32, 32), :] = jnp.zeros((32, LANES), f32)
    put_rows(packed, 1 - me_c, dot_nt(left[1 - me_c], cells[1 - me_c]))
    core_copies = []
    for k, d in enumerate(FAR_FIRST):
        core_copies.append(send(packed.at[1 - me_c, :, at_y(d)], core_in.at[k], core_sem, k, peer_c))
    put_rows(packed, me_c, dot_nt(left[me_c], cells[me_c]))
    xs_copies = []
    for k, d in enumerate(FAR_FIRST):
        core_copies[k].wait_recv()
        total = packed[me_c, :, at_y(d)] + core_in[k]
        x_out[k] = total.astype(bf16)
        part[k] = packed[me_c, me_x, at_y(d)] + core_in[k, me_x]
        for e in (2, 1, 3):
            xs_copies.append(
                send(x_out.at[k, at_x(e)], x_in.at[k, e - 1], x_sem, k * 3 + e - 1, peer_x(e))
            )
    sent += core_copies + xs_copies

    h_copies = {}
    for cell in halo:
        h_copies[cell] = send(left.at[0, h_own], h_cells.at[cell], hh_sem, cell, earlier(cell))

    gained = jnp.zeros((3 * C, C), f32)
    for cell in range(9):
        gained = gained + k1[cell].astype(f32) * dot_nt(left[0], d_cells[band_of(cell), :])
    vz[me_z] = jnp.zeros((8, LANES), f32)
    lanes = pl.ds(0, C)
    vz[me_z, pl.ds(0, 1), lanes] = to_row(raw_bias)
    vz[me_z, pl.ds(1, 1), lanes] = jnp.sum(gained, axis=0, keepdims=True)
    vz[me_z, pl.ds(2, 1), lanes] = to_row(raw_gain_second)
    vz[me_z, pl.ds(3, 1), lanes] = to_row(raw_cot)
    v_copies = [send(vz.at[me_z], vz.at[me_z], vz_sem, d - 1, peer_z(d)) for d in range(1, 8)]

    def vector_total(slots, count):
        for copy in v_copies:
            copy.wait_recv()
        sent.extend(v_copies)
        whole = slots[0]
        for e in range(1, count):
            whole = whole + slots[e]
        return whole

    y_copies = []
    for k, d in enumerate(FAR_FIRST):
        total = part[k]
        for copy in xs_copies[3 * k : 3 * k + 3]:
            copy.wait_recv()
        for e in range(3):
            total = total + x_in[k, e].astype(f32)
        if d > 0:
            y_out[k] = total.astype(bf16)
            y_copies.append(send(y_out.at[k], y_in.at[d - 1], y_sem, d - 1, peer_y(d)))
    vy[me_y] = vector_total(vz, 8)
    v_copies = [send(vy.at[me_y], vy.at[me_y], vy_sem, d - 1, peer_y(d)) for d in range(1, 8)]
    for copy in y_copies:
        copy.wait_recv()
    for e in range(7):
        total = total + y_in[e].astype(f32)

    z_in[me_z] = total.astype(bf16)
    z_copies = []
    for d in (4, 3, 5, 2, 6, 1, 7):
        z_copies.append(send(z_in.at[me_z], z_in.at[me_z], z_sem, d - 1, peer_z(d)))
    for copy in sent:
        copy.wait_send()
    sent = []
    for here in (0, 1):

        @pl.when(me_c == here)
        def _():
            each_sent(lambda copy: copy.wait_send(), here)
            for copy in (x_relays, c_relays)[here]:
                copy.wait_send()

    sums = dot_nn(k1t[OWN], left[0, h_own, :])
    for cell in ORDER[1:]:
        h_copies[cell].wait_recv()

        @pl.when(jnp.logical_not(after(cell)))
        def _():
            h_cells[cell] = jnp.zeros((C, W), bf16)

        sums = sums + dot_nn(k1t[cell], h_cells[cell])
    grad_first = shift_columns(sums[:C], 1) + sums[C : 2 * C] + shift_columns(sums[2 * C :], -1)
    input_term = back_through_norm(grad_first * own_slope, gain_first, own_unit, own_inverse)
    grad_in_ref[...] = (c_own.astype(f32) + input_term).astype(bf16)

    sent += list(h_copies.values())
    vx[me_x] = vector_total(vy, 8)
    v_copies = [send(vx.at[me_x], vx.at[me_x], vx_sem, d - 1, peer_x(d)) for d in range(1, 4)]
    for copy in z_copies:
        copy.wait_recv()
    total = z_in[0].astype(f32)
    for e in range(1, 8):
        total = total + z_in[e].astype(f32)
    rounded = total.astype(bf16)
    g_ref[me_c, me_x, me_y] = rounded
    own_squares = rounded.astype(f32)
    own_squares = own_squares * own_squares
    sent += y_copies + z_copies

    own = g_ref.at[me_c, me_x, me_y]
    gy_copies, gx_copies, gc_copies = {}, {}, []
    for d in (4, 3, 5, 2, 6, 1, 7):
        gy_copies[d] = send(own, own, gy_sem, d - 1, peer_y(d))

    def square(c, x, y):
        whole = jnp.zeros((16, LANES), f32)
        for n in range(4):
            part = g_ref[c, x, y, pl.ds(16 * n, 16), :].astype(f32)
            whole = whole + part * part
        squares[pl.ds(pl.multiple_of((c * 32 + x * 8 + y) * 16, 16), 16), :] = whole

    def pass_on(k, d):
        piece = g_ref.at[me_c, me_x, at_y(8 - d)]
        for e in (2, 1, 3):
            gx_copies[k, e] = send(piece, piece, gx_sem, k * 3 + e - 1, peer_x(e))
        gc_copies.append(send(piece, piece, gc_sem, k * 4, peer_c))
        if d > 0:
            square(me_c, me_x, at_y(8 - d))

    pass_on(0, 0)
    own_rows = pl.ds(pl.multiple_of((me_c * 32 + me_x * 8 + me_y) * 16, 16), 16)
    squares[own_rows, :] = (
        own_squares[:16] + own_squares[16:32] + own_squares[32:48] + own_squares[48:]
    )

    for k, d in enumerate((1, 7, 2, 6, 3, 5, 4)):
        gy_copies[d].wait_recv()
        pass_on(k + 1, d)
    for k, d in enumerate((0, 1, 7, 2, 6, 3, 5, 4)):
        for e in (1, 3, 2):
            gx_copies[k, e].wait_recv()
            piece = g_ref.at[me_c, at_x(4 - e), at_y(8 - d)]
            gc_copies.append(send(piece, piece, gc_sem, k * 4 + e, peer_c))
            square(me_c, at_x(4 - e), at_y(8 - d))
        if k == 0:
            vc[me_c] = vector_total(vx, 4)
            v_copies = [send(vc.at[me_c], vc.at[me_c], vc_sem, 0, peer_c)]
    for copy in sent:
        copy.wait_send()
    sent = list(gy_copies.values()) + list(gx_copies.values()) + gc_copies
    stats_ref[pl.ds(0, 8), :] = vector_total(vc, 2)
    for k, d in enumerate((0, 1, 7, 2, 6, 3, 5, 4)):
        gc_copies[k].wait_recv()
        square(1 - me_c, me_x, at_y(8 - d))
    for k, d in enumerate((0, 1, 7, 2, 6, 3, 5, 4)):
        for n, e in enumerate((1, 3, 2)):
            gc_copies[8 + 3 * k + n].wait_recv()
            square(1 - me_c, at_x(4 - e), at_y(8 - d))

    def add_squares(n, whole):
        return whole + squares[pl.ds(pl.multiple_of(n * 128, 128), 128), :]

    whole = lax.fori_loop(0, 8, add_squares, jnp.zeros((128, LANES), f32))
    whole = jnp.sum(whole, axis=0, keepdims=True)
    stats_ref[pl.ds(8, 8), :] = jnp.broadcast_to(whole * 0.125, (8, LANES))
    for copy in sent:
        copy.wait_send()


def scale_kernel(g_ref, stats_ref, grad_in_ref, first_hbm, second_hbm, vectors_ref, copy_hbm,
                 first_ref, second_ref, copy_sem, first_sem, second_sem):
    through = pltpu.make_async_copy(grad_in_ref, copy_hbm, copy_sem.at[0])
    through.start()
    stats = stats_ref[...]
    kind = lax.broadcasted_iota(jnp.int32, (16, LANES), 0)
    total = jnp.sum(jnp.where(kind < 8, stats * stats, stats), axis=1, keepdims=True)
    total = jnp.sqrt(jnp.sum(total, axis=0, keepdims=True))
    factor = jnp.minimum(1.0, max_norm / (total + epsilon))
    vectors_ref[...] = stats_ref[pl.ds(0, 4), pl.ds(0, C)] * factor
    target = lax.broadcasted_iota(jnp.int32, (C, LANES), 0)
    lane = lax.broadcasted_iota(jnp.int32, (C, LANES), 1)
    stores = []
    for cell in range(9):
        tiles = range(cell * C // LANES, (cell * C + C - 1) // LANES + 1)
        first = jnp.zeros((3 * C, C), f32)
        second = [jnp.zeros((C, C), f32) for _ in range(3)]
        for j in tiles:
            pick = jnp.where(lane + (j * LANES - cell * C) == target, 1.0, 0.0).astype(bf16)
            first = first + dot_nt(g_ref[pl.ds(j * 3 * C, 3 * C), :], pick)
            for s in range(3):
                start = HALF_ROWS + j * 3 * C + s * C
                second[s] = second[s] + dot_nt(pick, g_ref[pl.ds(start, C), :])
        first_ref[cell] = first * factor
        for s in range(3):
            second_ref[cell, pl.ds(s * C, C), :] = second[s] * factor
        stores.append(
            pltpu.make_async_copy(first_ref.at[cell], first_hbm.at[cell], first_sem.at[cell])
        )
        stores[-1].start()
        stores.append(
            pltpu.make_async_copy(second_ref.at[cell], second_hbm.at[cell], second_sem.at[cell])
        )
        stores[-1].start()
    through.wait()
    for copy in stores:
        copy.wait()


def body(inputs, cotangent, gain_first, gain_second, bias_first, kernel_first, kernel_second):
    dma, vmem = pltpu.SemaphoreType.DMA, pltpu.VMEM
    in_vmem = pl.BlockSpec(memory_space=pltpu.VMEM)
    in_any = pl.BlockSpec(memory_space=pl.ANY)
    summed, stats, grad_inputs = pl.pallas_call(
        block_kernel,
        out_shape=(
            jax.ShapeDtypeStruct((2, 4, 8, 64, LANES), bf16),
            jax.ShapeDtypeStruct((16, LANES), f32),
            jax.ShapeDtypeStruct((C, W), bf16),
        ),
        in_specs=[pl.BlockSpec(memory_space=pltpu.HBM)] * 7,
        out_specs=(in_vmem, in_vmem, in_vmem),
        scratch_shapes=[
            vmem((1024, LANES), f32),
            vmem((C, W), bf16), vmem((C, W), bf16),
            vmem((1, C), f32), vmem((1, C), f32), vmem((1, C), f32),
            vmem((9, 3 * C, C), bf16), vmem((9, 3 * C, C), bf16),
            vmem((9, 3 * C, C), bf16), vmem((9, 3 * C, C), bf16),
            vmem((9, C, W), bf16), vmem((9, C, W), bf16), vmem((9 * C, W), bf16),
            vmem((2, 3 * C, W), bf16), vmem((2, 9 * C + 32, W), bf16),
            vmem((2, 4, 8, 64, LANES), f32),
            vmem((8, 4, 64, LANES), f32),
            vmem((8, 64, LANES), f32),
            vmem((8, 4, 64, LANES), bf16),
            vmem((8, 3, 64, LANES), bf16),
            vmem((7, 64, LANES), bf16),
            vmem((7, 64, LANES), bf16),
            vmem((8, 64, LANES), bf16),
            vmem((8, 8, LANES), f32), vmem((8, 8, LANES), f32),
            vmem((4, 8, LANES), f32), vmem((2, 8, LANES), f32),
            dma((7,)), dma((2, 9)), dma((2, 9)), dma((2, 9)), dma((5,)),
            dma((2, 8)), dma((2, 24)), dma((2, 7)), dma((2, 7)),
            dma((2, 7)), dma((2, 24)), dma((2, 32)),
            dma((2, 7)), dma((2, 7)), dma((2, 3)), dma((2, 1)),
        ],
        compiler_params=pltpu.CompilerParams(
            collective_id=0, has_side_effects=True, vmem_limit_bytes=44 * 1024 * 1024
        ),
    )(
        *(
            pltpu.with_memory_space_constraint(operand, pltpu.HBM)
            for operand in (
                inputs.reshape(C, W), cotangent.reshape(C, W),
                gain_first.reshape(1, C), gain_second.reshape(1, C), bias_first.reshape(1, C),
                kernel_first.reshape(9, 3 * C, C), kernel_second.reshape(9, 3 * C, C),
            )
        )
    )
    grad_first, grad_second, vectors, grad_inputs = pl.pallas_call(
        scale_kernel,
        out_shape=(
            jax.ShapeDtypeStruct((9, 3 * C, C), f32),
            jax.ShapeDtypeStruct((9, 3 * C, C), f32),
            jax.ShapeDtypeStruct((4, C), f32),
            jax.ShapeDtypeStruct((C, W), bf16),
        ),
        in_specs=[in_vmem] * 3,
        out_specs=(in_any, in_any, in_vmem, in_any),
        scratch_shapes=[
            vmem((9, 3 * C, C), f32), vmem((9, 3 * C, C), f32),
            dma((1,)), dma((9,)), dma((9,)),
        ],
        compiler_params=pltpu.CompilerParams(vmem_limit_bytes=44 * 1024 * 1024),
    )(summed.reshape(2 * HALF_ROWS, LANES), stats, grad_inputs)
    return (
        grad_inputs.reshape(inputs.shape),
        grad_first.reshape(kernel_first.shape),
        grad_second.reshape(kernel_second.shape),
        vectors,
    )


def solution(mesh):
    in_specs = (P(None, "tm", "row", None), P(None, "tm", "row", None), P(), P(), P(), P(), P())
    out_specs = (P(None, "tm", "row", None), P(), P(), P())
    return jax.shard_map(body, mesh=mesh, in_specs=in_specs, out_specs=out_specs, check_vma=False)
```

```python
import jax
import jax.numpy as jnp
from jax import lax
from jax.experimental import pallas as pl
from jax.experimental.pallas import tpu as pltpu
from jax.sharding import PartitionSpec as P

epsilon = 1e-06
max_norm = 500.0
C = 96
W = 256
HALF_ROWS = 2048
LANES = 128
MESH = pl.DeviceIdType.MESH
f32, bf16 = jnp.float32, jnp.bfloat16


def dot_nt(a, b):
    return lax.dot_general(a, b, (((1,), (1,)), ((), ())), preferred_element_type=f32)


def dot_nn(a, b):
    return lax.dot_general(a, b, (((1,), (0,)), ((), ())), preferred_element_type=f32)


def eye_mask():
    rows = lax.broadcasted_iota(jnp.int32, (C, C), 0)
    return rows == lax.broadcasted_iota(jnp.int32, (C, C), 1)


def to_column(row):
    spread = jnp.broadcast_to(row, (C, C))
    return jnp.sum(jnp.where(eye_mask(), spread, 0.0), axis=1, keepdims=True)


def to_row(column):
    spread = jnp.broadcast_to(column, (C, C))
    return jnp.sum(jnp.where(eye_mask(), spread, 0.0), axis=0, keepdims=True)


def shift_columns(values, offset):
    if offset == 0:
        return values
    column = lax.broadcasted_iota(jnp.int32, values.shape, 1)
    rolled = pltpu.roll(values, (-offset) % W, 1)
    edge = W - 1 if offset > 0 else 0
    return jnp.where(column == edge, 0.0, rolled)


def normalised(values):
    meansq = jnp.mean(values * values, axis=0, keepdims=True)
    inverse = lax.rsqrt(meansq + epsilon)
    return values * inverse, inverse


def act_parts(values, gain):
    unit, inverse = normalised(values)
    scaled = unit * gain
    gate = 1.0 / (1.0 + jnp.exp(-scaled))
    slope = gate * (1.0 + scaled * (1.0 - gate))
    return scaled * gate, slope, unit, inverse


def back_through_norm(grad_scaled, gain, unit, inverse):
    grad_unit = grad_scaled * gain
    return inverse * (grad_unit - unit * jnp.mean(grad_unit * unit, axis=0, keepdims=True))


CELLS = [(p, q) for p in range(3) for q in range(3)]
OWN = CELLS.index((2, 1))
ORDER = [7, 6, 8, 4, 1, 3, 5, 0, 2]


SHARED = [3, 5, 4, 6, 8]
UNSHARED = [1, 0, 2]
FAR_FIRST = (4, 5, 3, 6, 2, 7, 1, 0)


def band_of(cell):
    return pl.ds(cell * C, C)


def put_rows(packed, half, raw):
    for n in range(63):
        start = n * 32
        j, r = start // (3 * C), start % (3 * C)
        block = start // 64
        packed[half, block // 8, block % 8, pl.ds(start % 64, 32), :] = raw[
            r : r + 32, j * LANES : (j + 1) * LANES
        ]


def block_kernel(x_hbm, cot_hbm, gain_first_hbm, gain_second_hbm, bias_hbm, k1_hbm, k2_hbm,
                 g_ref, stats_ref, grad_in_ref,
                 squares, x_ref, cot_ref, gain_first_ref, gain_second_ref, bias_ref, k1, k2, k1t, k2t, x_cells, h_cells, d_cells,
                 left, cells, packed,
                 core_in, part, x_out, x_in, y_out, y_in, z_in, vz, vy, vx, vc,
                 local_sem, hx_sem, hc_sem, hh_sem, relay_sem, h_relay_sem,
                 core_sem, x_sem, y_sem, z_sem, gy_sem, gx_sem, gc_sem,
                 vz_sem, vy_sem, vx_sem, vc_sem):
    tm, row = lax.axis_index("tm"), lax.axis_index("row")
    me_x, me_c = tm // 2, tm % 2
    me_z, me_y = row // 8, row % 8
    peer_c = {"tm": me_x * 2 + 1 - me_c, "row": row}

    def at_x(d):
        return lax.rem(me_x + d, 4)

    def at_y(d):
        return lax.rem(me_y + d, 8)

    def at_z(d):
        return lax.rem(me_z + d, 8)

    def peer_x(d):
        return {"tm": at_x(d) * 2 + me_c, "row": row}

    def peer_y(d):
        return {"tm": tm, "row": me_z * 8 + at_y(d)}

    def peer_z(d):
        return {"tm": tm, "row": at_z(d) * 8 + me_y}

    def later(cell):
        p, q = CELLS[cell]
        return {"tm": lax.rem(tm + 2 - p, 8), "row": lax.rem(row + 65 - q, 64)}

    def earlier(cell):
        p, q = CELLS[cell]
        return {"tm": lax.rem(tm + 6 + p, 8), "row": lax.rem(row + 63 + q, 64)}

    def remote(src, dst, sems, slot, device):
        return pltpu.make_async_remote_copy(
            src_ref=src, dst_ref=dst, send_sem=sems.at[0, slot], recv_sem=sems.at[1, slot],
            device_id=device, device_id_type=MESH,
        )

    def send(src, dst, sems, slot, device):
        copy = remote(src, dst, sems, slot, device)
        copy.start()
        return copy

    pairs = [(x_hbm, x_ref), (cot_hbm, cot_ref), (gain_first_hbm, gain_first_ref),
             (gain_second_hbm, gain_second_ref), (bias_hbm, bias_ref), (k1_hbm, k1), (k2_hbm, k2)]
    loads = [pltpu.make_async_copy(a, b, local_sem.at[k]) for k, (a, b) in enumerate(pairs)]
    for load in loads:
        load.start()

    barrier = pltpu.get_barrier_semaphore()
    halo = [cell for cell in ORDER if cell != OWN]
    peers = [later(cell) for cell in halo] + [earlier(cell) for cell in halo]
    peers += [peer_c] + [peer_x(d) for d in range(1, 4)]
    peers += [peer_y(d) for d in range(1, 8)] + [peer_z(d) for d in range(1, 8)]
    for peer in peers:
        pl.semaphore_signal(barrier, inc=1, device_id=peer, device_id_type=MESH)
    for load in loads[:2]:
        load.wait()
    pl.semaphore_wait(barrier, len(peers))

    sent = []
    x_copies, c_copies = {}, {}
    for cell in halo:
        x_copies[cell] = remote(x_ref, x_cells.at[cell], hx_sem, cell, later(cell))
        c_copies[cell] = remote(
            cot_ref, cells.at[1, band_of(cell)], hc_sem, cell, earlier(cell)
        )

    def each_sent(act, here):
        for cell in SHARED:
            p, q = CELLS[cell]
            if here == 1 or (p, q) == (1, 1) or p == 2:
                act(x_copies[cell])
            if here == 0 or (p, q) == (1, 1) or p == 2:
                act(c_copies[cell])
        for cell in UNSHARED:
            act((x_copies if here == 0 else c_copies)[cell])

    for here in (0, 1):

        @pl.when(me_c == here)
        def _():
            each_sent(lambda copy: copy.start(), here)

    for load in loads[2:]:
        load.wait()
    gain_first = to_column(gain_first_ref[...])
    gain_second = to_column(gain_second_ref[...])
    bias = to_column(bias_ref[...])
    identity = jnp.where(eye_mask(), 1.0, 0.0).astype(bf16)
    for cell in range(9):
        for s in range(3):
            band = pl.ds(s * C, C)
            k2t[cell, band, :] = dot_nt(identity, k2[cell, band, :]).astype(bf16)
            k1t[cell, band, :] = dot_nt(identity, k1[cell, band, :]).astype(bf16)

    pad = jnp.zeros((32, W), bf16)
    cells[0, pl.ds(9 * C, 32), :] = pad
    cells[1, pl.ds(9 * C, 32), :] = pad
    c_own = cot_ref[...]
    cells[1, band_of(OWN), :] = c_own

    def before(cell):
        p, q = CELLS[cell]
        return (tm + p >= 2) & (row + q >= 1) & (row + q <= 64)

    def after(cell):
        p, q = CELLS[cell]
        return (tm + 2 - p <= 7) & (row + 1 - q >= 0) & (row + 1 - q <= 63)

    def take_x(cell):
        x_copies[cell].wait_recv()

        @pl.when(jnp.logical_not(before(cell)))
        def _():
            x_cells[cell] = jnp.zeros((C, W), bf16)

    def take_c(cell):
        c_copies[cell].wait_recv()

        @pl.when(jnp.logical_not(after(cell)))
        def _():
            cells[1, band_of(cell), :] = jnp.zeros((C, W), bf16)

    def relay(src, dst, sems, relay_sem, n, cell):
        return pltpu.make_async_remote_copy(
            src_ref=src, dst_ref=dst, send_sem=relay_sem.at[n], recv_sem=sems.at[1, cell - 3],
            device_id=peer_c, device_id_type=MESH,
        )

    x_relays = [
        relay(x_cells.at[cell], x_cells.at[cell - 3], hx_sem, relay_sem, n, cell)
        for n, cell in enumerate(SHARED)
    ]
    c_relays = [
        relay(
            cells.at[1, band_of(cell)], cells.at[1, band_of(cell - 3)], hc_sem, relay_sem, n, cell
        )
        for n, cell in enumerate(SHARED)
    ]

    @pl.when(me_c == 0)
    def _():
        for n, cell in enumerate(SHARED):
            take_x(cell)
            x_relays[n].start()

    @pl.when(me_c == 1)
    def _():
        for n, cell in enumerate(SHARED):
            take_c(cell)
            c_relays[n].start()

    sums = jnp.zeros((3 * C, W), f32)
    for cell in ORDER:
        if cell == OWN:
            wide = x_ref[...].astype(f32)
        else:
            if cell in SHARED:
                pl.when(me_c == 1)(lambda cell=cell: take_x(cell))
            else:
                take_x(cell)
            wide = x_cells[cell].astype(f32)
        value, slope, unit, inverse = act_parts(wide, gain_first)
        if cell == OWN:
            own_slope, own_unit, own_inverse = slope, unit, inverse
        band = band_of(cell)
        rounded = value.astype(bf16)
        cells[0, band, :] = rounded
        d_cells[band, :] = (slope * unit).astype(bf16)
        sums = sums + dot_nn(k1[cell], rounded)
    hidden = shift_columns(sums[:C], -1) + sums[C : 2 * C] + shift_columns(sums[2 * C :], 1)
    hidden = hidden + bias
    second, slope, unit, inverse = act_parts(hidden, gain_second)
    second = second.astype(bf16).astype(f32)
    for s in range(3):
        left[1, pl.ds(s * C, C), :] = shift_columns(second, s - 1).astype(bf16)

    sums = jnp.zeros((3 * C, W), f32)
    for cell in ORDER:
        if cell != OWN:
            if cell in SHARED:
                pl.when(me_c == 0)(lambda cell=cell: take_c(cell))
            else:
                take_c(cell)

        sums = sums + dot_nn(k2t[cell], cells[1, band_of(cell), :])
    grad_second = shift_columns(sums[:C], 1) + sums[C : 2 * C] + shift_columns(sums[2 * C :], -1)
    grad_scaled = grad_second * slope
    raw_gain_second = jnp.sum(grad_scaled * unit, axis=1, keepdims=True)
    grad_hidden = back_through_norm(grad_scaled, gain_second, unit, inverse)
    raw_bias = jnp.sum(grad_hidden, axis=1, keepdims=True)
    rounded = grad_hidden.astype(bf16)
    raw_cot = jnp.sum(c_own.astype(f32), axis=1, keepdims=True)
    hidden_cot = rounded.astype(f32)
    for s in range(3):
        left[0, pl.ds(s * C, C), :] = shift_columns(hidden_cot, 1 - s).astype(bf16)
    h_own = pl.ds(C, C)

    for half in (0, 1):
        packed[half, 3, 7, pl.ds(32, 32), :] = jnp.zeros((32, LANES), f32)
    put_rows(packed, 1 - me_c, dot_nt(left[1 - me_c], cells[1 - me_c]))
    core_copies = []
    for k, d in enumerate(FAR_FIRST):
        core_copies.append(send(packed.at[1 - me_c, :, at_y(d)], core_in.at[k], core_sem, k, peer_c))
    put_rows(packed, me_c, dot_nt(left[me_c], cells[me_c]))
    xs_copies = []
    for k, d in enumerate(FAR_FIRST):
        core_copies[k].wait_recv()
        total = packed[me_c, :, at_y(d)] + core_in[k]
        x_out[k] = total.astype(bf16)
        part[k] = packed[me_c, me_x, at_y(d)] + core_in[k, me_x]
        for e in (2, 1, 3):
            xs_copies.append(
                send(x_out.at[k, at_x(e)], x_in.at[k, e - 1], x_sem, k * 3 + e - 1, peer_x(e))
            )
    sent += core_copies + xs_copies

    h_copies = {}
    for cell in halo:
        h_copies[cell] = remote(left.at[0, h_own], h_cells.at[cell], hh_sem, cell, earlier(cell))
    h_relays = [
        pltpu.make_async_remote_copy(
            src_ref=h_cells.at[cell], dst_ref=h_cells.at[cell - 3],
            send_sem=h_relay_sem.at[n], recv_sem=hh_sem.at[1, cell - 3],
            device_id=peer_c, device_id_type=MESH,
        )
        for n, cell in enumerate(SHARED)
    ]

    def each_hidden(act, here):
        for cell in SHARED:
            p, q = CELLS[cell]
            if here == 0 or (p, q) == (1, 1) or p == 2:
                act(h_copies[cell])
        if here == 1:
            for cell in UNSHARED:
                act(h_copies[cell])

    for here in (0, 1):

        @pl.when(me_c == here)
        def _():
            each_hidden(lambda copy: copy.start(), here)

    gained = jnp.zeros((3 * C, C), f32)
    for cell in range(9):
        gained = gained + k1[cell].astype(f32) * dot_nt(left[0], d_cells[band_of(cell), :])
    vz[me_z] = jnp.zeros((8, LANES), f32)
    lanes = pl.ds(0, C)
    vz[me_z, pl.ds(0, 1), lanes] = to_row(raw_bias)
    vz[me_z, pl.ds(1, 1), lanes] = jnp.sum(gained, axis=0, keepdims=True)
    vz[me_z, pl.ds(2, 1), lanes] = to_row(raw_gain_second)
    vz[me_z, pl.ds(3, 1), lanes] = to_row(raw_cot)
    v_copies = [send(vz.at[me_z], vz.at[me_z], vz_sem, d - 1, peer_z(d)) for d in range(1, 8)]

    def vector_total(slots, count):
        for copy in v_copies:
            copy.wait_recv()
        sent.extend(v_copies)
        whole = slots[0]
        for e in range(1, count):
            whole = whole + slots[e]
        return whole

    y_copies = []
    for k, d in enumerate(FAR_FIRST):
        total = part[k]
        for copy in xs_copies[3 * k : 3 * k + 3]:
            copy.wait_recv()
        for e in range(3):
            total = total + x_in[k, e].astype(f32)
        if d > 0:
            y_out[k] = total.astype(bf16)
            y_copies.append(send(y_out.at[k], y_in.at[d - 1], y_sem, d - 1, peer_y(d)))
    vy[me_y] = vector_total(vz, 8)
    v_copies = [send(vy.at[me_y], vy.at[me_y], vy_sem, d - 1, peer_y(d)) for d in range(1, 8)]
    for copy in y_copies:
        copy.wait_recv()
    for e in range(7):
        total = total + y_in[e].astype(f32)

    z_in[me_z] = total.astype(bf16)
    z_copies = []
    for d in (4, 3, 5, 2, 6, 1, 7):
        z_copies.append(send(z_in.at[me_z], z_in.at[me_z], z_sem, d - 1, peer_z(d)))
    for copy in sent:
        copy.wait_send()
    sent = []
    for here in (0, 1):

        @pl.when(me_c == here)
        def _():
            each_sent(lambda copy: copy.wait_send(), here)
            for copy in (x_relays, c_relays)[here]:
                copy.wait_send()

    def take_h(cell):
        h_copies[cell].wait_recv()

        @pl.when(jnp.logical_not(after(cell)))
        def _():
            h_cells[cell] = jnp.zeros((C, W), bf16)

    @pl.when(me_c == 1)
    def _():
        for n, cell in enumerate(SHARED):
            take_h(cell)
            h_relays[n].start()

    sums = dot_nn(k1t[OWN], left[0, h_own, :])
    for cell in ORDER[1:]:
        if cell in SHARED:
            pl.when(me_c == 0)(lambda cell=cell: take_h(cell))
        else:
            take_h(cell)
        sums = sums + dot_nn(k1t[cell], h_cells[cell])
    grad_first = shift_columns(sums[:C], 1) + sums[C : 2 * C] + shift_columns(sums[2 * C :], -1)
    input_term = back_through_norm(grad_first * own_slope, gain_first, own_unit, own_inverse)
    grad_in_ref[...] = (c_own.astype(f32) + input_term).astype(bf16)

    vx[me_x] = vector_total(vy, 8)
    v_copies = [send(vx.at[me_x], vx.at[me_x], vx_sem, d - 1, peer_x(d)) for d in range(1, 4)]
    for copy in z_copies:
        copy.wait_recv()
    total = z_in[0].astype(f32)
    for e in range(1, 8):
        total = total + z_in[e].astype(f32)
    rounded = total.astype(bf16)
    g_ref[me_c, me_x, me_y] = rounded
    own_squares = rounded.astype(f32)
    own_squares = own_squares * own_squares
    sent += y_copies + z_copies

    own = g_ref.at[me_c, me_x, me_y]
    gy_copies, gx_copies, gc_copies = {}, {}, []
    for d in (4, 3, 5, 2, 6, 1, 7):
        gy_copies[d] = send(own, own, gy_sem, d - 1, peer_y(d))

    def square(c, x, y):
        whole = jnp.zeros((16, LANES), f32)
        for n in range(4):
            part = g_ref[c, x, y, pl.ds(16 * n, 16), :].astype(f32)
            whole = whole + part * part
        squares[pl.ds(pl.multiple_of((c * 32 + x * 8 + y) * 16, 16), 16), :] = whole

    def pass_on(k, d):
        piece = g_ref.at[me_c, me_x, at_y(8 - d)]
        for e in (2, 1, 3):
            gx_copies[k, e] = send(piece, piece, gx_sem, k * 3 + e - 1, peer_x(e))
        gc_copies.append(send(piece, piece, gc_sem, k * 4, peer_c))
        if d > 0:
            square(me_c, me_x, at_y(8 - d))

    pass_on(0, 0)
    own_rows = pl.ds(pl.multiple_of((me_c * 32 + me_x * 8 + me_y) * 16, 16), 16)
    squares[own_rows, :] = (
        own_squares[:16] + own_squares[16:32] + own_squares[32:48] + own_squares[48:]
    )

    for k, d in enumerate((1, 7, 2, 6, 3, 5, 4)):
        gy_copies[d].wait_recv()
        pass_on(k + 1, d)
    for k, d in enumerate((0, 1, 7, 2, 6, 3, 5, 4)):
        for e in (1, 3, 2):
            gx_copies[k, e].wait_recv()
            piece = g_ref.at[me_c, at_x(4 - e), at_y(8 - d)]
            gc_copies.append(send(piece, piece, gc_sem, k * 4 + e, peer_c))
            square(me_c, at_x(4 - e), at_y(8 - d))
        if k == 0:
            vc[me_c] = vector_total(vx, 4)
            v_copies = [send(vc.at[me_c], vc.at[me_c], vc_sem, 0, peer_c)]
    for here in (0, 1):

        @pl.when(me_c == here)
        def _():
            each_hidden(lambda copy: copy.wait_send(), here)
            if here == 1:
                for copy in h_relays:
                    copy.wait_send()

    for copy in sent:
        copy.wait_send()
    sent = list(gy_copies.values()) + list(gx_copies.values()) + gc_copies
    stats_ref[pl.ds(0, 8), :] = vector_total(vc, 2)
    for k, d in enumerate((0, 1, 7, 2, 6, 3, 5, 4)):
        gc_copies[k].wait_recv()
        square(1 - me_c, me_x, at_y(8 - d))
    for k, d in enumerate((0, 1, 7, 2, 6, 3, 5, 4)):
        for n, e in enumerate((1, 3, 2)):
            gc_copies[8 + 3 * k + n].wait_recv()
            square(1 - me_c, at_x(4 - e), at_y(8 - d))

    def add_squares(n, whole):
        return whole + squares[pl.ds(pl.multiple_of(n * 128, 128), 128), :]

    whole = lax.fori_loop(0, 8, add_squares, jnp.zeros((128, LANES), f32))
    whole = jnp.sum(whole, axis=0, keepdims=True)
    stats_ref[pl.ds(8, 8), :] = jnp.broadcast_to(whole * 0.125, (8, LANES))
    for copy in sent:
        copy.wait_send()


def scale_kernel(g_ref, stats_ref, grad_in_ref, first_hbm, second_hbm, vectors_ref, copy_hbm,
                 first_ref, second_ref, copy_sem, first_sem, second_sem):
    through = pltpu.make_async_copy(grad_in_ref, copy_hbm, copy_sem.at[0])
    through.start()
    stats = stats_ref[...]
    kind = lax.broadcasted_iota(jnp.int32, (16, LANES), 0)
    total = jnp.sum(jnp.where(kind < 8, stats * stats, stats), axis=1, keepdims=True)
    total = jnp.sqrt(jnp.sum(total, axis=0, keepdims=True))
    factor = jnp.minimum(1.0, max_norm / (total + epsilon))
    vectors_ref[...] = stats_ref[pl.ds(0, 4), pl.ds(0, C)] * factor
    target = lax.broadcasted_iota(jnp.int32, (C, LANES), 0)
    lane = lax.broadcasted_iota(jnp.int32, (C, LANES), 1)
    stores = []
    for cell in range(9):
        tiles = range(cell * C // LANES, (cell * C + C - 1) // LANES + 1)
        first = jnp.zeros((3 * C, C), f32)
        second = [jnp.zeros((C, C), f32) for _ in range(3)]
        for j in tiles:
            pick = jnp.where(lane + (j * LANES - cell * C) == target, 1.0, 0.0).astype(bf16)
            first = first + dot_nt(g_ref[pl.ds(j * 3 * C, 3 * C), :], pick)
            for s in range(3):
                start = HALF_ROWS + j * 3 * C + s * C
                second[s] = second[s] + dot_nt(pick, g_ref[pl.ds(start, C), :])
        first_ref[cell] = first * factor
        for s in range(3):
            second_ref[cell, pl.ds(s * C, C), :] = second[s] * factor
        stores.append(
            pltpu.make_async_copy(first_ref.at[cell], first_hbm.at[cell], first_sem.at[cell])
        )
        stores[-1].start()
        stores.append(
            pltpu.make_async_copy(second_ref.at[cell], second_hbm.at[cell], second_sem.at[cell])
        )
        stores[-1].start()
    through.wait()
    for copy in stores:
        copy.wait()


def body(inputs, cotangent, gain_first, gain_second, bias_first, kernel_first, kernel_second):
    dma, vmem = pltpu.SemaphoreType.DMA, pltpu.VMEM
    in_vmem = pl.BlockSpec(memory_space=pltpu.VMEM)
    in_any = pl.BlockSpec(memory_space=pl.ANY)
    summed, stats, grad_inputs = pl.pallas_call(
        block_kernel,
        out_shape=(
            jax.ShapeDtypeStruct((2, 4, 8, 64, LANES), bf16),
            jax.ShapeDtypeStruct((16, LANES), f32),
            jax.ShapeDtypeStruct((C, W), bf16),
        ),
        in_specs=[pl.BlockSpec(memory_space=pltpu.HBM)] * 7,
        out_specs=(in_vmem, in_vmem, in_vmem),
        scratch_shapes=[
            vmem((1024, LANES), f32),
            vmem((C, W), bf16), vmem((C, W), bf16),
            vmem((1, C), f32), vmem((1, C), f32), vmem((1, C), f32),
            vmem((9, 3 * C, C), bf16), vmem((9, 3 * C, C), bf16),
            vmem((9, 3 * C, C), bf16), vmem((9, 3 * C, C), bf16),
            vmem((9, C, W), bf16), vmem((9, C, W), bf16), vmem((9 * C, W), bf16),
            vmem((2, 3 * C, W), bf16), vmem((2, 9 * C + 32, W), bf16),
            vmem((2, 4, 8, 64, LANES), f32),
            vmem((8, 4, 64, LANES), f32),
            vmem((8, 64, LANES), f32),
            vmem((8, 4, 64, LANES), bf16),
            vmem((8, 3, 64, LANES), bf16),
            vmem((7, 64, LANES), bf16),
            vmem((7, 64, LANES), bf16),
            vmem((8, 64, LANES), bf16),
            vmem((8, 8, LANES), f32), vmem((8, 8, LANES), f32),
            vmem((4, 8, LANES), f32), vmem((2, 8, LANES), f32),
            dma((7,)), dma((2, 9)), dma((2, 9)), dma((2, 9)), dma((5,)), dma((5,)),
            dma((2, 8)), dma((2, 24)), dma((2, 7)), dma((2, 7)),
            dma((2, 7)), dma((2, 24)), dma((2, 32)),
            dma((2, 7)), dma((2, 7)), dma((2, 3)), dma((2, 1)),
        ],
        compiler_params=pltpu.CompilerParams(
            collective_id=0, has_side_effects=True, vmem_limit_bytes=44 * 1024 * 1024
        ),
    )(
        *(
            pltpu.with_memory_space_constraint(operand, pltpu.HBM)
            for operand in (
                inputs.reshape(C, W), cotangent.reshape(C, W),
                gain_first.reshape(1, C), gain_second.reshape(1, C), bias_first.reshape(1, C),
                kernel_first.reshape(9, 3 * C, C), kernel_second.reshape(9, 3 * C, C),
            )
        )
    )
    grad_first, grad_second, vectors, grad_inputs = pl.pallas_call(
        scale_kernel,
        out_shape=(
            jax.ShapeDtypeStruct((9, 3 * C, C), f32),
            jax.ShapeDtypeStruct((9, 3 * C, C), f32),
            jax.ShapeDtypeStruct((4, C), f32),
            jax.ShapeDtypeStruct((C, W), bf16),
        ),
        in_specs=[in_vmem] * 3,
        out_specs=(in_any, in_any, in_vmem, in_any),
        scratch_shapes=[
            vmem((9, 3 * C, C), f32), vmem((9, 3 * C, C), f32),
            dma((1,)), dma((9,)), dma((9,)),
        ],
        compiler_params=pltpu.CompilerParams(vmem_limit_bytes=44 * 1024 * 1024),
    )(summed.reshape(2 * HALF_ROWS, LANES), stats, grad_inputs)
    return (
        grad_inputs.reshape(inputs.shape),
        grad_first.reshape(kernel_first.shape),
        grad_second.reshape(kernel_second.shape),
        vectors,
    )


def solution(mesh):
    in_specs = (P(None, "tm", "row", None), P(None, "tm", "row", None), P(), P(), P(), P(), P())
    out_specs = (P(None, "tm", "row", None), P(), P(), P())
    return jax.shard_map(body, mesh=mesh, in_specs=in_specs, out_specs=out_specs, check_vma=False)
```
